32 devices in a mesh: ens: 2 (over y), mom: 8 (over z, x), src: 2 (over core).
Axes of the slice: x: 2, y: 2, z: 4, core: 2. Of those that a mesh axis runs over, the one named last changes fastest.
Arguments:
- fields: bfloat16 [16, 8, 2, 6, 2, 128, 128], P(('ens', 'mom'), 'src'), parts along dimension 0, may hold values from -0.29882812 to 0.29882812
- block_cols: int32 [16, 8, 6, 2], P(('ens', 'mom'), 'src'), parts along dimension 0, may hold values from 0 to 5, as said below
- sources: int32 [2], P('src'), may hold values from 0 to 7, as said below
- deltas: int32 [4], replicated, may hold values from 1 to 7
- partner: int32 [8], P('mom'), may hold values from 0 to 7, as said below
Outputs:
- correlator: float32 [2, 4, 16], P(None, 'src', ('ens', 'mom')), parts along dimension 2
The draws below stay inside these ranges and needn't reach their ends.
There are 2 independent parts, one for each index of `ens`. The reference program is written for one: setup_inputs(seed, part) draws one part's arguments, and reference() takes and returns one part's arrays. A program takes and returns all parts, laid end to end along the dimension named above; an argument that names none is the same for every part. Nothing has to cross between parts.
Inputs may be any that keep to these rules, and one draw needn't show every extreme that they name: `block_cols`: within each block row of each field the 2 block columns are distinct. `sources`: entry s lies among the timeslices s * 4 to (s + 1) * 4 - 1. partner is an involution without fixed points. Momenta g * 1 to (g + 1) - 1 form group g; the partners of group g's momenta are the momenta of group g XOR (8 / 2).
All inputs are finite; a program needn't handle non-finite values.
Results may differ from the reference program's by a relative error of at most 0.0095.
Values may be sent and summed in bfloat16 or wider, within the bound.
No kernel may reach another device: no remote copies, remote signals or barrier semaphores. Data moves between devices by JAX's collectives and lax.ppermute only.
A program may use at most 128 MiB of HBM per device.

```python
import jax
import jax.numpy as jnp
from jax import lax

BS = 128
NB = 6
ROWNZ = 2
MOM_DEV = 1
TS_DEV = 4
NDELTA = 4
MOM = 8
TIMES = 8
SRC = 2


def draw_block_cols(key, part):
    key = jax.random.fold_in(key, 11)
    total_rows = MOM * TIMES * NB
    key_list = jax.random.split(key, total_rows)
    orders = jax.vmap(lambda single: jax.random.permutation(single, NB))(key_list)
    return orders[:, :ROWNZ].reshape(MOM, TIMES, NB, ROWNZ).astype(jnp.int32)


def draw_sources(key, part):
    key = jax.random.fold_in(key, 27)
    offsets = jax.random.randint(key, (SRC,), 0, TS_DEV, dtype=jnp.int32)
    return (jnp.arange(SRC, dtype=jnp.int32) * TS_DEV + offsets).astype(jnp.int32)


def draw_partner(key, part):
    key = jax.random.fold_in(key, 41)
    groups = MOM // MOM_DEV
    half_groups = groups // 2
    scores = jax.random.randint(key, (half_groups, MOM_DEV), 0, 1 << 20, dtype=jnp.int32)
    scores = scores * MOM_DEV + jnp.arange(MOM_DEV, dtype=jnp.int32)[None, :]
    orders = jnp.argsort(scores, axis=1, stable=True).astype(jnp.int32)
    inverse = jnp.argsort(orders, axis=1, stable=True).astype(jnp.int32)
    group_ids = jnp.arange(half_groups, dtype=jnp.int32)[:, None]
    low_side = (group_ids + half_groups) * MOM_DEV + orders
    high_side = group_ids * MOM_DEV + inverse
    return jnp.concatenate([low_side, high_side], axis=0).reshape(MOM).astype(jnp.int32)


def touch_ends(array, rng, low, largest):
    longest = array.shape.index(max(array.shape))
    spots = []
    for shift in (0, 1):
        where = [jax.random.randint(jax.random.fold_in(rng, axis), (), 0, length) for axis, length in enumerate(array.shape)]
        where[longest] = (where[longest] + shift) % array.shape[longest]
        spots.append(tuple(where))
    return array.at[spots[0]].set(low).at[spots[1]].set(largest)


def levels(rng, extent, cuts, low, largest):
    level = 1.0
    for axis_at, parts in cuts:
        draws = jax.random.uniform(jax.random.fold_in(jax.random.fold_in(rng, 6), axis_at), (parts,), jnp.float32, low / len(cuts), largest / len(cuts))
        level = level * jnp.repeat(jnp.exp(draws), extent[axis_at] // parts).reshape((-1,) + (1,) * (len(extent) - 1 - axis_at))
    return level


def centred(rng, shape, scale, limit, pieces=(), held_as=jnp.bfloat16):
    values = jax.random.normal(rng, shape, jnp.float32) * scale
    if len(pieces) > 0:
        values = levels(rng, shape, pieces, -0.22, 0.18) * values
    return jnp.clip(values, min=-limit, max=limit).astype(held_as)


def setup_inputs(seed: int = 0, part: int = 0) -> dict:
    splits = jax.random.split(jax.random.key(seed), 6)
    part_splits = jax.random.split(jax.random.fold_in(splits[5], part), 6)
    return {
        "fields": centred(part_splits[0], (MOM, TIMES, 2, NB, ROWNZ, BS, BS), 0.05, 0.29882812, ((0, 8), (1, 2))),
        "block_cols": draw_block_cols(jax.random.fold_in(jax.random.fold_in(splits[5], part), 71), part),
        "sources": draw_sources(jax.random.fold_in(splits[5], 71), part),
        "deltas": touch_ends(jax.random.randint(splits[3], (NDELTA,), 1, TIMES), jax.random.fold_in(splits[3], 1), 1, TIMES - 1).astype(jnp.int32),
        "partner": draw_partner(jax.random.fold_in(splits[5], 71), part),
    }


def block_product(left, left_cols, right, right_cols):
    row_blocks = left.shape[1]
    per_row = left.shape[2]
    block_size = left.shape[3]
    flat_cols = left_cols.reshape(-1).astype(jnp.int32)
    picked = jnp.take(right, flat_cols, axis=1).reshape(2, row_blocks, per_row, per_row, block_size, block_size)
    target = jnp.take(right_cols, flat_cols, axis=0).reshape(row_blocks, per_row, per_row)
    left_wide = left.astype(jnp.float32)
    picked_wide = picked.astype(jnp.float32)
    real_part = jnp.einsum("rjab,rjkbe->rjkae", left_wide[0], picked_wide[0]) - jnp.einsum("rjab,rjkbe->rjkae", left_wide[1], picked_wide[1])
    imag_part = jnp.einsum("rjab,rjkbe->rjkae", left_wide[0], picked_wide[1]) + jnp.einsum("rjab,rjkbe->rjkae", left_wide[1], picked_wide[0])
    onehot = (target[..., None] == jnp.arange(row_blocks, dtype=jnp.int32)).astype(jnp.float32)
    stacked = jnp.stack([real_part, imag_part])
    combined = jnp.einsum("rjkc,xrjkae->xrace", onehot, stacked, precision=lax.Precision.HIGHEST)
    return combined.reshape(2, row_blocks * block_size, row_blocks * block_size).astype(jnp.bfloat16)


def pair_term(first, second):
    first_wide = first.astype(jnp.float32)
    second_wide = second.astype(jnp.float32)
    trace_first = jnp.trace(first_wide, axis1=1, axis2=2)
    trace_second = jnp.trace(second_wide, axis1=1, axis2=2)
    direct_real = trace_first[0] * trace_second[0] - trace_first[1] * trace_second[1]
    direct_imag = trace_first[0] * trace_second[1] + trace_first[1] * trace_second[0]
    second_flip = jnp.swapaxes(second_wide, 1, 2)
    cross_real = jnp.sum(first_wide[0] * second_flip[0] - first_wide[1] * second_flip[1])
    cross_imag = jnp.sum(first_wide[0] * second_flip[1] + first_wide[1] * second_flip[0])
    return jnp.stack([direct_real - cross_real, direct_imag - cross_imag])


def reference(fields, block_cols, sources, deltas, partner):
    def one_momentum(momentum):
        mirror = partner[momentum]

        def one_source(source_row):
            source_time = sources[source_row]

            def one_delta(delta_row):
                sink_time = ((source_time + deltas[delta_row]) % TIMES).astype(jnp.int32)
                first = block_product(fields[momentum, source_time], block_cols[momentum, source_time], fields[mirror, sink_time], block_cols[mirror, sink_time])
                second = block_product(fields[mirror, source_time], block_cols[mirror, source_time], fields[momentum, sink_time], block_cols[momentum, sink_time])
                return pair_term(first, second)

            return lax.map(one_delta, jnp.arange(NDELTA, dtype=jnp.int32))

        return jnp.sum(lax.map(one_source, jnp.arange(SRC, dtype=jnp.int32)), axis=0)

    per_momentum = lax.map(one_momentum, jnp.arange(MOM, dtype=jnp.int32))
    return jnp.transpose(per_momentum, (2, 1, 0))
```

```python
import functools

import jax
import jax.numpy as jnp
from jax import lax
from jax.experimental import pallas as pl
from jax.experimental.pallas import tpu as pltpu
from jax.sharding import PartitionSpec as P

F32 = jnp.float32
BF16 = jnp.bfloat16


def one_way_pairs(count):
    half = count // 2
    outer = half // 2
    return [(g + half, g) if g < outer else (g, g + half) for g in range(half)]


def weights_kernel(
    order_ref, a_cols, d_cols, b_cols, m_cols, a_ref, d_ref, b_ref, u_ref, la, ld, bs, yacc, yn, uacc
):
    slot = pl.program_id(0)
    rows, per_row, size = a_ref.shape[1], a_ref.shape[2], a_ref.shape[3]
    base = slot * rows * per_row
    lo, hi = pl.ds(0, size), pl.ds(size, size)

    @pl.when(slot == 0)
    def _():
        for r in range(rows):
            for j in range(per_row):
                real, imag = a_ref[0, r, j], a_ref[1, r, j]
                la[r, j, lo, lo] = real
                la[r, j, lo, hi] = -imag
                la[r, j, hi, lo] = imag
                la[r, j, hi, hi] = real
                real, imag = d_ref[0, r, j].T, d_ref[1, r, j].T
                up, down = pl.ds(2 * j * size, size), pl.ds((2 * j + 1) * size, size)
                ld[r, up, lo] = real
                ld[r, up, hi] = -imag
                ld[r, down, lo] = imag
                ld[r, down, hi] = real

    for r in range(rows):
        for j in range(per_row):
            bs[r, lo, pl.ds(j * size, size)] = b_ref[0, 0, r, j]
            bs[r, hi, pl.ds(j * size, size)] = b_ref[0, 1, r, j]

    yacc[...] = jnp.zeros_like(yacc)
    for r in range(rows):
        for j in range(per_row):
            inner = a_cols[r * per_row + j]
            part = jnp.dot(la[r, j], bs[inner], preferred_element_type=F32)
            for k in range(per_row):
                col = b_cols[base + inner * per_row + k]
                yacc[r, col] += part[:, k * size : (k + 1) * size]

    diagonal = lax.broadcasted_iota(jnp.int32, (size, size), 0) == lax.broadcasted_iota(
        jnp.int32, (size, size), 1
    )
    trace_real = jnp.zeros((size, size), F32)
    trace_imag = jnp.zeros((size, size), F32)
    for col in range(rows):
        for r in range(rows):
            real = yacc[r, col, lo].astype(BF16)
            imag = yacc[r, col, hi].astype(BF16)
            yn[col, pl.ds(r * size, size), lo] = real
            yn[col, pl.ds(r * size, size), hi] = imag
            if r == col:
                trace_real += real.astype(F32)
                trace_imag += imag.astype(F32)
    trace_real = jnp.sum(jnp.where(diagonal, trace_real, 0.0))
    trace_imag = jnp.sum(jnp.where(diagonal, trace_imag, 0.0))

    uacc[...] = jnp.zeros_like(uacc)
    wide = 2 if rows % 2 == 0 else 1
    for r in range(rows):
        for pair in range(rows // wide):
            part = lax.dot_general(
                ld[r],
                yn[r, pl.ds(pair * wide * size, wide * size)],
                (((1,), (1,)), ((), ())),
                preferred_element_type=F32,
            )
            for j in range(per_row):
                row = d_cols[r * per_row + j]
                for k in range(wide):
                    uacc[row, pair * wide + k] += part[
                        2 * j * size : 2 * (j + 1) * size, k * size : (k + 1) * size
                    ]

    for r in range(rows):
        for j in range(per_row):
            col = m_cols[base + r * per_row + j]
            pick = jnp.int32(0)
            found = jnp.int32(0)
            for k in range(per_row):
                hit = d_cols[col * per_row + k] == r
                pick = jnp.where(hit, k, pick)
                found = jnp.where(hit, 1, found)
            keep = found.astype(F32)
            at = pl.multiple_of(pick * 2 * size, 2 * size)
            real = ld[col, pl.ds(at, size), lo].astype(F32)
            imag = ld[col, pl.ds(at + size, size), lo].astype(F32)
            weight_real, weight_imag = trace_real * keep, trace_imag * keep
            u_ref[0, r, j, 0] = weight_real * real - weight_imag * imag - uacc[r, col, lo]
            u_ref[0, r, j, 1] = weight_real * imag + weight_imag * real - uacc[r, col, hi]


def weights(order, a_cols, d_cols, b_cols, m_cols, a, d, fields):
    times = fields.shape[0]
    _, rows, per_row, size, _ = a.shape
    whole = lambda slot, *_: (0, 0, 0, 0, 0)
    return pl.pallas_call(
        weights_kernel,
        out_shape=jax.ShapeDtypeStruct((times, rows, per_row, 2, size, size), F32),
        grid_spec=pltpu.PrefetchScalarGridSpec(
            num_scalar_prefetch=5,
            grid=(times,),
            in_specs=[
                pl.BlockSpec(a.shape, whole),
                pl.BlockSpec(a.shape, whole),
                pl.BlockSpec((1,) + a.shape, lambda slot, order, *_: (order[slot], 0, 0, 0, 0, 0)),
            ],
            out_specs=pl.BlockSpec(
                (1, rows, per_row, 2, size, size), lambda slot, *_: (slot, 0, 0, 0, 0, 0)
            ),
            scratch_shapes=[
                pltpu.VMEM((rows, per_row, 2 * size, 2 * size), BF16),
                pltpu.VMEM((rows, per_row * 2 * size, 2 * size), BF16),
                pltpu.VMEM((rows, 2 * size, per_row * size), BF16),
                pltpu.VMEM((rows, rows, 2 * size, size), F32),
                pltpu.VMEM((rows, rows * size, 2 * size), BF16),
                pltpu.VMEM((rows, rows, 2 * size, size), F32),
            ],
        ),
        compiler_params=pltpu.CompilerParams(vmem_limit_bytes=40 * 2**20),
        cost_estimate=pl.CostEstimate(
            flops=times * 1_600_000_000, bytes_accessed=times * 8_000_000, transcendentals=0
        ),
        name="weights",
    )(order, a_cols, d_cols, b_cols, m_cols, a, d, fields)


def products(field_ref, u_refs, acc):
    per_row, size = field_ref.shape[2], field_ref.shape[3]
    for j in range(per_row):
        real = field_ref[0, 0, j].astype(F32)
        imag = field_ref[1, 0, j].astype(F32)
        for s, u_ref in enumerate(u_refs):
            u_real, u_imag = u_ref[0, 0, j, 0], u_ref[0, 0, j, 1]
            fold = lambda x: jnp.sum(x.reshape(size // 8, 8, size), axis=0)
            acc[2 * s] += fold(real * u_real - imag * u_imag)
            acc[2 * s + 1] += fold(real * u_imag + imag * u_real)


def inner_kernel(field_ref, u0_ref, u1_ref, out_ref):
    @pl.when(pl.program_id(0) == 0)
    def _():
        out_ref[...] = jnp.zeros_like(out_ref)

    products(field_ref, (u0_ref, u1_ref), out_ref)


def last_kernel(times_ref, sinks_ref, *refs):
    *earlier, field_ref, u0_ref, u1_ref, out_ref, acc = refs
    slots = len(earlier) + 1
    deltas = out_ref.shape[0] // 2

    @pl.when(pl.program_id(0) == 0)
    def _():
        acc[...] = jnp.zeros_like(acc)

    products(field_ref, (u0_ref, u1_ref), acc)

    @pl.when(pl.program_id(0) == pl.num_programs(0) - 1)
    def _():
        lines = [jnp.zeros((8, acc.shape[2]), F32) for _ in range(2 * deltas)]
        for slot in range(slots):
            held = acc if slot == slots - 1 else earlier[slot]
            for s in range(2):
                for k in range(deltas):
                    keep = (sinks_ref[s * deltas + k] == times_ref[slot]).astype(F32)
                    for part in range(2):
                        lines[part * deltas + k] += keep * held[2 * s + part]
        table = jnp.concatenate([jnp.sum(line, axis=0, keepdims=True) for line in lines], axis=0)
        out_ref[...] = jnp.broadcast_to(jnp.sum(table, axis=1, keepdims=True), out_ref.shape)


def field_specs(field, slot):
    _, rows, per_row, size, _ = field.shape
    return [
        pl.BlockSpec((2, 1, per_row, size, size), lambda r, *_: (0, r, 0, 0, 0)),
        pl.BlockSpec((1, 1, per_row, 2, size, size), lambda r, *_: (slot, r, 0, 0, 0, 0)),
        pl.BlockSpec((1, 1, per_row, 2, size, size), lambda r, *_: (slot, r, 0, 0, 0, 0)),
    ]


def inner(field, u0, u1, slot):
    rows, size = field.shape[1], field.shape[3]
    return pl.pallas_call(
        inner_kernel,
        out_shape=jax.ShapeDtypeStruct((4, 8, size), F32),
        grid=(rows,),
        in_specs=field_specs(field, slot),
        out_specs=pl.BlockSpec((4, 8, size), lambda r: (0, 0, 0)),
        cost_estimate=pl.CostEstimate(flops=4_000_000, bytes_accessed=4_000_000, transcendentals=0),
        name="inner",
    )(field, u0, u1)


def last(times, sinks, earlier, field, u0, u1):
    rows, size = field.shape[1], field.shape[3]
    lines = sinks.shape[0]
    whole = pl.BlockSpec((4, 8, size), lambda r, *_: (0, 0, 0))
    return pl.pallas_call(
        last_kernel,
        out_shape=jax.ShapeDtypeStruct((lines, size), F32),
        grid_spec=pltpu.PrefetchScalarGridSpec(
            num_scalar_prefetch=2,
            grid=(rows,),
            in_specs=[whole] * len(earlier) + field_specs(field, len(earlier)),
            out_specs=pl.BlockSpec((lines, size), lambda r, *_: (0, 0)),
            scratch_shapes=[pltpu.VMEM((4, 8, size), F32)],
        ),
        cost_estimate=pl.CostEstimate(flops=4_000_000, bytes_accessed=4_000_000, transcendentals=0),
        name="last",
    )(times, sinks, *earlier, field, u0, u1)


def local(fields, block_cols, sources, deltas, partner):
    assert fields.shape[0] == 1 and lax.axis_size("src") == 2
    del partner
    fields, block_cols = fields[0], block_cols[0]
    times, _, rows, per_row, size, _ = fields.shape
    per_field = rows * per_row
    total_times = 2 * times
    delta_count = deltas.shape[0]
    core = lax.axis_index("src")
    pairs = one_way_pairs(lax.axis_size("mom"))
    swap = lambda value: lax.ppermute(value, "src", [(0, 1), (1, 0)])
    to_partner = lambda value: lax.ppermute(value, "mom", pairs)

    source = sources[0] - core * times
    order = (source + jnp.arange(times, dtype=jnp.int32)) % times
    picked = [lax.dynamic_index_in_dim(fields, order[i], 0, keepdims=False) for i in range(times)]
    far = [to_partner(field) for field in picked]

    cols = jnp.take(block_cols.reshape(times, per_field), order, axis=0).reshape(-1)
    pack = jnp.concatenate([cols, sources])
    other_pack = swap(pack)
    far_pack, far_other_pack = jnp.split(to_partner(jnp.concatenate([pack, other_pack])), 2)
    m_cols = far_pack[:-1]
    other_source = other_pack[-1]
    other_field = swap(picked[0])
    far_other = swap(far[0])

    u0 = weights(order, far_pack[:per_field], cols[:per_field], cols, m_cols, far[0], picked[0], fields)
    u1 = weights(
        order, far_other_pack[:per_field], other_pack[:per_field], cols, m_cols, far_other, other_field, fields
    )
    sinks = jnp.concatenate(
        [(sources[0] + deltas) % total_times, (other_source + deltas) % total_times]
    )
    slot_times = order + core * times
    earlier = [inner(far[i], u0, u1, i) for i in range(times - 1)]
    own = last(slot_times, sinks, earlier, far[-1], u0, u1)

    both = ("mom", "src")
    straight = [(2 * a + c, 2 * b + c) for b, a in pairs for c in range(2)]
    crossed = [(2 * a + c, 2 * b + 1 - c) for b, a in pairs for c in range(2)]
    total = own + swap(own) + lax.ppermute(own, both, straight) + lax.ppermute(own, both, crossed)
    total = total[:, :1].reshape(2, delta_count, 1)
    share = delta_count // 2
    return lax.dynamic_slice_in_dim(total, core * share, share, axis=1)


def solution(mesh):
    in_specs = (
        P(("ens", "mom"), "src", None, None, None, None, None),
        P(("ens", "mom"), "src", None, None),
        P("src"),
        P(),
        P("mom"),
    )
    out_specs = P(None, "src", ("ens", "mom"))
    return jax.shard_map(local, mesh=mesh, in_specs=in_specs, out_specs=out_specs, check_vma=False)
```

```python
import jax
import jax.numpy as jnp
from jax import lax
from jax.experimental import pallas as pl
from jax.experimental.pallas import tpu as pltpu
from jax.sharding import PartitionSpec as P

F32 = jnp.float32
BF16 = jnp.bfloat16
I32 = jnp.int32
SMEM = pl.BlockSpec(memory_space=pltpu.SMEM)
VMEM = pl.BlockSpec(memory_space=pltpu.VMEM)
ANY = pl.BlockSpec(memory_space=pl.ANY)


def one_way_pairs(count):
    half = count // 2
    outer = half // 2
    return [(g + half, g) if g < outer else (g, g + half) for g in range(half)]


def cost(flops, size):
    return pl.CostEstimate(flops=flops, bytes_accessed=size, transcendentals=0)


def pick_source_kernel(source_ref, fields_ref, out_ref, sem):
    time = lax.rem(source_ref[0], I32(fields_ref.shape[0]))
    copy = pltpu.make_async_copy(fields_ref.at[time], out_ref, sem)
    copy.start()
    copy.wait()


def pick_source(source, fields):
    return pl.pallas_call(
        pick_source_kernel,
        out_shape=jax.ShapeDtypeStruct(fields.shape[1:], fields.dtype),
        in_specs=[SMEM, ANY],
        out_specs=ANY,
        scratch_shapes=[pltpu.SemaphoreType.DMA],
        cost_estimate=cost(0, 1_600_000),
        compiler_params=pltpu.CompilerParams(vmem_limit_bytes=60 * 2**20),
        name="pick_source",
    )(source, fields)


def pick_kernel(order_ref, fields_ref, *refs):
    *outs, sems = refs
    copies = [
        pltpu.make_async_copy(fields_ref.at[order_ref[slot + 1]], out, sems.at[slot])
        for slot, out in enumerate(outs)
    ]
    for copy in copies:
        copy.start()
    for copy in copies:
        copy.wait()


def pick_others(order, fields):
    others = fields.shape[0] - 1
    return pl.pallas_call(
        pick_kernel,
        out_shape=[jax.ShapeDtypeStruct(fields.shape[1:], fields.dtype)] * others,
        in_specs=[SMEM, ANY],
        out_specs=[ANY] * others,
        scratch_shapes=[pltpu.SemaphoreType.DMA((others,))],
        cost_estimate=cost(0, others * 1_600_000),
        compiler_params=pltpu.CompilerParams(vmem_limit_bytes=60 * 2**20),
        name="pick_others",
    )(order, fields)


def plan_kernel(core_ref, own_ref, other_ref, deltas_ref, order_ref, sinks_ref):
    times = order_ref.shape[0]
    deltas = deltas_ref.shape[0]
    sinks = []
    for s, ref in enumerate((own_ref, other_ref)):
        for k in range(deltas):
            sink = lax.rem(ref[0] + deltas_ref[k], I32(2 * times))
            sinks_ref[s * deltas + k] = sink
            sinks.append(sink)
    base = core_ref[0] * times
    first = own_ref[0] - base
    keys = []
    for t in range(times):
        needed = sinks[0] == base + t
        for sink in sinks[1:]:
            needed = needed | (sink == base + t)
        key = jnp.where(needed, I32(t), I32(times + t))
        keys.append(jnp.where(first == t, I32(-1), key))
    for t in range(times):
        rank = I32(0)
        for other in range(times):
            if other != t:
                rank += (keys[other] < keys[t]).astype(I32)
        order_ref[rank] = I32(t)


def plan(core, own, other, deltas, times):
    return pl.pallas_call(
        plan_kernel,
        out_shape=[
            jax.ShapeDtypeStruct((times,), I32),
            jax.ShapeDtypeStruct((2 * deltas.shape[0],), I32),
        ],
        in_specs=[SMEM] * 4,
        out_specs=[SMEM] * 2,
        cost_estimate=cost(0, 1000),
        name="plan",
    )(core, own, other, deltas)


def weights_kernel(
    order_ref, far_ref, own_ref, far_cols, own_cols, m_cols, b_cols, a_ref, d_ref, b_ref, u_ref, la, ld, bs, yn
):
    slot = pl.program_id(0)
    rows, per_row, size = a_ref.shape[1], a_ref.shape[2], a_ref.shape[3]
    times = order_ref.shape[0]
    step = rows * per_row
    base = order_ref[slot] * step
    a_base = lax.rem(far_ref[0], I32(times)) * step
    d_base = lax.rem(own_ref[0], I32(times)) * step
    lo, hi = pl.ds(0, size), pl.ds(size, size)

    @pl.when(slot == 0)
    def _():
        for r in range(rows):
            for j in range(per_row):
                real, imag = a_ref[0, r, j], a_ref[1, r, j]
                la[r, j, lo, lo] = real
                la[r, j, lo, hi] = -imag
                la[r, j, hi, lo] = imag
                la[r, j, hi, hi] = real
                real, imag = d_ref[0, r, j].T, d_ref[1, r, j].T
                ld[r, j, lo, lo] = real
                ld[r, j, lo, hi] = -imag
                ld[r, j, hi, lo] = imag
                ld[r, j, hi, hi] = real

    for r in range(rows):
        for j in range(per_row):
            bs[r, lo, pl.ds(j * size, size)] = b_ref[0, 0, r, j]
            bs[r, hi, pl.ds(j * size, size)] = b_ref[0, 1, r, j]

    yn[...] = jnp.zeros_like(yn)
    for r in range(rows):
        inners = [far_cols[a_base + r * per_row + j] for j in range(per_row)]
        parts = [
            jnp.dot(la[r, j], bs[inners[j]], preferred_element_type=F32) for j in range(per_row)
        ]
        pieces = []
        for j in range(per_row):
            for k in range(per_row):
                col = b_cols[base + inners[j] * per_row + k]
                pieces.append((j, col, parts[j][:, k * size : (k + 1) * size]))
        for at in reversed(range(len(pieces))):
            j, col, value = pieces[at]
            for other_j, other_col, other in pieces:
                if other_j > j:
                    value = value + jnp.where(other_col == col, 1.0, 0.0) * other
            yn[col, pl.ds(r * size, size), lo] = value[:size].astype(BF16)
            yn[col, pl.ds(r * size, size), hi] = value[size:].astype(BF16)

    trace_real = jnp.zeros((size, size), F32)
    trace_imag = jnp.zeros((size, size), F32)
    for r in range(rows):
        trace_real += yn[r, pl.ds(r * size, size), lo].astype(F32)
        trace_imag += yn[r, pl.ds(r * size, size), hi].astype(F32)
    diagonal = lax.broadcasted_iota(I32, (size, size), 0) == lax.broadcasted_iota(I32, (size, size), 1)
    trace_real = jnp.sum(jnp.where(diagonal, trace_real, 0.0))
    trace_imag = jnp.sum(jnp.where(diagonal, trace_imag, 0.0))

    for r in range(rows):
        for j in range(per_row):
            col = m_cols[base + r * per_row + j]
            pick = I32(0)
            keep = F32(0)
            for k in range(per_row):
                hit = own_cols[d_base + col * per_row + k] == r
                pick = jnp.where(hit, I32(k), pick)
                keep = jnp.where(hit, F32(1), keep)
            real = ld[col, pick, lo, lo].astype(F32)
            imag = ld[col, pick, hi, lo].astype(F32)
            weight_real, weight_imag = trace_real * keep, trace_imag * keep
            u_ref[0, r, j, 0] = weight_real * real - weight_imag * imag
            u_ref[0, r, j, 1] = weight_real * imag + weight_imag * real

    for i in range(rows):
        for j in range(per_row):
            r = own_cols[d_base + i * per_row + j]
            met = [m_cols[base + r * per_row + k] for k in range(per_row)]
            right = jnp.concatenate(
                [yn[i, pl.ds(pl.multiple_of(col * size, size), size)] for col in met], axis=0
            )
            part = lax.dot_general(
                ld[i, j], right, (((1,), (1,)), ((), ())), preferred_element_type=F32
            )
            for k in range(per_row):
                u_ref[0, r, k, 0] -= part[:size, k * size : (k + 1) * size]
                u_ref[0, r, k, 1] -= part[size:, k * size : (k + 1) * size]


def weights(order, far_time, own_time, far_cols, own_cols, m_cols, b_cols, a, d, fields):
    times = fields.shape[0]
    _, rows, per_row, size, _ = a.shape
    whole = lambda slot, *_: (0, 0, 0, 0, 0)
    return pl.pallas_call(
        weights_kernel,
        out_shape=jax.ShapeDtypeStruct((times, rows, per_row, 2, size, size), F32),
        grid_spec=pltpu.PrefetchScalarGridSpec(
            num_scalar_prefetch=7,
            grid=(times,),
            in_specs=[
                pl.BlockSpec(a.shape, whole),
                pl.BlockSpec(a.shape, whole),
                pl.BlockSpec((1,) + a.shape, lambda slot, order, *_: (order[slot], 0, 0, 0, 0, 0)),
            ],
            out_specs=pl.BlockSpec(
                (1, rows, per_row, 2, size, size), lambda slot, *_: (slot, 0, 0, 0, 0, 0)
            ),
            scratch_shapes=[
                pltpu.VMEM((rows, per_row, 2 * size, 2 * size), BF16),
                pltpu.VMEM((rows, per_row, 2 * size, 2 * size), BF16),
                pltpu.VMEM((rows, 2 * size, per_row * size), BF16),
                pltpu.VMEM((rows, rows * size, 2 * size), BF16),
            ],
        ),
        compiler_params=pltpu.CompilerParams(vmem_limit_bytes=24 * 2**20),
        cost_estimate=cost(times * 20_000_000_000, times * 8_000_000),
        name="weights",
    )(order, far_time, own_time, far_cols, own_cols, m_cols, b_cols, a, d, fields)


def products(field_ref, u_refs, slot):
    _, rows, per_row, size, _ = field_ref.shape
    chunk = min(size, 32)
    fold = lambda x: jnp.sum(x.reshape(chunk // 8, 8, size), axis=0)
    sums = [jnp.zeros((8, size), F32) for _ in range(2 * len(u_refs))]
    for r in range(rows):
        for j in range(per_row):
            for start in range(0, size, chunk):
                at = pl.ds(start, chunk)
                real = field_ref[0, r, j, at].astype(F32)
                imag = field_ref[1, r, j, at].astype(F32)
                for s, u_ref in enumerate(u_refs):
                    u_real, u_imag = u_ref[slot, r, j, 0, at], u_ref[slot, r, j, 1, at]
                    sums[2 * s] += fold(real * u_real - imag * u_imag)
                    sums[2 * s + 1] += fold(real * u_imag + imag * u_real)
    return sums


def inner_kernel(slot, field_ref, u0_ref, u1_ref, out_ref):
    for at, value in enumerate(products(field_ref, (u0_ref, u1_ref), slot)):
        out_ref[at] = value


def inner(slot, field, u0, u1):
    return pl.pallas_call(
        lambda *refs: inner_kernel(slot, *refs),
        out_shape=jax.ShapeDtypeStruct((4, 8, field.shape[-1]), F32),
        in_specs=[VMEM] * 3,
        out_specs=VMEM,
        cost_estimate=cost(4_000_000, 4_000_000),
        compiler_params=pltpu.CompilerParams(vmem_limit_bytes=24 * 2**20),
        name="inner",
    )(field, u0, u1)


def last_kernel(core_ref, order_ref, sinks_ref, *refs):
    *earlier, field_ref, u0_ref, u1_ref, mine_ref, theirs_ref = refs
    slots = order_ref.shape[0]
    deltas = sinks_ref.shape[0] // 2
    share = deltas // 2
    core = core_ref[0]
    sums = [[ref[at] for at in range(4)] for ref in earlier]
    sums.append(products(field_ref, (u0_ref, u1_ref), slots - 1))
    for out_ref, owner in ((mine_ref, core), (theirs_ref, 1 - core)):
        lines = [jnp.zeros(sums[0][0].shape, F32) for _ in range(2 * share)]
        for slot in range(slots):
            time = core * slots + order_ref[slot]
            for s in range(2):
                for k in range(share):
                    sink = sinks_ref[s * deltas + owner * share + k]
                    keep = jnp.where(sink == time, F32(1), F32(0))
                    for part in range(2):
                        lines[part * share + k] += keep * sums[slot][2 * s + part]
        table = jnp.concatenate([jnp.sum(line, axis=0, keepdims=True) for line in lines], axis=0)
        table = jnp.sum(table, axis=1, keepdims=True)
        for part in range(2):
            out_ref[part] = table[part * share : (part + 1) * share]


def last(core, order, sinks, earlier, field, u0, u1):
    share = sinks.shape[0] // 4
    return pl.pallas_call(
        last_kernel,
        out_shape=[jax.ShapeDtypeStruct((2, share, 1), F32)] * 2,
        in_specs=[SMEM] * 3 + [VMEM] * (len(earlier) + 3),
        out_specs=[VMEM] * 2,
        cost_estimate=cost(4_000_000, 4_000_000),
        compiler_params=pltpu.CompilerParams(vmem_limit_bytes=24 * 2**20),
        name="last",
    )(core, order, sinks, *earlier, field, u0, u1)


def local(fields, block_cols, sources, deltas, partner):
    assert fields.shape[0] == 1 and lax.axis_size("src") == 2
    del partner
    fields = fields[0]
    times = fields.shape[0]
    core = lax.axis_index("src").reshape(1)
    pairs = one_way_pairs(lax.axis_size("mom"))
    swap = lambda value: lax.ppermute(value, "src", [(0, 1), (1, 0)])
    to_partner = lambda value: lax.ppermute(value, "mom", pairs)

    cols = block_cols.reshape(-1)
    far_cols = to_partner(cols)
    own_field = pick_source(sources, fields)
    far = [to_partner(own_field)]

    other_time = swap(sources)
    order, sinks = plan(core, sources, other_time, deltas, times)
    far += [to_partner(field) for field in pick_others(order, fields)]

    other_cols = swap(cols)
    far_other_cols = swap(far_cols)
    other_field = swap(own_field)
    far_other = swap(far[0])
    u0 = weights(order, sources, sources, far_cols, cols, far_cols, cols, far[0], own_field, fields)
    u1 = weights(
        order, other_time, other_time, far_other_cols, other_cols, far_cols, cols, far_other, other_field, fields
    )
    earlier = [inner(slot, far[slot], u0, u1) for slot in range(times - 1)]
    mine, theirs = last(core, order, sinks, earlier, far[-1], u0, u1)

    both = ("mom", "src")
    straight = [(2 * a + c, 2 * b + c) for b, a in pairs for c in range(2)]
    crossed = [(2 * a + c, 2 * b + 1 - c) for b, a in pairs for c in range(2)]
    return mine + swap(theirs) + lax.ppermute(mine, both, straight) + lax.ppermute(theirs, both, crossed)


def solution(mesh):
    in_specs = (
        P(("ens", "mom"), "src", None, None, None, None, None),
        P(("ens", "mom"), "src", None, None),
        P("src"),
        P(),
        P("mom"),
    )
    out_specs = P(None, "src", ("ens", "mom"))
    return jax.shard_map(local, mesh=mesh, in_specs=in_specs, out_specs=out_specs, check_vma=False)
```

```python
import jax
import jax.numpy as jnp
from jax import lax
from jax.experimental import pallas as pl
from jax.experimental.pallas import tpu as pltpu
from jax.sharding import PartitionSpec as P

F32 = jnp.float32
BF16 = jnp.bfloat16
I32 = jnp.int32
SMEM = pl.BlockSpec(memory_space=pltpu.SMEM)
VMEM = pl.BlockSpec(memory_space=pltpu.VMEM)
ANY = pl.BlockSpec(memory_space=pl.ANY)


def one_way_pairs(count):
    half = count // 2
    outer = half // 2
    return [(g + half, g) if g < outer else (g, g + half) for g in range(half)]


def cost(flops, size):
    return pl.CostEstimate(flops=flops, bytes_accessed=size, transcendentals=0)


def pick_source_kernel(source_ref, fields_ref, out_ref, sem):
    time = lax.rem(source_ref[0], I32(fields_ref.shape[0]))
    copy = pltpu.make_async_copy(fields_ref.at[time], out_ref, sem)
    copy.start()
    copy.wait()


def pick_source(source, fields):
    return pl.pallas_call(
        pick_source_kernel,
        out_shape=jax.ShapeDtypeStruct(fields.shape[1:], fields.dtype),
        in_specs=[SMEM, ANY],
        out_specs=VMEM,
        scratch_shapes=[pltpu.SemaphoreType.DMA],
        cost_estimate=cost(0, 1_600_000),
        compiler_params=pltpu.CompilerParams(vmem_limit_bytes=56 * 2**20),
        name="pick_source",
    )(source, fields)


def pick_kernel(order_ref, fields_ref, *refs):
    *outs, sems = refs
    copies = [
        pltpu.make_async_copy(fields_ref.at[order_ref[slot + 1]], out, sems.at[slot])
        for slot, out in enumerate(outs)
    ]
    for copy in copies:
        copy.start()
    for copy in copies:
        copy.wait()


def pick_others(order, fields):
    others = fields.shape[0] - 1
    return pl.pallas_call(
        pick_kernel,
        out_shape=[jax.ShapeDtypeStruct(fields.shape[1:], fields.dtype)] * others,
        in_specs=[SMEM, ANY],
        out_specs=[VMEM] * others,
        scratch_shapes=[pltpu.SemaphoreType.DMA((others,))],
        cost_estimate=cost(0, others * 1_600_000),
        compiler_params=pltpu.CompilerParams(vmem_limit_bytes=24 * 2**20),
        name="pick_others",
    )(order, fields)


def plan_kernel(core_ref, own_ref, other_ref, deltas_ref, order_ref, sinks_ref):
    times = order_ref.shape[0]
    deltas = deltas_ref.shape[0]
    sinks = []
    for s, ref in enumerate((own_ref, other_ref)):
        for k in range(deltas):
            sink = lax.rem(ref[0] + deltas_ref[k], I32(2 * times))
            sinks_ref[s * deltas + k] = sink
            sinks.append(sink)
    base = core_ref[0] * times
    first = own_ref[0] - base
    keys = []
    for t in range(times):
        needed = sinks[0] == base + t
        for sink in sinks[1:]:
            needed = needed | (sink == base + t)
        key = jnp.where(needed, I32(t), I32(times + t))
        keys.append(jnp.where(first == t, I32(-1), key))
    for t in range(times):
        rank = I32(0)
        for other in range(times):
            if other != t:
                rank += (keys[other] < keys[t]).astype(I32)
        order_ref[rank] = I32(t)


def plan(core, own, other, deltas, times):
    return pl.pallas_call(
        plan_kernel,
        out_shape=[
            jax.ShapeDtypeStruct((times,), I32),
            jax.ShapeDtypeStruct((2 * deltas.shape[0],), I32),
        ],
        in_specs=[SMEM] * 4,
        out_specs=[SMEM] * 2,
        cost_estimate=cost(0, 1000),
        name="plan",
    )(core, own, other, deltas)


def weights_kernel(
    order_ref, far_ref, own_ref, far_cols, own_cols, m_cols, b_cols, a_ref, d_ref, b_ref, u_ref, la, ld, bs, yn
):
    slot = pl.program_id(0)
    rows, per_row, size = a_ref.shape[1], a_ref.shape[2], a_ref.shape[3]
    times = order_ref.shape[0]
    step = rows * per_row
    base = order_ref[slot] * step
    a_base = lax.rem(far_ref[0], I32(times)) * step
    d_base = lax.rem(own_ref[0], I32(times)) * step
    lo, hi = pl.ds(0, size), pl.ds(size, size)

    @pl.when(slot == 0)
    def _():
        for r in range(rows):
            for j in range(per_row):
                real, imag = a_ref[0, r, j], a_ref[1, r, j]
                la[r, j, lo, lo] = real
                la[r, j, lo, hi] = -imag
                la[r, j, hi, lo] = imag
                la[r, j, hi, hi] = real
                real, imag = d_ref[0, r, j].T, d_ref[1, r, j].T
                ld[r, j, lo, lo] = real
                ld[r, j, lo, hi] = -imag
                ld[r, j, hi, lo] = imag
                ld[r, j, hi, hi] = real

    for r in range(rows):
        for j in range(per_row):
            bs[r, lo, pl.ds(j * size, size)] = b_ref[0, 0, r, j]
            bs[r, hi, pl.ds(j * size, size)] = b_ref[0, 1, r, j]

    yn[...] = jnp.zeros_like(yn)
    for r in range(rows):
        inners = [far_cols[a_base + r * per_row + j] for j in range(per_row)]
        parts = [
            jnp.dot(la[r, j], bs[inners[j]], preferred_element_type=F32) for j in range(per_row)
        ]
        pieces = []
        for j in range(per_row):
            for k in range(per_row):
                col = b_cols[base + inners[j] * per_row + k]
                pieces.append((j, col, parts[j][:, k * size : (k + 1) * size]))
        for at in reversed(range(len(pieces))):
            j, col, value = pieces[at]
            for other_j, other_col, other in pieces:
                if other_j > j:
                    value = value + jnp.where(other_col == col, 1.0, 0.0) * other
            yn[col, pl.ds(r * size, size), lo] = value[:size].astype(BF16)
            yn[col, pl.ds(r * size, size), hi] = value[size:].astype(BF16)

    trace_real = jnp.zeros((size, size), F32)
    trace_imag = jnp.zeros((size, size), F32)
    for r in range(rows):
        trace_real += yn[r, pl.ds(r * size, size), lo].astype(F32)
        trace_imag += yn[r, pl.ds(r * size, size), hi].astype(F32)
    diagonal = lax.broadcasted_iota(I32, (size, size), 0) == lax.broadcasted_iota(I32, (size, size), 1)
    trace_real = jnp.sum(jnp.where(diagonal, trace_real, 0.0))
    trace_imag = jnp.sum(jnp.where(diagonal, trace_imag, 0.0))

    for r in range(rows):
        for j in range(per_row):
            col = m_cols[base + r * per_row + j]
            pick = I32(0)
            keep = F32(0)
            for k in range(per_row):
                hit = own_cols[d_base + col * per_row + k] == r
                pick = jnp.where(hit, I32(k), pick)
                keep = jnp.where(hit, F32(1), keep)
            real = ld[col, pick, lo, lo].astype(F32)
            imag = ld[col, pick, hi, lo].astype(F32)
            weight_real, weight_imag = trace_real * keep, trace_imag * keep
            u_ref[0, r, j, 0] = weight_real * real - weight_imag * imag
            u_ref[0, r, j, 1] = weight_real * imag + weight_imag * real

    for i in range(rows):
        for j in range(per_row):
            r = own_cols[d_base + i * per_row + j]
            met = [m_cols[base + r * per_row + k] for k in range(per_row)]
            right = jnp.concatenate(
                [yn[i, pl.ds(pl.multiple_of(col * size, size), size)] for col in met], axis=0
            )
            part = lax.dot_general(
                ld[i, j], right, (((1,), (1,)), ((), ())), preferred_element_type=F32
            )
            for k in range(per_row):
                u_ref[0, r, k, 0] -= part[:size, k * size : (k + 1) * size]
                u_ref[0, r, k, 1] -= part[size:, k * size : (k + 1) * size]


def weights(order, far_time, own_time, far_cols, own_cols, m_cols, b_cols, a, d, fields):
    times = fields.shape[0]
    _, rows, per_row, size, _ = a.shape
    whole = lambda slot, *_: (0, 0, 0, 0, 0)
    return pl.pallas_call(
        weights_kernel,
        out_shape=jax.ShapeDtypeStruct((times, rows, per_row, 2, size, size), F32),
        grid_spec=pltpu.PrefetchScalarGridSpec(
            num_scalar_prefetch=7,
            grid=(times,),
            in_specs=[
                pl.BlockSpec(a.shape, whole),
                pl.BlockSpec(a.shape, whole),
                pl.BlockSpec((1,) + a.shape, lambda slot, order, *_: (order[slot], 0, 0, 0, 0, 0)),
            ],
            out_specs=pl.BlockSpec(
                (1, rows, per_row, 2, size, size), lambda slot, *_: (slot, 0, 0, 0, 0, 0)
            ),
            scratch_shapes=[
                pltpu.VMEM((rows, per_row, 2 * size, 2 * size), BF16),
                pltpu.VMEM((rows, per_row, 2 * size, 2 * size), BF16),
                pltpu.VMEM((rows, 2 * size, per_row * size), BF16),
                pltpu.VMEM((rows, rows * size, 2 * size), BF16),
            ],
        ),
        compiler_params=pltpu.CompilerParams(vmem_limit_bytes=24 * 2**20),
        cost_estimate=cost(times * 20_000_000_000, times * 8_000_000),
        name="weights",
    )(order, far_time, own_time, far_cols, own_cols, m_cols, b_cols, a, d, fields)


def products(field_ref, u_refs, slot):
    _, rows, per_row, size, _ = field_ref.shape
    chunk = min(size, 32)
    fold = lambda x: jnp.sum(x.reshape(chunk // 8, 8, size), axis=0)
    sums = [jnp.zeros((8, size), F32) for _ in range(2 * len(u_refs))]
    for r in range(rows):
        for j in range(per_row):
            for start in range(0, size, chunk):
                at = pl.ds(start, chunk)
                real = field_ref[0, r, j, at].astype(F32)
                imag = field_ref[1, r, j, at].astype(F32)
                for s, u_ref in enumerate(u_refs):
                    u_real, u_imag = u_ref[slot, r, j, 0, at], u_ref[slot, r, j, 1, at]
                    sums[2 * s] += fold(real * u_real - imag * u_imag)
                    sums[2 * s + 1] += fold(real * u_imag + imag * u_real)
    return sums


def inner_kernel(slot, field_ref, u0_ref, u1_ref, out_ref):
    for at, value in enumerate(products(field_ref, (u0_ref, u1_ref), slot)):
        out_ref[at] = value


def inner(slot, field, u0, u1):
    return pl.pallas_call(
        lambda *refs: inner_kernel(slot, *refs),
        out_shape=jax.ShapeDtypeStruct((4, 8, field.shape[-1]), F32),
        in_specs=[VMEM] * 3,
        out_specs=VMEM,
        cost_estimate=cost(4_000_000, 4_000_000),
        compiler_params=pltpu.CompilerParams(vmem_limit_bytes=24 * 2**20),
        name="inner",
    )(field, u0, u1)


def last_kernel(core_ref, order_ref, sinks_ref, *refs):
    *earlier, field_ref, u0_ref, u1_ref, mine_ref, theirs_ref = refs
    slots = order_ref.shape[0]
    deltas = sinks_ref.shape[0] // 2
    share = deltas // 2
    core = core_ref[0]
    sums = [[ref[at] for at in range(4)] for ref in earlier]
    sums.append(products(field_ref, (u0_ref, u1_ref), slots - 1))
    for out_ref, owner in ((mine_ref, core), (theirs_ref, 1 - core)):
        lines = [jnp.zeros(sums[0][0].shape, F32) for _ in range(2 * share)]
        for slot in range(slots):
            time = core * slots + order_ref[slot]
            for s in range(2):
                for k in range(share):
                    sink = sinks_ref[s * deltas + owner * share + k]
                    keep = jnp.where(sink == time, F32(1), F32(0))
                    for part in range(2):
                        lines[part * share + k] += keep * sums[slot][2 * s + part]
        table = jnp.concatenate([jnp.sum(line, axis=0, keepdims=True) for line in lines], axis=0)
        table = jnp.sum(table, axis=1, keepdims=True)
        for part in range(2):
            out_ref[part] = table[part * share : (part + 1) * share]


def last(core, order, sinks, earlier, field, u0, u1):
    share = sinks.shape[0] // 4
    return pl.pallas_call(
        last_kernel,
        out_shape=[jax.ShapeDtypeStruct((2, share, 1), F32)] * 2,
        in_specs=[SMEM] * 3 + [VMEM] * (len(earlier) + 3),
        out_specs=[VMEM] * 2,
        cost_estimate=cost(4_000_000, 4_000_000),
        compiler_params=pltpu.CompilerParams(vmem_limit_bytes=24 * 2**20),
        name="last",
    )(core, order, sinks, *earlier, field, u0, u1)


def local(fields, block_cols, sources, deltas, partner):
    assert fields.shape[0] == 1 and lax.axis_size("src") == 2
    del partner
    fields = fields[0]
    times = fields.shape[0]
    core = lax.axis_index("src").reshape(1)
    pairs = one_way_pairs(lax.axis_size("mom"))
    swap = lambda value: lax.ppermute(value, "src", [(0, 1), (1, 0)])
    to_partner = lambda value: lax.ppermute(value, "mom", pairs)

    cols = block_cols.reshape(-1)
    far_cols = to_partner(cols)
    own_field = pick_source(sources, fields)
    far = [to_partner(own_field)]

    other_time = swap(sources)
    order, sinks = plan(core, sources, other_time, deltas, times)
    far += [to_partner(field) for field in pick_others(order, fields)]

    other_cols = swap(cols)
    far_other_cols = swap(far_cols)
    other_field = swap(own_field)
    far_other = swap(far[0])
    u0 = weights(order, sources, sources, far_cols, cols, far_cols, cols, far[0], own_field, fields)
    u1 = weights(
        order, other_time, other_time, far_other_cols, other_cols, far_cols, cols, far_other, other_field, fields
    )
    earlier = [inner(slot, far[slot], u0, u1) for slot in range(times - 1)]
    mine, theirs = last(core, order, sinks, earlier, far[-1], u0, u1)

    both = ("mom", "src")
    straight = [(2 * a + c, 2 * b + c) for b, a in pairs for c in range(2)]
    crossed = [(2 * a + c, 2 * b + 1 - c) for b, a in pairs for c in range(2)]
    return mine + swap(theirs) + lax.ppermute(mine, both, straight) + lax.ppermute(theirs, both, crossed)


def solution(mesh):
    in_specs = (
        P(("ens", "mom"), "src", None, None, None, None, None),
        P(("ens", "mom"), "src", None, None),
        P("src"),
        P(),
        P("mom"),
    )
    out_specs = P(None, "src", ("ens", "mom"))
    return jax.shard_map(local, mesh=mesh, in_specs=in_specs, out_specs=out_specs, check_vma=False)
```

```python
import jax
import jax.numpy as jnp
from jax import lax
from jax.experimental import pallas as pl
from jax.experimental.pallas import tpu as pltpu
from jax.sharding import PartitionSpec as P

F32 = jnp.float32
BF16 = jnp.bfloat16
I32 = jnp.int32
SMEM = pl.BlockSpec(memory_space=pltpu.SMEM)
VMEM = pl.BlockSpec(memory_space=pltpu.VMEM)
ANY = pl.BlockSpec(memory_space=pl.ANY)


def one_way_pairs(count):
    half = count // 2
    outer = half // 2
    return [(g + half, g) if g < outer else (g, g + half) for g in range(half)]


def cost(flops, size):
    return pl.CostEstimate(flops=flops, bytes_accessed=size, transcendentals=0)


def pick_source_kernel(source_ref, fields_ref, out_ref, sem):
    time = lax.rem(source_ref[0], I32(fields_ref.shape[0]))
    copy = pltpu.make_async_copy(fields_ref.at[time], out_ref, sem)
    copy.start()
    copy.wait()


def pick_source(source, fields):
    return pl.pallas_call(
        pick_source_kernel,
        out_shape=jax.ShapeDtypeStruct(fields.shape[1:], fields.dtype),
        in_specs=[SMEM, ANY],
        out_specs=VMEM,
        scratch_shapes=[pltpu.SemaphoreType.DMA],
        cost_estimate=cost(0, 1_600_000),
        compiler_params=pltpu.CompilerParams(vmem_limit_bytes=56 * 2**20),
        name="pick_source",
    )(source, fields)


def pick_kernel(order_ref, fields_ref, *refs):
    *outs, sems = refs
    copies = [
        pltpu.make_async_copy(fields_ref.at[order_ref[slot + 1]], out, sems.at[slot])
        for slot, out in enumerate(outs)
    ]
    for copy in copies:
        copy.start()
    for copy in copies:
        copy.wait()


def pick_others(order, fields):
    others = fields.shape[0] - 1
    return pl.pallas_call(
        pick_kernel,
        out_shape=[jax.ShapeDtypeStruct(fields.shape[1:], fields.dtype)] * others,
        in_specs=[SMEM, ANY],
        out_specs=[VMEM] * others,
        scratch_shapes=[pltpu.SemaphoreType.DMA((others,))],
        cost_estimate=cost(0, others * 1_600_000),
        compiler_params=pltpu.CompilerParams(vmem_limit_bytes=24 * 2**20),
        name="pick_others",
    )(order, fields)


def plan_kernel(core_ref, own_ref, other_ref, deltas_ref, order_ref, sinks_ref, full_ref):
    times = order_ref.shape[0]
    deltas = deltas_ref.shape[0]
    sinks = []
    for s, ref in enumerate((own_ref, other_ref)):
        for k in range(deltas):
            sink = lax.rem(ref[0] + deltas_ref[k], I32(2 * times))
            sinks_ref[s * deltas + k] = sink
            sinks.append(sink)
    base = core_ref[0] * times
    first = own_ref[0] - base
    keys = []
    for t in range(times):
        needed = sinks[0] == base + t
        for sink in sinks[1:]:
            needed = needed | (sink == base + t)
        key = jnp.where(needed, I32(t), I32(times + t))
        keys.append(jnp.where(first == t, I32(-1), key))
    for t in range(times):
        rank = I32(0)
        for other in range(times):
            if other != t:
                rank += (keys[other] < keys[t]).astype(I32)
        order_ref[rank] = I32(t)
    full = I32(0)
    for c in range(2):
        count = I32(0)
        for t in range(times):
            needed = (own_ref[0] == c * times + t) | (other_ref[0] == c * times + t)
            for sink in sinks:
                needed = needed | (sink == c * times + t)
            count += needed.astype(I32)
        full += jnp.where(count == times, I32(1 << c), I32(0))
    full_ref[0] = full


def plan(core, own, other, deltas, times):
    return pl.pallas_call(
        plan_kernel,
        out_shape=[
            jax.ShapeDtypeStruct((times,), I32),
            jax.ShapeDtypeStruct((2 * deltas.shape[0],), I32),
            jax.ShapeDtypeStruct((1,), I32),
        ],
        in_specs=[SMEM] * 4,
        out_specs=[SMEM] * 3,
        cost_estimate=cost(0, 1000),
        name="plan",
    )(core, own, other, deltas)


def weights_kernel(
    order_ref, far_ref, own_ref, far_cols, own_cols, m_cols, b_cols, a_ref, d_ref, b_ref, u_ref, la, ld, bs, yn
):
    slot = pl.program_id(0)
    rows, per_row, size = a_ref.shape[1], a_ref.shape[2], a_ref.shape[3]
    times = order_ref.shape[0]
    step = rows * per_row
    base = order_ref[slot] * step
    a_base = lax.rem(far_ref[0], I32(times)) * step
    d_base = lax.rem(own_ref[0], I32(times)) * step
    lo, hi = pl.ds(0, size), pl.ds(size, size)

    @pl.when(slot == 0)
    def _():
        for r in range(rows):
            for j in range(per_row):
                real, imag = a_ref[0, r, j], a_ref[1, r, j]
                la[r, j, lo, lo] = real
                la[r, j, lo, hi] = -imag
                la[r, j, hi, lo] = imag
                la[r, j, hi, hi] = real
                real, imag = d_ref[0, r, j].T, d_ref[1, r, j].T
                ld[r, j, lo, lo] = real
                ld[r, j, lo, hi] = -imag
                ld[r, j, hi, lo] = imag
                ld[r, j, hi, hi] = real

    for r in range(rows):
        for j in range(per_row):
            bs[r, lo, pl.ds(j * size, size)] = b_ref[0, 0, r, j]
            bs[r, hi, pl.ds(j * size, size)] = b_ref[0, 1, r, j]

    yn[...] = jnp.zeros_like(yn)
    for r in range(rows):
        inners = [far_cols[a_base + r * per_row + j] for j in range(per_row)]
        parts = [
            jnp.dot(la[r, j], bs[inners[j]], preferred_element_type=F32) for j in range(per_row)
        ]
        pieces = []
        for j in range(per_row):
            for k in range(per_row):
                col = b_cols[base + inners[j] * per_row + k]
                pieces.append((j, col, parts[j][:, k * size : (k + 1) * size]))
        for at in reversed(range(len(pieces))):
            j, col, value = pieces[at]
            for other_j, other_col, other in pieces:
                if other_j > j:
                    value = value + jnp.where(other_col == col, 1.0, 0.0) * other
            yn[col, pl.ds(r * size, size), lo] = value[:size].astype(BF16)
            yn[col, pl.ds(r * size, size), hi] = value[size:].astype(BF16)

    trace_real = jnp.zeros((size, size), F32)
    trace_imag = jnp.zeros((size, size), F32)
    for r in range(rows):
        trace_real += yn[r, pl.ds(r * size, size), lo].astype(F32)
        trace_imag += yn[r, pl.ds(r * size, size), hi].astype(F32)
    diagonal = lax.broadcasted_iota(I32, (size, size), 0) == lax.broadcasted_iota(I32, (size, size), 1)
    trace_real = jnp.sum(jnp.where(diagonal, trace_real, 0.0))
    trace_imag = jnp.sum(jnp.where(diagonal, trace_imag, 0.0))

    for r in range(rows):
        for j in range(per_row):
            col = m_cols[base + r * per_row + j]
            pick = I32(0)
            keep = F32(0)
            for k in range(per_row):
                hit = own_cols[d_base + col * per_row + k] == r
                pick = jnp.where(hit, I32(k), pick)
                keep = jnp.where(hit, F32(1), keep)
            real = ld[col, pick, lo, lo].astype(F32)
            imag = ld[col, pick, hi, lo].astype(F32)
            weight_real, weight_imag = trace_real * keep, trace_imag * keep
            u_ref[0, r, j, 0] = weight_real * real - weight_imag * imag
            u_ref[0, r, j, 1] = weight_real * imag + weight_imag * real

    for i in range(rows):
        for j in range(per_row):
            r = own_cols[d_base + i * per_row + j]
            met = [m_cols[base + r * per_row + k] for k in range(per_row)]
            right = jnp.concatenate(
                [yn[i, pl.ds(pl.multiple_of(col * size, size), size)] for col in met], axis=0
            )
            part = lax.dot_general(
                ld[i, j], right, (((1,), (1,)), ((), ())), preferred_element_type=F32
            )
            for k in range(per_row):
                u_ref[0, r, k, 0] -= part[:size, k * size : (k + 1) * size]
                u_ref[0, r, k, 1] -= part[size:, k * size : (k + 1) * size]


def weights(flops, order, far_time, own_time, far_cols, own_cols, m_cols, b_cols, a, d, fields):
    times = fields.shape[0]
    _, rows, per_row, size, _ = a.shape
    whole = lambda slot, *_: (0, 0, 0, 0, 0)
    return pl.pallas_call(
        weights_kernel,
        out_shape=jax.ShapeDtypeStruct((times, rows, per_row, 2, size, size), F32),
        grid_spec=pltpu.PrefetchScalarGridSpec(
            num_scalar_prefetch=7,
            grid=(times,),
            in_specs=[
                pl.BlockSpec(a.shape, whole),
                pl.BlockSpec(a.shape, whole),
                pl.BlockSpec((1,) + a.shape, lambda slot, order, *_: (order[slot], 0, 0, 0, 0, 0)),
            ],
            out_specs=pl.BlockSpec(
                (1, rows, per_row, 2, size, size), lambda slot, *_: (slot, 0, 0, 0, 0, 0)
            ),
            scratch_shapes=[
                pltpu.VMEM((rows, per_row, 2 * size, 2 * size), BF16),
                pltpu.VMEM((rows, per_row, 2 * size, 2 * size), BF16),
                pltpu.VMEM((rows, 2 * size, per_row * size), BF16),
                pltpu.VMEM((rows, rows * size, 2 * size), BF16),
            ],
        ),
        compiler_params=pltpu.CompilerParams(vmem_limit_bytes=24 * 2**20),
        cost_estimate=cost(flops, times * 1_000_000),
        name="weights",
    )(order, far_time, own_time, far_cols, own_cols, m_cols, b_cols, a, d, fields)


def products(field_ref, u_refs, slot):
    _, rows, per_row, size, _ = field_ref.shape
    chunk = min(size, 32)
    fold = lambda x: jnp.sum(x.reshape(chunk // 8, 8, size), axis=0)
    sums = [jnp.zeros((8, size), F32) for _ in range(2 * len(u_refs))]
    for r in range(rows):
        for j in range(per_row):
            for start in range(0, size, chunk):
                at = pl.ds(start, chunk)
                real = field_ref[0, r, j, at].astype(F32)
                imag = field_ref[1, r, j, at].astype(F32)
                for s, u_ref in enumerate(u_refs):
                    u_real, u_imag = u_ref[slot, r, j, 0, at], u_ref[slot, r, j, 1, at]
                    sums[2 * s] += fold(real * u_real - imag * u_imag)
                    sums[2 * s + 1] += fold(real * u_imag + imag * u_real)
    return sums


def inner_kernel(slot, field_ref, u0_ref, u1_ref, out_ref):
    for at, value in enumerate(products(field_ref, (u0_ref, u1_ref), slot)):
        out_ref[at] = value


def inner(slot, field, u0, u1):
    return pl.pallas_call(
        lambda *refs: inner_kernel(slot, *refs),
        out_shape=jax.ShapeDtypeStruct((4, 8, field.shape[-1]), F32),
        in_specs=[VMEM] * 3,
        out_specs=VMEM,
        cost_estimate=cost(4_000_000, 4_000_000),
        compiler_params=pltpu.CompilerParams(vmem_limit_bytes=24 * 2**20),
        name="inner",
    )(field, u0, u1)


def last_kernel(core_ref, order_ref, sinks_ref, *refs):
    *others, field_ref, u0_ref, u1_ref, mine_ref, theirs_ref = refs
    slots = order_ref.shape[0]
    deltas = sinks_ref.shape[0] // 2
    share = deltas // 2
    core = core_ref[0]
    sums = [[ref[at] for at in range(4)] for ref in others]
    sums.insert(slots - 2, products(field_ref, (u0_ref, u1_ref), slots - 2))
    for out_ref, owner in ((mine_ref, core), (theirs_ref, 1 - core)):
        lines = [jnp.zeros(sums[0][0].shape, F32) for _ in range(2 * share)]
        for slot in range(slots):
            time = core * slots + order_ref[slot]
            for s in range(2):
                for k in range(share):
                    sink = sinks_ref[s * deltas + owner * share + k]
                    keep = jnp.where(sink == time, F32(1), F32(0))
                    for part in range(2):
                        lines[part * share + k] += keep * sums[slot][2 * s + part]
        table = jnp.concatenate([jnp.sum(line, axis=0, keepdims=True) for line in lines], axis=0)
        table = jnp.sum(table, axis=1, keepdims=True)
        for part in range(2):
            out_ref[part] = table[part * share : (part + 1) * share]


def last(core, order, sinks, others, field, u0, u1):
    share = sinks.shape[0] // 4
    return pl.pallas_call(
        last_kernel,
        out_shape=[jax.ShapeDtypeStruct((2, share, 1), F32)] * 2,
        in_specs=[SMEM] * 3 + [VMEM] * (len(others) + 3),
        out_specs=[VMEM] * 2,
        cost_estimate=cost(4_000_000, 4_000_000),
        compiler_params=pltpu.CompilerParams(vmem_limit_bytes=24 * 2**20),
        name="last",
    )(core, order, sinks, *others, field, u0, u1)


def local(fields, block_cols, sources, deltas, partner):
    assert fields.shape[0] == 1 and lax.axis_size("src") == 2
    del partner
    fields = fields[0]
    times = fields.shape[0]
    core = lax.axis_index("src").reshape(1)
    pairs = one_way_pairs(lax.axis_size("mom"))
    swap = lambda value: lax.ppermute(value, "src", [(0, 1), (1, 0)])
    to_partner = lambda value: lax.ppermute(value, "mom", pairs)

    cols = block_cols.reshape(-1)
    far_cols = to_partner(cols)
    own_field = pick_source(sources, fields)
    far = [to_partner(own_field)]

    other_time = swap(sources)
    order, sinks, full = plan(core, sources, other_time, deltas, times)
    *early, late = pick_others(order, fields)
    for field in early:
        if len(far) > 1:
            field, far[-2] = lax.optimization_barrier((field, far[-2]))
        far.append(to_partner(field))

    other_cols = swap(cols)
    far_other_cols = swap(far_cols)
    other_field = swap(own_field)
    far_other = swap(far[0])
    u0 = weights(80_000_000_000, order, sources, sources, far_cols, cols, far_cols, cols, far[0], own_field, fields)
    u1 = weights(
        2_000_000_000,
        order,
        other_time,
        other_time,
        far_other_cols,
        other_cols,
        far_cols,
        cols,
        far_other,
        other_field,
        fields,
    )
    sums = [inner(slot, far[slot], u0, u1) for slot in range(times - 2)]

    both = ("mom", "src")

    def last_slot(cores):
        routes = [(2 * a + c, 2 * b + c) for a, b in pairs for c in cores]
        return lambda field, u0, u1: inner(times - 1, lax.ppermute(field, both, routes), u0, u1)

    no_slot = lambda field, u0, u1: jnp.zeros(sums[0].shape, F32)
    branches = [no_slot, last_slot([0]), last_slot([1]), last_slot([0, 1])]
    late, *sums = lax.optimization_barrier((late, *sums))
    sums.append(lax.switch(full[0], branches, late, u0, u1))
    mine, theirs = last(core, order, sinks, sums, far[-1], u0, u1)

    straight = [(2 * a + c, 2 * b + c) for b, a in pairs for c in range(2)]
    crossed = [(2 * a + c, 2 * b + 1 - c) for b, a in pairs for c in range(2)]
    return mine + swap(theirs) + lax.ppermute(mine, both, straight) + lax.ppermute(theirs, both, crossed)


def solution(mesh):
    in_specs = (
        P(("ens", "mom"), "src", None, None, None, None, None),
        P(("ens", "mom"), "src", None, None),
        P("src"),
        P(),
        P("mom"),
    )
    out_specs = P(None, "src", ("ens", "mom"))
    return jax.shard_map(local, mesh=mesh, in_specs=in_specs, out_specs=out_specs, check_vma=False)
```

```python
import jax
import jax.numpy as jnp
from jax import lax
from jax.experimental import pallas as pl
from jax.experimental.pallas import tpu as pltpu
from jax.sharding import PartitionSpec as P

F32 = jnp.float32
BF16 = jnp.bfloat16
I32 = jnp.int32
SMEM = pl.BlockSpec(memory_space=pltpu.SMEM)
VMEM = pl.BlockSpec(memory_space=pltpu.VMEM)
ANY = pl.BlockSpec(memory_space=pl.ANY)


def one_way_pairs(count):
    half = count // 2
    outer = half // 2
    return [(g + half, g) if g < outer else (g, g + half) for g in range(half)]


def cost(flops, size):
    return pl.CostEstimate(flops=flops, bytes_accessed=size, transcendentals=0)


def pick_source_kernel(source_ref, fields_ref, out_ref, sems):
    time = lax.rem(source_ref[0], I32(fields_ref.shape[0]))
    copies = [
        pltpu.make_async_copy(fields_ref.at[time, part, r], out_ref.at[part, r], sems.at[part, r])
        for part in range(fields_ref.shape[1])
        for r in range(fields_ref.shape[2])
    ]
    for copy in copies:
        copy.start()
    for copy in copies:
        copy.wait()


def pick_source(source, fields):
    return pl.pallas_call(
        pick_source_kernel,
        out_shape=jax.ShapeDtypeStruct(fields.shape[1:], fields.dtype),
        in_specs=[SMEM, ANY],
        out_specs=VMEM,
        scratch_shapes=[pltpu.SemaphoreType.DMA(fields.shape[1:3])],
        cost_estimate=cost(0, 1_600_000),
        compiler_params=pltpu.CompilerParams(vmem_limit_bytes=52 * 2**20),
        name="pick_source",
    )(source, fields)


def pick_kernel(order_ref, fields_ref, *refs):
    *outs, sems = refs
    copies = [
        pltpu.make_async_copy(fields_ref.at[order_ref[slot + 1]], out, sems.at[slot])
        for slot, out in enumerate(outs)
    ]
    for copy in copies:
        copy.start()
    for copy in copies:
        copy.wait()


def pick_others(order, fields):
    others = fields.shape[0] - 1
    return pl.pallas_call(
        pick_kernel,
        out_shape=[jax.ShapeDtypeStruct(fields.shape[1:], fields.dtype)] * others,
        in_specs=[SMEM, ANY],
        out_specs=[VMEM] * others,
        scratch_shapes=[pltpu.SemaphoreType.DMA((others,))],
        cost_estimate=cost(0, others * 1_600_000),
        compiler_params=pltpu.CompilerParams(vmem_limit_bytes=24 * 2**20),
        name="pick_others",
    )(order, fields)


def plan_kernel(core_ref, own_ref, other_ref, deltas_ref, order_ref, sinks_ref, full_ref):
    times = order_ref.shape[0]
    deltas = deltas_ref.shape[0]
    sinks = []
    for s, ref in enumerate((own_ref, other_ref)):
        for k in range(deltas):
            sink = lax.rem(ref[0] + deltas_ref[k], I32(2 * times))
            sinks_ref[s * deltas + k] = sink
            sinks.append(sink)
    base = core_ref[0] * times
    first = own_ref[0] - base
    keys = []
    for t in range(times):
        needed = sinks[0] == base + t
        for sink in sinks[1:]:
            needed = needed | (sink == base + t)
        key = jnp.where(needed, I32(t), I32(times + t))
        keys.append(jnp.where(first == t, I32(-1), key))
    for t in range(times):
        rank = I32(0)
        for other in range(times):
            if other != t:
                rank += (keys[other] < keys[t]).astype(I32)
        order_ref[rank] = I32(t)
    full = I32(0)
    for c in range(2):
        count = I32(0)
        for t in range(times):
            needed = (own_ref[0] == c * times + t) | (other_ref[0] == c * times + t)
            for sink in sinks:
                needed = needed | (sink == c * times + t)
            count += needed.astype(I32)
        full += jnp.where(count == times, I32(1 << c), I32(0))
    full_ref[0] = full


def plan(core, own, other, deltas, times):
    return pl.pallas_call(
        plan_kernel,
        out_shape=[
            jax.ShapeDtypeStruct((times,), I32),
            jax.ShapeDtypeStruct((2 * deltas.shape[0],), I32),
            jax.ShapeDtypeStruct((1,), I32),
        ],
        in_specs=[SMEM] * 4,
        out_specs=[SMEM] * 3,
        cost_estimate=cost(0, 1000),
        name="plan",
    )(core, own, other, deltas)


def weights_kernel(
    order_ref, far_ref, own_ref, far_cols, own_cols, m_cols, b_cols, a_ref, d_ref, b_ref, u_ref, la, ld, bs, yn
):
    slot = pl.program_id(0)
    rows, per_row, size = a_ref.shape[1], a_ref.shape[2], a_ref.shape[3]
    times = order_ref.shape[0]
    step = rows * per_row
    base = order_ref[slot] * step
    a_base = lax.rem(far_ref[0], I32(times)) * step
    d_base = lax.rem(own_ref[0], I32(times)) * step
    lo, hi = pl.ds(0, size), pl.ds(size, size)

    @pl.when(slot == 0)
    def _():
        for r in range(rows):
            for j in range(per_row):
                real, imag = a_ref[0, r, j], a_ref[1, r, j]
                la[r, j, lo, lo] = real
                la[r, j, lo, hi] = -imag
                la[r, j, hi, lo] = imag
                la[r, j, hi, hi] = real
                real, imag = d_ref[0, r, j].T, d_ref[1, r, j].T
                ld[r, j, lo, lo] = real
                ld[r, j, lo, hi] = -imag
                ld[r, j, hi, lo] = imag
                ld[r, j, hi, hi] = real

    for r in range(rows):
        for j in range(per_row):
            bs[r, lo, pl.ds(j * size, size)] = b_ref[0, 0, r, j]
            bs[r, hi, pl.ds(j * size, size)] = b_ref[0, 1, r, j]

    yn[...] = jnp.zeros_like(yn)
    for r in range(rows):
        inners = [far_cols[a_base + r * per_row + j] for j in range(per_row)]
        parts = [
            jnp.dot(la[r, j], bs[inners[j]], preferred_element_type=F32) for j in range(per_row)
        ]
        pieces = []
        for j in range(per_row):
            for k in range(per_row):
                col = b_cols[base + inners[j] * per_row + k]
                pieces.append((j, col, parts[j][:, k * size : (k + 1) * size]))
        for at in reversed(range(len(pieces))):
            j, col, value = pieces[at]
            for other_j, other_col, other in pieces:
                if other_j > j:
                    value = value + jnp.where(other_col == col, 1.0, 0.0) * other
            yn[col, pl.ds(r * size, size), lo] = value[:size].astype(BF16)
            yn[col, pl.ds(r * size, size), hi] = value[size:].astype(BF16)

    trace_real = jnp.zeros((size, size), F32)
    trace_imag = jnp.zeros((size, size), F32)
    for r in range(rows):
        trace_real += yn[r, pl.ds(r * size, size), lo].astype(F32)
        trace_imag += yn[r, pl.ds(r * size, size), hi].astype(F32)
    diagonal = lax.broadcasted_iota(I32, (size, size), 0) == lax.broadcasted_iota(I32, (size, size), 1)
    trace_real = jnp.sum(jnp.where(diagonal, trace_real, 0.0))
    trace_imag = jnp.sum(jnp.where(diagonal, trace_imag, 0.0))

    for r in range(rows):
        for j in range(per_row):
            col = m_cols[base + r * per_row + j]
            pick = I32(0)
            keep = F32(0)
            for k in range(per_row):
                hit = own_cols[d_base + col * per_row + k] == r
                pick = jnp.where(hit, I32(k), pick)
                keep = jnp.where(hit, F32(1), keep)
            real = ld[col, pick, lo, lo].astype(F32)
            imag = ld[col, pick, hi, lo].astype(F32)
            weight_real, weight_imag = trace_real * keep, trace_imag * keep
            u_ref[0, r, j, 0] = weight_real * real - weight_imag * imag
            u_ref[0, r, j, 1] = weight_real * imag + weight_imag * real

    for i in range(rows):
        for j in range(per_row):
            r = own_cols[d_base + i * per_row + j]
            met = [m_cols[base + r * per_row + k] for k in range(per_row)]
            right = jnp.concatenate(
                [yn[i, pl.ds(pl.multiple_of(col * size, size), size)] for col in met], axis=0
            )
            part = lax.dot_general(
                ld[i, j], right, (((1,), (1,)), ((), ())), preferred_element_type=F32
            )
            for k in range(per_row):
                u_ref[0, r, k, 0] -= part[:size, k * size : (k + 1) * size]
                u_ref[0, r, k, 1] -= part[size:, k * size : (k + 1) * size]


def weights(flops, order, far_time, own_time, far_cols, own_cols, m_cols, b_cols, a, d, fields):
    times = fields.shape[0]
    _, rows, per_row, size, _ = a.shape
    whole = lambda slot, *_: (0, 0, 0, 0, 0)
    return pl.pallas_call(
        weights_kernel,
        out_shape=jax.ShapeDtypeStruct((times, rows, per_row, 2, size, size), F32),
        grid_spec=pltpu.PrefetchScalarGridSpec(
            num_scalar_prefetch=7,
            grid=(times,),
            in_specs=[
                pl.BlockSpec(a.shape, whole),
                pl.BlockSpec(a.shape, whole),
                pl.BlockSpec((1,) + a.shape, lambda slot, order, *_: (order[slot], 0, 0, 0, 0, 0)),
            ],
            out_specs=pl.BlockSpec(
                (1, rows, per_row, 2, size, size), lambda slot, *_: (slot, 0, 0, 0, 0, 0)
            ),
            scratch_shapes=[
                pltpu.VMEM((rows, per_row, 2 * size, 2 * size), BF16),
                pltpu.VMEM((rows, per_row, 2 * size, 2 * size), BF16),
                pltpu.VMEM((rows, 2 * size, per_row * size), BF16),
                pltpu.VMEM((rows, rows * size, 2 * size), BF16),
            ],
        ),
        compiler_params=pltpu.CompilerParams(vmem_limit_bytes=24 * 2**20),
        cost_estimate=cost(flops, times * 1_000_000),
        name="weights",
    )(order, far_time, own_time, far_cols, own_cols, m_cols, b_cols, a, d, fields)


def products(field_ref, u_refs, slot):
    _, rows, per_row, size, _ = field_ref.shape
    chunk = min(size, 32)
    fold = lambda x: jnp.sum(x.reshape(chunk // 8, 8, size), axis=0)
    sums = [jnp.zeros((8, size), F32) for _ in range(2 * len(u_refs))]
    for r in range(rows):
        for j in range(per_row):
            for start in range(0, size, chunk):
                at = pl.ds(start, chunk)
                real = field_ref[0, r, j, at].astype(F32)
                imag = field_ref[1, r, j, at].astype(F32)
                for s, u_ref in enumerate(u_refs):
                    u_real, u_imag = u_ref[slot, r, j, 0, at], u_ref[slot, r, j, 1, at]
                    sums[2 * s] += fold(real * u_real - imag * u_imag)
                    sums[2 * s + 1] += fold(real * u_imag + imag * u_real)
    return sums


def inner_kernel(slot, field_ref, u0_ref, u1_ref, out_ref):
    for at, value in enumerate(products(field_ref, (u0_ref, u1_ref), slot)):
        out_ref[at] = value


def inner(slot, field, u0, u1):
    return pl.pallas_call(
        lambda *refs: inner_kernel(slot, *refs),
        out_shape=jax.ShapeDtypeStruct((4, 8, field.shape[-1]), F32),
        in_specs=[VMEM] * 3,
        out_specs=VMEM,
        cost_estimate=cost(4_000_000, 4_000_000),
        compiler_params=pltpu.CompilerParams(vmem_limit_bytes=24 * 2**20),
        name="inner",
    )(field, u0, u1)


def last_kernel(core_ref, order_ref, sinks_ref, full_ref, *refs):
    *earlier, field_ref, late_ref, u0_ref, u1_ref, mine_ref, theirs_ref, late_sums = refs
    slots = order_ref.shape[0]
    deltas = sinks_ref.shape[0] // 2
    share = deltas // 2
    core = core_ref[0]
    late_sums[...] = jnp.zeros_like(late_sums)

    @pl.when((full_ref[0] >> core) % 2 == 1)
    def _():
        for at, value in enumerate(products(late_ref, (u0_ref, u1_ref), slots - 1)):
            late_sums[at] = value

    sums = [[ref[at] for at in range(4)] for ref in earlier]
    sums.append(products(field_ref, (u0_ref, u1_ref), slots - 2))
    sums.append([late_sums[at] for at in range(4)])
    for out_ref, owner in ((mine_ref, core), (theirs_ref, 1 - core)):
        lines = [jnp.zeros(sums[0][0].shape, F32) for _ in range(2 * share)]
        for slot in range(slots):
            time = core * slots + order_ref[slot]
            for s in range(2):
                for k in range(share):
                    sink = sinks_ref[s * deltas + owner * share + k]
                    keep = jnp.where(sink == time, F32(1), F32(0))
                    for part in range(2):
                        lines[part * share + k] += keep * sums[slot][2 * s + part]
        table = jnp.concatenate([jnp.sum(line, axis=0, keepdims=True) for line in lines], axis=0)
        table = jnp.sum(table, axis=1, keepdims=True)
        for part in range(2):
            out_ref[part] = table[part * share : (part + 1) * share]


def last(core, order, sinks, full, earlier, field, late, u0, u1):
    share = sinks.shape[0] // 4
    return pl.pallas_call(
        last_kernel,
        out_shape=[jax.ShapeDtypeStruct((2, share, 1), F32)] * 2,
        in_specs=[SMEM] * 4 + [VMEM] * (len(earlier) + 4),
        out_specs=[VMEM] * 2,
        scratch_shapes=[pltpu.VMEM((4, 8, field.shape[-1]), F32)],
        cost_estimate=cost(4_000_000, 4_000_000),
        compiler_params=pltpu.CompilerParams(vmem_limit_bytes=24 * 2**20),
        name="last",
    )(core, order, sinks, full, *earlier, field, late, u0, u1)


def local(fields, block_cols, sources, deltas, partner):
    assert fields.shape[0] == 1 and lax.axis_size("src") == 2
    del partner
    fields = fields[0]
    times = fields.shape[0]
    core = lax.axis_index("src").reshape(1)
    pairs = one_way_pairs(lax.axis_size("mom"))
    swap = lambda value: lax.ppermute(value, "src", [(0, 1), (1, 0)])
    to_partner = lambda value: lax.ppermute(value, "mom", pairs)

    cols = block_cols.reshape(-1)
    far_cols = to_partner(cols)
    own_field = pick_source(sources, fields)
    far = [to_partner(own_field)]

    other_time = swap(sources)
    order, sinks, full = plan(core, sources, other_time, deltas, times)
    *early, late = pick_others(order, fields)
    for field in early:
        if len(far) > 1:
            field, far[-2] = lax.optimization_barrier((field, far[-2]))
        far.append(to_partner(field))

    other_cols = swap(cols)
    far_other_cols = swap(far_cols)
    other_field = swap(own_field)
    far_other = swap(far[0])
    u0 = weights(80_000_000_000, order, sources, sources, far_cols, cols, far_cols, cols, far[0], own_field, fields)
    u1 = weights(
        2_000_000_000,
        order,
        other_time,
        other_time,
        far_other_cols,
        other_cols,
        far_cols,
        cols,
        far_other,
        other_field,
        fields,
    )
    sums = [inner(slot, far[slot], u0, u1) for slot in range(times - 2)]

    both = ("mom", "src")

    def travel(cores):
        routes = [(2 * a + c, 2 * b + c) for a, b in pairs for c in cores]
        return lambda field: lax.ppermute(field, both, routes)

    late, *sums = lax.optimization_barrier((late, *sums))
    late = lax.switch(full[0], [jnp.zeros_like, travel([0]), travel([1]), travel([0, 1])], late)
    mine, theirs = last(core, order, sinks, full, sums, far[-1], late, u0, u1)

    straight = [(2 * a + c, 2 * b + c) for b, a in pairs for c in range(2)]
    crossed = [(2 * a + c, 2 * b + 1 - c) for b, a in pairs for c in range(2)]
    return mine + swap(theirs) + lax.ppermute(mine, both, straight) + lax.ppermute(theirs, both, crossed)


def solution(mesh):
    in_specs = (
        P(("ens", "mom"), "src", None, None, None, None, None),
        P(("ens", "mom"), "src", None, None),
        P("src"),
        P(),
        P("mom"),
    )
    out_specs = P(None, "src", ("ens", "mom"))
    return jax.shard_map(local, mesh=mesh, in_specs=in_specs, out_specs=out_specs, check_vma=False)
```

```python
import jax
import jax.numpy as jnp
from jax import lax
from jax.experimental import pallas as pl
from jax.experimental.pallas import tpu as pltpu
from jax.sharding import PartitionSpec as P

F32 = jnp.float32
BF16 = jnp.bfloat16
I32 = jnp.int32
SMEM = pl.BlockSpec(memory_space=pltpu.SMEM)
VMEM = pl.BlockSpec(memory_space=pltpu.VMEM)
ANY = pl.BlockSpec(memory_space=pl.ANY)


def one_way_pairs(count):
    half = count // 2
    outer = half // 2
    return [(g + half, g) if g < outer else (g, g + half) for g in range(half)]


def cost(flops, size):
    return pl.CostEstimate(flops=flops, bytes_accessed=size, transcendentals=0)


def pick_source_kernel(source_ref, fields_ref, out_ref, sems):
    time = lax.rem(source_ref[0], I32(fields_ref.shape[0]))
    copies = [
        pltpu.make_async_copy(fields_ref.at[time, part, r], out_ref.at[part, r], sems.at[part, r])
        for part in range(fields_ref.shape[1])
        for r in range(fields_ref.shape[2])
    ]
    for copy in copies:
        copy.start()
    for copy in copies:
        copy.wait()


def pick_source(source, fields):
    return pl.pallas_call(
        pick_source_kernel,
        out_shape=jax.ShapeDtypeStruct(fields.shape[1:], fields.dtype),
        in_specs=[SMEM, ANY],
        out_specs=VMEM,
        scratch_shapes=[pltpu.SemaphoreType.DMA(fields.shape[1:3])],
        cost_estimate=cost(0, 1_600_000),
        compiler_params=pltpu.CompilerParams(vmem_limit_bytes=52 * 2**20),
        name="pick_source",
    )(source, fields)


def pick_kernel(order_ref, fields_ref, *refs):
    *outs, sems = refs
    copies = [
        pltpu.make_async_copy(fields_ref.at[order_ref[slot + 1]], out, sems.at[slot])
        for slot, out in enumerate(outs)
    ]
    for copy in copies:
        copy.start()
    for copy in copies:
        copy.wait()


def pick_others(order, fields):
    others = fields.shape[0] - 1
    return pl.pallas_call(
        pick_kernel,
        out_shape=[jax.ShapeDtypeStruct(fields.shape[1:], fields.dtype)] * others,
        in_specs=[SMEM, ANY],
        out_specs=[VMEM] * others,
        scratch_shapes=[pltpu.SemaphoreType.DMA((others,))],
        cost_estimate=cost(0, others * 1_600_000),
        compiler_params=pltpu.CompilerParams(vmem_limit_bytes=24 * 2**20),
        name="pick_others",
    )(order, fields)


def plan_kernel(core_ref, own_ref, other_ref, deltas_ref, order_ref, sinks_ref, full_ref):
    times = order_ref.shape[0]
    deltas = deltas_ref.shape[0]
    sinks = []
    for s, ref in enumerate((own_ref, other_ref)):
        for k in range(deltas):
            sink = lax.rem(ref[0] + deltas_ref[k], I32(2 * times))
            sinks_ref[s * deltas + k] = sink
            sinks.append(sink)
    base = core_ref[0] * times
    first = own_ref[0] - base
    keys = []
    for t in range(times):
        needed = sinks[0] == base + t
        for sink in sinks[1:]:
            needed = needed | (sink == base + t)
        key = jnp.where(needed, I32(t), I32(times + t))
        keys.append(jnp.where(first == t, I32(-1), key))
    for t in range(times):
        rank = I32(0)
        for other in range(times):
            if other != t:
                rank += (keys[other] < keys[t]).astype(I32)
        order_ref[rank] = I32(t)
    full = I32(0)
    for c in range(2):
        count = I32(0)
        for t in range(times):
            needed = (own_ref[0] == c * times + t) | (other_ref[0] == c * times + t)
            for sink in sinks:
                needed = needed | (sink == c * times + t)
            count += needed.astype(I32)
        full += jnp.where(count == times, I32(1 << c), I32(0))
    full_ref[0] = full


def plan(core, own, other, deltas, times):
    return pl.pallas_call(
        plan_kernel,
        out_shape=[
            jax.ShapeDtypeStruct((times,), I32),
            jax.ShapeDtypeStruct((2 * deltas.shape[0],), I32),
            jax.ShapeDtypeStruct((1,), I32),
        ],
        in_specs=[SMEM] * 4,
        out_specs=[SMEM] * 3,
        cost_estimate=cost(0, 1000),
        name="plan",
    )(core, own, other, deltas)


def weights_kernel(
    order_ref, far_ref, own_ref, far_cols, own_cols, m_cols, b_cols, a_ref, d_ref, b_ref, u_ref, la, ld, bs, yn
):
    slot = pl.program_id(0)
    rows, per_row, size = a_ref.shape[1], a_ref.shape[2], a_ref.shape[3]
    times = order_ref.shape[0]
    step = rows * per_row
    base = order_ref[slot] * step
    a_base = lax.rem(far_ref[0], I32(times)) * step
    d_base = lax.rem(own_ref[0], I32(times)) * step
    lo, hi = pl.ds(0, size), pl.ds(size, size)

    @pl.when(slot == 0)
    def _():
        for r in range(rows):
            for j in range(per_row):
                real, imag = a_ref[0, r, j], a_ref[1, r, j]
                la[r, j, lo, lo] = real
                la[r, j, lo, hi] = -imag
                la[r, j, hi, lo] = imag
                la[r, j, hi, hi] = real
                real, imag = d_ref[0, r, j].T, d_ref[1, r, j].T
                ld[r, j, lo, lo] = real
                ld[r, j, lo, hi] = -imag
                ld[r, j, hi, lo] = imag
                ld[r, j, hi, hi] = real

    for r in range(rows):
        for j in range(per_row):
            bs[r, lo, pl.ds(j * size, size)] = b_ref[0, 0, r, j]
            bs[r, hi, pl.ds(j * size, size)] = b_ref[0, 1, r, j]

    yn[...] = jnp.zeros_like(yn)
    for r in range(rows):
        inners = [far_cols[a_base + r * per_row + j] for j in range(per_row)]
        parts = [
            jnp.dot(la[r, j], bs[inners[j]], preferred_element_type=F32) for j in range(per_row)
        ]
        pieces = []
        for j in range(per_row):
            for k in range(per_row):
                col = b_cols[base + inners[j] * per_row + k]
                pieces.append((j, col, parts[j][:, k * size : (k + 1) * size]))
        for at in reversed(range(len(pieces))):
            j, col, value = pieces[at]
            for other_j, other_col, other in pieces:
                if other_j > j:
                    value = value + jnp.where(other_col == col, 1.0, 0.0) * other
            yn[col, pl.ds(r * size, size), lo] = value[:size].astype(BF16)
            yn[col, pl.ds(r * size, size), hi] = value[size:].astype(BF16)

    trace_real = jnp.zeros((size, size), F32)
    trace_imag = jnp.zeros((size, size), F32)
    for r in range(rows):
        trace_real += yn[r, pl.ds(r * size, size), lo].astype(F32)
        trace_imag += yn[r, pl.ds(r * size, size), hi].astype(F32)
    diagonal = lax.broadcasted_iota(I32, (size, size), 0) == lax.broadcasted_iota(I32, (size, size), 1)
    trace_real = jnp.sum(jnp.where(diagonal, trace_real, 0.0))
    trace_imag = jnp.sum(jnp.where(diagonal, trace_imag, 0.0))

    for r in range(rows):
        for j in range(per_row):
            col = m_cols[base + r * per_row + j]
            pick = I32(0)
            keep = F32(0)
            for k in range(per_row):
                hit = own_cols[d_base + col * per_row + k] == r
                pick = jnp.where(hit, I32(k), pick)
                keep = jnp.where(hit, F32(1), keep)
            real = ld[col, pick, lo, lo].astype(F32)
            imag = ld[col, pick, hi, lo].astype(F32)
            weight_real, weight_imag = trace_real * keep, trace_imag * keep
            u_ref[0, r, j, 0] = weight_real * real - weight_imag * imag
            u_ref[0, r, j, 1] = weight_real * imag + weight_imag * real

    for i in range(rows):
        for j in range(per_row):
            r = own_cols[d_base + i * per_row + j]
            met = [m_cols[base + r * per_row + k] for k in range(per_row)]
            right = jnp.concatenate(
                [yn[i, pl.ds(pl.multiple_of(col * size, size), size)] for col in met], axis=0
            )
            part = lax.dot_general(
                ld[i, j], right, (((1,), (1,)), ((), ())), preferred_element_type=F32
            )
            for k in range(per_row):
                u_ref[0, r, k, 0] -= part[:size, k * size : (k + 1) * size]
                u_ref[0, r, k, 1] -= part[size:, k * size : (k + 1) * size]


def weights(flops, order, far_time, own_time, far_cols, own_cols, m_cols, b_cols, a, d, fields):
    times = fields.shape[0]
    _, rows, per_row, size, _ = a.shape
    whole = lambda slot, *_: (0, 0, 0, 0, 0)
    return pl.pallas_call(
        weights_kernel,
        out_shape=jax.ShapeDtypeStruct((times, rows, per_row, 2, size, size), F32),
        grid_spec=pltpu.PrefetchScalarGridSpec(
            num_scalar_prefetch=7,
            grid=(times,),
            in_specs=[
                pl.BlockSpec(a.shape, whole),
                pl.BlockSpec(a.shape, whole),
                pl.BlockSpec((1,) + a.shape, lambda slot, order, *_: (order[slot], 0, 0, 0, 0, 0)),
            ],
            out_specs=pl.BlockSpec(
                (1, rows, per_row, 2, size, size), lambda slot, *_: (slot, 0, 0, 0, 0, 0)
            ),
            scratch_shapes=[
                pltpu.VMEM((rows, per_row, 2 * size, 2 * size), BF16),
                pltpu.VMEM((rows, per_row, 2 * size, 2 * size), BF16),
                pltpu.VMEM((rows, 2 * size, per_row * size), BF16),
                pltpu.VMEM((rows, rows * size, 2 * size), BF16),
            ],
        ),
        compiler_params=pltpu.CompilerParams(vmem_limit_bytes=24 * 2**20),
        cost_estimate=cost(flops, times * 1_000_000),
        name="weights",
    )(order, far_time, own_time, far_cols, own_cols, m_cols, b_cols, a, d, fields)


def products(field_ref, u_refs, slot):
    _, rows, per_row, size, _ = field_ref.shape
    chunk = min(size, 32)
    fold = lambda x: jnp.sum(x.reshape(chunk // 8, 8, size), axis=0)
    sums = [jnp.zeros((8, size), F32) for _ in range(2 * len(u_refs))]
    for r in range(rows):
        for j in range(per_row):
            for start in range(0, size, chunk):
                at = pl.ds(start, chunk)
                real = field_ref[0, r, j, at].astype(F32)
                imag = field_ref[1, r, j, at].astype(F32)
                for s, u_ref in enumerate(u_refs):
                    u_real, u_imag = u_ref[slot, r, j, 0, at], u_ref[slot, r, j, 1, at]
                    sums[2 * s] += fold(real * u_real - imag * u_imag)
                    sums[2 * s + 1] += fold(real * u_imag + imag * u_real)
    return sums


def inner_kernel(slot, field_ref, u0_ref, u1_ref, out_ref):
    for at, value in enumerate(products(field_ref, (u0_ref, u1_ref), slot)):
        out_ref[at] = value


def inner(slot, field, u0, u1):
    return pl.pallas_call(
        lambda *refs: inner_kernel(slot, *refs),
        out_shape=jax.ShapeDtypeStruct((4, 8, field.shape[-1]), F32),
        in_specs=[VMEM] * 3,
        out_specs=VMEM,
        cost_estimate=cost(4_000_000, 4_000_000),
        compiler_params=pltpu.CompilerParams(vmem_limit_bytes=24 * 2**20),
        name="inner",
    )(field, u0, u1)


def stage_kernel(slot, u0_ref, u1_ref, out0_ref, out1_ref, sems):
    copies = [
        pltpu.make_async_copy(u_ref.at[slot, r], out_ref.at[0, r], sems.at[s, r])
        for s, (u_ref, out_ref) in enumerate(((u0_ref, out0_ref), (u1_ref, out1_ref)))
        for r in range(u_ref.shape[1])
    ]
    for copy in copies:
        copy.start()
    for copy in copies:
        copy.wait()


def stage(slot, u0, u1):
    one = jax.ShapeDtypeStruct((1,) + u0.shape[1:], u0.dtype)
    return pl.pallas_call(
        lambda *refs: stage_kernel(slot, *refs),
        out_shape=[one, one],
        in_specs=[ANY] * 2,
        out_specs=[VMEM] * 2,
        scratch_shapes=[pltpu.SemaphoreType.DMA((2, u0.shape[1]))],
        cost_estimate=cost(0, 6_000_000),
        compiler_params=pltpu.CompilerParams(vmem_limit_bytes=24 * 2**20),
        name="stage",
    )(u0, u1)


def last_kernel(core_ref, order_ref, sinks_ref, *refs):
    *others, field_ref, u0_ref, u1_ref, mine_ref, theirs_ref = refs
    slots = order_ref.shape[0]
    deltas = sinks_ref.shape[0] // 2
    share = deltas // 2
    core = core_ref[0]
    sums = [[ref[at] for at in range(4)] for ref in others]
    sums.insert(slots - 2, products(field_ref, (u0_ref, u1_ref), 0))
    for out_ref, owner in ((mine_ref, core), (theirs_ref, 1 - core)):
        lines = [jnp.zeros(sums[0][0].shape, F32) for _ in range(2 * share)]
        for slot in range(slots):
            time = core * slots + order_ref[slot]
            for s in range(2):
                for k in range(share):
                    sink = sinks_ref[s * deltas + owner * share + k]
                    keep = jnp.where(sink == time, F32(1), F32(0))
                    for part in range(2):
                        lines[part * share + k] += keep * sums[slot][2 * s + part]
        table = jnp.concatenate([jnp.sum(line, axis=0, keepdims=True) for line in lines], axis=0)
        table = jnp.sum(table, axis=1, keepdims=True)
        for part in range(2):
            out_ref[part] = table[part * share : (part + 1) * share]


def last(core, order, sinks, others, field, u0, u1):
    share = sinks.shape[0] // 4
    return pl.pallas_call(
        last_kernel,
        out_shape=[jax.ShapeDtypeStruct((2, share, 1), F32)] * 2,
        in_specs=[SMEM] * 3 + [VMEM] * (len(others) + 3),
        out_specs=[VMEM] * 2,
        cost_estimate=cost(4_000_000, 4_000_000),
        compiler_params=pltpu.CompilerParams(vmem_limit_bytes=24 * 2**20),
        name="last",
    )(core, order, sinks, *others, field, u0, u1)


def local(fields, block_cols, sources, deltas, partner):
    assert fields.shape[0] == 1 and lax.axis_size("src") == 2
    del partner
    fields = fields[0]
    times = fields.shape[0]
    core = lax.axis_index("src").reshape(1)
    pairs = one_way_pairs(lax.axis_size("mom"))
    swap = lambda value: lax.ppermute(value, "src", [(0, 1), (1, 0)])
    to_partner = lambda value: lax.ppermute(value, "mom", pairs)

    cols = block_cols.reshape(-1)
    far_cols = to_partner(cols)
    own_field = pick_source(sources, fields)
    far = [to_partner(own_field)]

    other_time = swap(sources)
    order, sinks, full = plan(core, sources, other_time, deltas, times)
    *early, late = pick_others(order, fields)
    for field in early:
        if len(far) > 1:
            field, far[-2] = lax.optimization_barrier((field, far[-2]))
        far.append(to_partner(field))

    other_cols = swap(cols)
    far_other_cols = swap(far_cols)
    other_field = swap(own_field)
    far_other = swap(far[0])
    u0 = weights(80_000_000_000, order, sources, sources, far_cols, cols, far_cols, cols, far[0], own_field, fields)
    u1 = weights(
        2_000_000_000,
        order,
        other_time,
        other_time,
        far_other_cols,
        other_cols,
        far_cols,
        cols,
        far_other,
        other_field,
        fields,
    )
    sums = [inner(slot, far[slot], u0, u1) for slot in range(times - 2)]

    both = ("mom", "src")

    def with_slot(cores):
        routes = [(2 * a + c, 2 * b + c) for a, b in pairs for c in cores]

        def branch(field, u0, u1):
            field = lax.ppermute(field, both, routes)
            return inner(times - 1, field, u0, u1), *stage(times - 2, u0, u1)

        return branch

    def without_slot(field, u0, u1):
        return jnp.zeros(sums[0].shape, F32), *stage(times - 2, u0, u1)

    branches = [without_slot, with_slot([0]), with_slot([1]), with_slot([0, 1])]
    late, *sums = lax.optimization_barrier((late, *sums))
    late_sums, staged0, staged1 = lax.switch(full[0], branches, late, u0, u1)
    mine, theirs = last(core, order, sinks, [*sums, late_sums], far[-1], staged0, staged1)

    straight = [(2 * a + c, 2 * b + c) for b, a in pairs for c in range(2)]
    crossed = [(2 * a + c, 2 * b + 1 - c) for b, a in pairs for c in range(2)]
    return mine + swap(theirs) + lax.ppermute(mine, both, straight) + lax.ppermute(theirs, both, crossed)


def solution(mesh):
    in_specs = (
        P(("ens", "mom"), "src", None, None, None, None, None),
        P(("ens", "mom"), "src", None, None),
        P("src"),
        P(),
        P("mom"),
    )
    out_specs = P(None, "src", ("ens", "mom"))
    return jax.shard_map(local, mesh=mesh, in_specs=in_specs, out_specs=out_specs, check_vma=False)
```

```python
import jax
import jax.numpy as jnp
from jax import lax
from jax.experimental import pallas as pl
from jax.experimental.pallas import tpu as pltpu
from jax.sharding import PartitionSpec as P

F32 = jnp.float32
BF16 = jnp.bfloat16
I32 = jnp.int32
SMEM = pl.BlockSpec(memory_space=pltpu.SMEM)
VMEM = pl.BlockSpec(memory_space=pltpu.VMEM)
ANY = pl.BlockSpec(memory_space=pl.ANY)


def one_way_pairs(count):
    half = count // 2
    outer = half // 2
    return [(g + half, g) if g < outer else (g, g + half) for g in range(half)]


def cost(flops, size):
    return pl.CostEstimate(flops=flops, bytes_accessed=size, transcendentals=0)


def pick_source_kernel(source_ref, fields_ref, out_ref, sems):
    time = lax.rem(source_ref[0], I32(fields_ref.shape[0]))
    copies = [
        pltpu.make_async_copy(fields_ref.at[time, part, r], out_ref.at[part, r], sems.at[part, r])
        for part in range(fields_ref.shape[1])
        for r in range(fields_ref.shape[2])
    ]
    for copy in copies:
        copy.start()
    for copy in copies:
        copy.wait()


def pick_source(source, fields):
    return pl.pallas_call(
        pick_source_kernel,
        out_shape=jax.ShapeDtypeStruct(fields.shape[1:], fields.dtype),
        in_specs=[SMEM, ANY],
        out_specs=VMEM,
        scratch_shapes=[pltpu.SemaphoreType.DMA(fields.shape[1:3])],
        cost_estimate=cost(0, 1_600_000),
        compiler_params=pltpu.CompilerParams(vmem_limit_bytes=52 * 2**20),
        name="pick_source",
    )(source, fields)


def pick_kernel(order_ref, fields_ref, *refs):
    *outs, sems = refs
    copies = [
        pltpu.make_async_copy(fields_ref.at[order_ref[slot + 1], part], out.at[part], sems.at[slot, part])
        for slot, out in enumerate(outs)
        for part in range(2)
    ]
    for copy in copies:
        copy.start()
    for copy in copies:
        copy.wait()


def pick_others(order, fields):
    others = fields.shape[0] - 1
    return pl.pallas_call(
        pick_kernel,
        out_shape=[jax.ShapeDtypeStruct(fields.shape[1:], fields.dtype)] * others,
        in_specs=[SMEM, ANY],
        out_specs=[VMEM] * others,
        scratch_shapes=[pltpu.SemaphoreType.DMA((others, 2))],
        cost_estimate=cost(0, others * 1_600_000),
        compiler_params=pltpu.CompilerParams(vmem_limit_bytes=58 * 2**20),
        name="pick_others",
    )(order, fields)


def plan_kernel(core_ref, own_ref, other_ref, deltas_ref, order_ref, sinks_ref, active_ref, full_ref):
    times = order_ref.shape[0]
    deltas = deltas_ref.shape[0]
    sinks = []
    for s, ref in enumerate((own_ref, other_ref)):
        for k in range(deltas):
            sink = lax.rem(ref[0] + deltas_ref[k], I32(2 * times))
            sinks_ref[s * deltas + k] = sink
            sinks.append(sink)
    base = core_ref[0] * times
    first = own_ref[0] - base
    keys = []
    for t in range(times):
        needed = sinks[0] == base + t
        for sink in sinks[1:]:
            needed = needed | (sink == base + t)
        key = jnp.where(needed, I32(t), I32(times + t))
        keys.append(jnp.where(first == t, I32(-1), key))
    for t in range(times):
        rank = I32(0)
        for other in range(times):
            if other != t:
                rank += (keys[other] < keys[t]).astype(I32)
        order_ref[rank] = I32(t)
        for s in range(2):
            active = sinks[s * deltas] == base + t
            for k in range(1, deltas):
                active = active | (sinks[s * deltas + k] == base + t)
            active_ref[s * times + rank] = active.astype(I32)
    full = I32(0)
    for c in range(2):
        count = I32(0)
        for t in range(times):
            needed = (own_ref[0] == c * times + t) | (other_ref[0] == c * times + t)
            for sink in sinks:
                needed = needed | (sink == c * times + t)
            count += needed.astype(I32)
        full += jnp.where(count == times, I32(1 << c), I32(0))
    full_ref[0] = full


def plan(core, own, other, deltas, times):
    return pl.pallas_call(
        plan_kernel,
        out_shape=[
            jax.ShapeDtypeStruct((times,), I32),
            jax.ShapeDtypeStruct((2 * deltas.shape[0],), I32),
            jax.ShapeDtypeStruct((2 * times,), I32),
            jax.ShapeDtypeStruct((1,), I32),
        ],
        in_specs=[SMEM] * 4,
        out_specs=[SMEM] * 4,
        cost_estimate=cost(0, 1000),
        name="plan",
    )(core, own, other, deltas)


def weights_kernel(s, order_ref, active_ref, *refs):
    far_ref, own_ref, far_cols, own_cols, m_cols, b_cols, a_ref, d_ref, *refs = refs
    *b_refs, u_ref, la, ld, bs, yn, held, sems = refs
    slot = pl.program_id(0)
    rows, per_row, size = a_ref.shape[1], a_ref.shape[2], a_ref.shape[3]
    times = order_ref.shape[0]
    step = rows * per_row
    base = order_ref[slot] * step
    a_base = lax.rem(far_ref[0], I32(times)) * step
    d_base = lax.rem(own_ref[0], I32(times)) * step
    lo, hi = pl.ds(0, size), pl.ds(size, size)

    b_copies = [
        pltpu.make_async_copy(b_ref, held.at[at % 2], sems.at[at % 2]) for at, b_ref in enumerate(b_refs)
    ]

    @pl.when(slot == 0)
    def _():
        b_copies[0].start()
        for r in range(rows):
            for j in range(per_row):
                real, imag = a_ref[0, r, j], a_ref[1, r, j]
                la[r, j, lo, lo] = real
                la[r, j, lo, hi] = -imag
                la[r, j, hi, lo] = imag
                la[r, j, hi, hi] = real
                real, imag = d_ref[0, r, j].T, d_ref[1, r, j].T
                ld[r, j, lo, lo] = real
                ld[r, j, lo, hi] = -imag
                ld[r, j, hi, lo] = imag
                ld[r, j, hi, hi] = real

    for at in range(times):

        @pl.when(slot == at)
        def _():
            if at + 1 < times:
                b_copies[at + 1].start()
            b_copies[at].wait()

    @pl.when(active_ref[s * times + slot] == 0)
    def _():
        u_ref[...] = jnp.zeros_like(u_ref)

    @pl.when(active_ref[s * times + slot] != 0)
    def _():
        for r in range(rows):
            for j in range(per_row):
                bs[r, lo, pl.ds(j * size, size)] = held[slot % 2, 0, r, j]
                bs[r, hi, pl.ds(j * size, size)] = held[slot % 2, 1, r, j]

        yn[...] = jnp.zeros_like(yn)
        for r in range(rows):
            inners = [far_cols[a_base + r * per_row + j] for j in range(per_row)]
            parts = [
                jnp.dot(la[r, j], bs[inners[j]], preferred_element_type=F32) for j in range(per_row)
            ]
            pieces = []
            for j in range(per_row):
                for k in range(per_row):
                    col = b_cols[base + inners[j] * per_row + k]
                    pieces.append((j, col, parts[j][:, k * size : (k + 1) * size]))
            for at in reversed(range(len(pieces))):
                j, col, value = pieces[at]
                for other_j, other_col, other in pieces:
                    if other_j > j:
                        value = value + jnp.where(other_col == col, 1.0, 0.0) * other
                yn[col, pl.ds(r * size, size), lo] = value[:size].astype(BF16)
                yn[col, pl.ds(r * size, size), hi] = value[size:].astype(BF16)

        trace_real = jnp.zeros((size, size), F32)
        trace_imag = jnp.zeros((size, size), F32)
        for r in range(rows):
            trace_real += yn[r, pl.ds(r * size, size), lo].astype(F32)
            trace_imag += yn[r, pl.ds(r * size, size), hi].astype(F32)
        diagonal = lax.broadcasted_iota(I32, (size, size), 0) == lax.broadcasted_iota(I32, (size, size), 1)
        trace_real = jnp.sum(jnp.where(diagonal, trace_real, 0.0))
        trace_imag = jnp.sum(jnp.where(diagonal, trace_imag, 0.0))

        for r in range(rows):
            for j in range(per_row):
                col = m_cols[base + r * per_row + j]
                pick = I32(0)
                keep = F32(0)
                for k in range(per_row):
                    hit = own_cols[d_base + col * per_row + k] == r
                    pick = jnp.where(hit, I32(k), pick)
                    keep = jnp.where(hit, F32(1), keep)
                real = ld[col, pick, lo, lo].astype(F32)
                imag = ld[col, pick, hi, lo].astype(F32)
                weight_real, weight_imag = trace_real * keep, trace_imag * keep
                u_ref[0, r, j, 0] = weight_real * real - weight_imag * imag
                u_ref[0, r, j, 1] = weight_real * imag + weight_imag * real

        for i in range(rows):
            for j in range(per_row):
                r = own_cols[d_base + i * per_row + j]
                met = [m_cols[base + r * per_row + k] for k in range(per_row)]
                right = jnp.concatenate(
                    [yn[i, pl.ds(pl.multiple_of(col * size, size), size)] for col in met], axis=0
                )
                part = lax.dot_general(
                    ld[i, j], right, (((1,), (1,)), ((), ())), preferred_element_type=F32
                )
                for k in range(per_row):
                    u_ref[0, r, k, 0] -= part[:size, k * size : (k + 1) * size]
                    u_ref[0, r, k, 1] -= part[size:, k * size : (k + 1) * size]


def weights(flops, s, order, active, far_time, own_time, far_cols, own_cols, m_cols, b_cols, a, d, picked):
    times = len(picked)
    _, rows, per_row, size, _ = a.shape
    whole = lambda slot, *_: (0, 0, 0, 0, 0)
    return pl.pallas_call(
        lambda *refs: weights_kernel(s, *refs),
        out_shape=jax.ShapeDtypeStruct((times, rows, per_row, 2, size, size), F32),
        grid_spec=pltpu.PrefetchScalarGridSpec(
            num_scalar_prefetch=8,
            grid=(times,),
            in_specs=[
                pl.BlockSpec(a.shape, whole),
                pl.BlockSpec(a.shape, whole),
                *[ANY] * times,
            ],
            out_specs=pl.BlockSpec(
                (1, rows, per_row, 2, size, size), lambda slot, *_: (slot, 0, 0, 0, 0, 0)
            ),
            scratch_shapes=[
                pltpu.VMEM((rows, per_row, 2 * size, 2 * size), BF16),
                pltpu.VMEM((rows, per_row, 2 * size, 2 * size), BF16),
                pltpu.VMEM((rows, 2 * size, per_row * size), BF16),
                pltpu.VMEM((rows, rows * size, 2 * size), BF16),
                pltpu.VMEM((2,) + a.shape, a.dtype),
                pltpu.SemaphoreType.DMA((2,)),
            ],
        ),
        compiler_params=pltpu.CompilerParams(vmem_limit_bytes=24 * 2**20),
        cost_estimate=cost(flops, times * 1_000_000),
        name="weights",
    )(order, active, far_time, own_time, far_cols, own_cols, m_cols, b_cols, a, d, *picked)


def products(field_ref, u_refs, slot, held, sems):
    _, rows, per_row, size, _ = field_ref.shape
    copies = [
        [
            pltpu.make_async_copy(field_ref.at[part, r], held.at[part, r], sems.at[part, r])
            for part in range(2)
        ]
        for r in range(rows)
    ]
    for row in copies:
        for copy in row:
            copy.start()
    chunk = min(size, 32)
    fold = lambda x: jnp.sum(x.reshape(chunk // 8, 8, size), axis=0)
    sums = [jnp.zeros((8, size), F32) for _ in range(2 * len(u_refs))]
    for r in range(rows):
        for copy in copies[r]:
            copy.wait()
        for j in range(per_row):
            for start in range(0, size, chunk):
                at = pl.ds(start, chunk)
                real = held[0, r, j, at].astype(F32)
                imag = held[1, r, j, at].astype(F32)
                for s, u_ref in enumerate(u_refs):
                    u_real, u_imag = u_ref[slot, r, j, 0, at], u_ref[slot, r, j, 1, at]
                    sums[2 * s] += fold(real * u_real - imag * u_imag)
                    sums[2 * s + 1] += fold(real * u_imag + imag * u_real)
    return sums


def products_scratch(field):
    return [pltpu.VMEM(field.shape, field.dtype), pltpu.SemaphoreType.DMA(field.shape[:2])]


def inner_kernel(slot, field_ref, u0_ref, u1_ref, out_ref, held, sems):
    for at, value in enumerate(products(field_ref, (u0_ref, u1_ref), slot, held, sems)):
        out_ref[at] = value


def inner(slot, field, u0, u1):
    return pl.pallas_call(
        lambda *refs: inner_kernel(slot, *refs),
        out_shape=jax.ShapeDtypeStruct((4, 8, field.shape[-1]), F32),
        in_specs=[ANY, VMEM, VMEM],
        out_specs=VMEM,
        scratch_shapes=products_scratch(field),
        cost_estimate=cost(4_000_000, 4_000_000),
        compiler_params=pltpu.CompilerParams(vmem_limit_bytes=24 * 2**20),
        name="inner",
    )(field, u0, u1)


def stage_kernel(slot, u0_ref, u1_ref, out0_ref, out1_ref, sems):
    copies = [
        pltpu.make_async_copy(u_ref.at[slot, r], out_ref.at[0, r], sems.at[s, r])
        for s, (u_ref, out_ref) in enumerate(((u0_ref, out0_ref), (u1_ref, out1_ref)))
        for r in range(u_ref.shape[1])
    ]
    for copy in copies:
        copy.start()
    for copy in copies:
        copy.wait()


def stage(slot, u0, u1):
    one = jax.ShapeDtypeStruct((1,) + u0.shape[1:], u0.dtype)
    return pl.pallas_call(
        lambda *refs: stage_kernel(slot, *refs),
        out_shape=[one, one],
        in_specs=[ANY] * 2,
        out_specs=[VMEM] * 2,
        scratch_shapes=[pltpu.SemaphoreType.DMA((2, u0.shape[1]))],
        cost_estimate=cost(0, 6_000_000),
        compiler_params=pltpu.CompilerParams(vmem_limit_bytes=24 * 2**20),
        name="stage",
    )(u0, u1)


def last_kernel(core_ref, order_ref, sinks_ref, *refs):
    *others, field_ref, u0_ref, u1_ref, mine_ref, theirs_ref, held, sems = refs
    slots = order_ref.shape[0]
    deltas = sinks_ref.shape[0] // 2
    share = deltas // 2
    core = core_ref[0]
    sums = [[ref[at] for at in range(4)] for ref in others]
    sums.insert(slots - 2, products(field_ref, (u0_ref, u1_ref), 0, held, sems))
    for out_ref, owner in ((mine_ref, core), (theirs_ref, 1 - core)):
        lines = [jnp.zeros(sums[0][0].shape, F32) for _ in range(2 * share)]
        for slot in range(slots):
            time = core * slots + order_ref[slot]
            for s in range(2):
                for k in range(share):
                    sink = sinks_ref[s * deltas + owner * share + k]
                    keep = jnp.where(sink == time, F32(1), F32(0))
                    for part in range(2):
                        lines[part * share + k] += keep * sums[slot][2 * s + part]
        table = jnp.concatenate([jnp.sum(line, axis=0, keepdims=True) for line in lines], axis=0)
        table = jnp.sum(table, axis=1, keepdims=True)
        for part in range(2):
            out_ref[part] = table[part * share : (part + 1) * share]


def last(core, order, sinks, others, field, u0, u1):
    share = sinks.shape[0] // 4
    return pl.pallas_call(
        last_kernel,
        out_shape=[jax.ShapeDtypeStruct((2, share, 1), F32)] * 2,
        in_specs=[SMEM] * 3 + [VMEM] * len(others) + [ANY, VMEM, VMEM],
        out_specs=[VMEM] * 2,
        scratch_shapes=products_scratch(field),
        cost_estimate=cost(4_000_000, 4_000_000),
        compiler_params=pltpu.CompilerParams(vmem_limit_bytes=24 * 2**20),
        name="last",
    )(core, order, sinks, *others, field, u0, u1)


def local(fields, block_cols, sources, deltas, partner):
    assert fields.shape[0] == 1 and lax.axis_size("src") == 2
    del partner
    fields = fields[0]
    times = fields.shape[0]
    core = lax.axis_index("src").reshape(1)
    pairs = one_way_pairs(lax.axis_size("mom"))
    swap = lambda value: lax.ppermute(value, "src", [(0, 1), (1, 0)])
    to_partner = lambda value: lax.ppermute(value, "mom", pairs)

    cols = block_cols.reshape(-1)
    far_cols = to_partner(cols)
    own_field = pick_source(sources, fields)
    far = [to_partner(own_field)]

    other_time = swap(sources)
    order, sinks, active, full = plan(core, sources, other_time, deltas, times)
    others = pick_others(order, fields)
    picked = [own_field, *others]
    *early, late = others
    for field in early:
        if len(far) > 1:
            field, far[-2] = lax.optimization_barrier((field, far[-2]))
        far.append(to_partner(field))

    other_cols = swap(cols)
    far_other_cols = swap(far_cols)
    other_field = swap(own_field)
    far_other = swap(far[0])
    u0 = weights(
        80_000_000_000,
        0,
        order,
        active,
        sources,
        sources,
        far_cols,
        cols,
        far_cols,
        cols,
        far[0],
        own_field,
        picked,
    )
    u1 = weights(
        2_000_000_000,
        1,
        order,
        active,
        other_time,
        other_time,
        far_other_cols,
        other_cols,
        far_cols,
        cols,
        far_other,
        other_field,
        picked,
    )
    sums = [inner(slot, far[slot], u0, u1) for slot in range(times - 2)]

    both = ("mom", "src")

    def with_slot(cores):
        routes = [(2 * a + c, 2 * b + c) for a, b in pairs for c in cores]

        def branch(field, u0, u1):
            field = lax.ppermute(field, both, routes)
            return inner(times - 1, field, u0, u1), *stage(times - 2, u0, u1)

        return branch

    def without_slot(field, u0, u1):
        return jnp.zeros(sums[0].shape, F32), *stage(times - 2, u0, u1)

    branches = [without_slot, with_slot([0]), with_slot([1]), with_slot([0, 1])]
    late, *sums = lax.optimization_barrier((late, *sums))
    late_sums, staged0, staged1 = lax.switch(full[0], branches, late, u0, u1)
    mine, theirs = last(core, order, sinks, [*sums, late_sums], far[-1], staged0, staged1)

    total = mine + swap(theirs)
    back = [(2 * a + c, 2 * b + c) for b, a in pairs for c in range(2)]
    return total + lax.ppermute(total, both, back)


def solution(mesh):
    in_specs = (
        P(("ens", "mom"), "src", None, None, None, None, None),
        P(("ens", "mom"), "src", None, None),
        P("src"),
        P(),
        P("mom"),
    )
    out_specs = P(None, "src", ("ens", "mom"))
    return jax.shard_map(local, mesh=mesh, in_specs=in_specs, out_specs=out_specs, check_vma=False)
```

```python
import jax
import jax.numpy as jnp
from jax import lax
from jax.experimental import pallas as pl
from jax.experimental.pallas import tpu as pltpu
from jax.sharding import PartitionSpec as P

F32 = jnp.float32
BF16 = jnp.bfloat16
I32 = jnp.int32
SMEM = pl.BlockSpec(memory_space=pltpu.SMEM)
VMEM = pl.BlockSpec(memory_space=pltpu.VMEM)
ANY = pl.BlockSpec(memory_space=pl.ANY)


def one_way_pairs(count):
    half = count // 2
    outer = half // 2
    return [(g + half, g) if g < outer else (g, g + half) for g in range(half)]


def cost(flops, size):
    return pl.CostEstimate(flops=flops, bytes_accessed=size, transcendentals=0)


def pick_source_kernel(source_ref, fields_ref, out_ref, sems):
    time = lax.rem(source_ref[0], I32(fields_ref.shape[0]))
    copies = [
        pltpu.make_async_copy(fields_ref.at[time, part, r], out_ref.at[part, r], sems.at[part, r])
        for part in range(fields_ref.shape[1])
        for r in range(fields_ref.shape[2])
    ]
    for copy in copies:
        copy.start()
    for copy in copies:
        copy.wait()


def pick_source(source, fields):
    return pl.pallas_call(
        pick_source_kernel,
        out_shape=jax.ShapeDtypeStruct(fields.shape[1:], fields.dtype),
        in_specs=[SMEM, ANY],
        out_specs=VMEM,
        scratch_shapes=[pltpu.SemaphoreType.DMA(fields.shape[1:3])],
        cost_estimate=cost(0, 1_600_000),
        compiler_params=pltpu.CompilerParams(vmem_limit_bytes=52 * 2**20),
        name="pick_source",
    )(source, fields)


def pick_kernel(order_ref, fields_ref, *refs):
    *outs, sems = refs
    copies = [
        pltpu.make_async_copy(fields_ref.at[order_ref[slot + 1], part], out.at[part], sems.at[slot, part])
        for slot, out in enumerate(outs)
        for part in range(2)
    ]
    for copy in copies:
        copy.start()
    for copy in copies:
        copy.wait()


def pick_others(order, fields):
    others = fields.shape[0] - 1
    return pl.pallas_call(
        pick_kernel,
        out_shape=[jax.ShapeDtypeStruct(fields.shape[1:], fields.dtype)] * others,
        in_specs=[SMEM, ANY],
        out_specs=[VMEM] * others,
        scratch_shapes=[pltpu.SemaphoreType.DMA((others, 2))],
        cost_estimate=cost(0, others * 1_600_000),
        compiler_params=pltpu.CompilerParams(vmem_limit_bytes=58 * 2**20),
        name="pick_others",
    )(order, fields)


def plan_kernel(core_ref, own_ref, other_ref, deltas_ref, order_ref, sinks_ref, active_ref, full_ref):
    times = order_ref.shape[0]
    deltas = deltas_ref.shape[0]
    sinks = []
    for s, ref in enumerate((own_ref, other_ref)):
        for k in range(deltas):
            sink = lax.rem(ref[0] + deltas_ref[k], I32(2 * times))
            sinks_ref[s * deltas + k] = sink
            sinks.append(sink)
    base = core_ref[0] * times
    first = own_ref[0] - base
    keys = []
    for t in range(times):
        needed = sinks[0] == base + t
        for sink in sinks[1:]:
            needed = needed | (sink == base + t)
        key = jnp.where(needed, I32(t), I32(times + t))
        keys.append(jnp.where(first == t, I32(-1), key))
    for t in range(times):
        rank = I32(0)
        for other in range(times):
            if other != t:
                rank += (keys[other] < keys[t]).astype(I32)
        order_ref[rank] = I32(t)
        for s in range(2):
            active = sinks[s * deltas] == base + t
            for k in range(1, deltas):
                active = active | (sinks[s * deltas + k] == base + t)
            active_ref[s * times + rank] = active.astype(I32)
    full = I32(0)
    for c in range(2):
        count = I32(0)
        for t in range(times):
            needed = (own_ref[0] == c * times + t) | (other_ref[0] == c * times + t)
            for sink in sinks:
                needed = needed | (sink == c * times + t)
            count += needed.astype(I32)
        full += jnp.where(count == times, I32(1 << c), I32(0))
    full_ref[0] = full


def plan(core, own, other, deltas, times):
    return pl.pallas_call(
        plan_kernel,
        out_shape=[
            jax.ShapeDtypeStruct((times,), I32),
            jax.ShapeDtypeStruct((2 * deltas.shape[0],), I32),
            jax.ShapeDtypeStruct((2 * times,), I32),
            jax.ShapeDtypeStruct((1,), I32),
        ],
        in_specs=[SMEM] * 4,
        out_specs=[SMEM] * 4,
        cost_estimate=cost(0, 1000),
        name="plan",
    )(core, own, other, deltas)


def weights_kernel(s, order_ref, active_ref, *refs):
    far_ref, own_ref, far_cols, own_cols, m_cols, b_cols, a_ref, d_ref, *refs = refs
    *b_refs, u_ref, la, ld, bs, yn, held, sems = refs
    slot = pl.program_id(0)
    rows, per_row, size = a_ref.shape[1], a_ref.shape[2], a_ref.shape[3]
    times = order_ref.shape[0]
    step = rows * per_row
    base = order_ref[slot] * step
    a_base = lax.rem(far_ref[0], I32(times)) * step
    d_base = lax.rem(own_ref[0], I32(times)) * step
    lo, hi = pl.ds(0, size), pl.ds(size, size)

    b_copies = [
        pltpu.make_async_copy(b_ref, held.at[at % 2], sems.at[at % 2]) for at, b_ref in enumerate(b_refs)
    ]

    @pl.when(slot == 0)
    def _():
        b_copies[0].start()
        for r in range(rows):
            for j in range(per_row):
                real, imag = a_ref[0, r, j], a_ref[1, r, j]
                la[r, j, lo, lo] = real
                la[r, j, lo, hi] = -imag
                la[r, j, hi, lo] = imag
                la[r, j, hi, hi] = real
                real, imag = d_ref[0, r, j].T, d_ref[1, r, j].T
                ld[r, j, lo, lo] = real
                ld[r, j, lo, hi] = -imag
                ld[r, j, hi, lo] = imag
                ld[r, j, hi, hi] = real

    for at in range(times):

        @pl.when(slot == at)
        def _():
            if at + 1 < times:
                b_copies[at + 1].start()
            b_copies[at].wait()

    @pl.when(active_ref[s * times + slot] == 0)
    def _():
        u_ref[...] = jnp.zeros_like(u_ref)

    @pl.when(active_ref[s * times + slot] != 0)
    def _():
        for r in range(rows):
            for j in range(per_row):
                bs[r, lo, pl.ds(j * size, size)] = held[slot % 2, 0, r, j]
                bs[r, hi, pl.ds(j * size, size)] = held[slot % 2, 1, r, j]

        yn[...] = jnp.zeros_like(yn)
        for r in range(rows):
            inners = [far_cols[a_base + r * per_row + j] for j in range(per_row)]
            parts = [
                jnp.dot(la[r, j], bs[inners[j]], preferred_element_type=F32) for j in range(per_row)
            ]
            pieces = []
            for j in range(per_row):
                for k in range(per_row):
                    col = b_cols[base + inners[j] * per_row + k]
                    pieces.append((j, col, parts[j][:, k * size : (k + 1) * size]))
            for at in reversed(range(len(pieces))):
                j, col, value = pieces[at]
                for other_j, other_col, other in pieces:
                    if other_j > j:
                        value = value + jnp.where(other_col == col, 1.0, 0.0) * other
                yn[col, pl.ds(r * size, size), lo] = value[:size].astype(BF16)
                yn[col, pl.ds(r * size, size), hi] = value[size:].astype(BF16)

        trace_real = jnp.zeros((size, size), F32)
        trace_imag = jnp.zeros((size, size), F32)
        for r in range(rows):
            trace_real += yn[r, pl.ds(r * size, size), lo].astype(F32)
            trace_imag += yn[r, pl.ds(r * size, size), hi].astype(F32)
        diagonal = lax.broadcasted_iota(I32, (size, size), 0) == lax.broadcasted_iota(I32, (size, size), 1)
        trace_real = jnp.sum(jnp.where(diagonal, trace_real, 0.0))
        trace_imag = jnp.sum(jnp.where(diagonal, trace_imag, 0.0))

        for r in range(rows):
            for j in range(per_row):
                col = m_cols[base + r * per_row + j]
                pick = I32(0)
                keep = F32(0)
                for k in range(per_row):
                    hit = own_cols[d_base + col * per_row + k] == r
                    pick = jnp.where(hit, I32(k), pick)
                    keep = jnp.where(hit, F32(1), keep)
                real = ld[col, pick, lo, lo].astype(F32)
                imag = ld[col, pick, hi, lo].astype(F32)
                weight_real, weight_imag = trace_real * keep, trace_imag * keep
                u_ref[0, r, j, 0] = weight_real * real - weight_imag * imag
                u_ref[0, r, j, 1] = weight_real * imag + weight_imag * real

        for i in range(rows):
            for j in range(per_row):
                r = own_cols[d_base + i * per_row + j]
                met = [m_cols[base + r * per_row + k] for k in range(per_row)]
                right = jnp.concatenate(
                    [yn[i, pl.ds(pl.multiple_of(col * size, size), size)] for col in met], axis=0
                )
                part = lax.dot_general(
                    ld[i, j], right, (((1,), (1,)), ((), ())), preferred_element_type=F32
                )
                for k in range(per_row):
                    u_ref[0, r, k, 0] -= part[:size, k * size : (k + 1) * size]
                    u_ref[0, r, k, 1] -= part[size:, k * size : (k + 1) * size]


def weights(flops, s, order, active, far_time, own_time, far_cols, own_cols, m_cols, b_cols, a, d, picked):
    times = len(picked)
    _, rows, per_row, size, _ = a.shape
    whole = lambda slot, *_: (0, 0, 0, 0, 0)
    return pl.pallas_call(
        lambda *refs: weights_kernel(s, *refs),
        out_shape=jax.ShapeDtypeStruct((times, rows, per_row, 2, size, size), F32),
        grid_spec=pltpu.PrefetchScalarGridSpec(
            num_scalar_prefetch=8,
            grid=(times,),
            in_specs=[
                pl.BlockSpec(a.shape, whole),
                pl.BlockSpec(a.shape, whole),
                *[ANY] * times,
            ],
            out_specs=pl.BlockSpec(
                (1, rows, per_row, 2, size, size), lambda slot, *_: (slot, 0, 0, 0, 0, 0)
            ),
            scratch_shapes=[
                pltpu.VMEM((rows, per_row, 2 * size, 2 * size), BF16),
                pltpu.VMEM((rows, per_row, 2 * size, 2 * size), BF16),
                pltpu.VMEM((rows, 2 * size, per_row * size), BF16),
                pltpu.VMEM((rows, rows * size, 2 * size), BF16),
                pltpu.VMEM((2,) + a.shape, a.dtype),
                pltpu.SemaphoreType.DMA((2,)),
            ],
        ),
        compiler_params=pltpu.CompilerParams(vmem_limit_bytes=24 * 2**20),
        cost_estimate=cost(flops, times * 1_000_000),
        name="weights",
    )(order, active, far_time, own_time, far_cols, own_cols, m_cols, b_cols, a, d, *picked)


def products(field_ref, u_refs, slot):
    _, rows, per_row, size, _ = field_ref.shape
    chunk = min(size, 32)
    fold = lambda x: jnp.sum(x.reshape(chunk // 8, 8, size), axis=0)
    sums = [jnp.zeros((8, size), F32) for _ in range(2 * len(u_refs))]
    for r in range(rows):
        for j in range(per_row):
            for start in range(0, size, chunk):
                at = pl.ds(start, chunk)
                real = field_ref[0, r, j, at].astype(F32)
                imag = field_ref[1, r, j, at].astype(F32)
                for s, u_ref in enumerate(u_refs):
                    u_real, u_imag = u_ref[slot, r, j, 0, at], u_ref[slot, r, j, 1, at]
                    sums[2 * s] += fold(real * u_real - imag * u_imag)
                    sums[2 * s + 1] += fold(real * u_imag + imag * u_real)
    return sums


def inner_kernel(slot, field_ref, u0_ref, u1_ref, out_ref):
    for at, value in enumerate(products(field_ref, (u0_ref, u1_ref), slot)):
        out_ref[at] = value


def inner(slot, field, u0, u1):
    return pl.pallas_call(
        lambda *refs: inner_kernel(slot, *refs),
        out_shape=jax.ShapeDtypeStruct((4, 8, field.shape[-1]), F32),
        in_specs=[VMEM] * 3,
        out_specs=VMEM,
        cost_estimate=cost(4_000_000, 4_000_000),
        compiler_params=pltpu.CompilerParams(vmem_limit_bytes=24 * 2**20),
        name="inner",
    )(field, u0, u1)


def stage_kernel(slot, u0_ref, u1_ref, out0_ref, out1_ref, sems):
    copies = [
        pltpu.make_async_copy(u_ref.at[slot, r], out_ref.at[0, r], sems.at[s, r])
        for s, (u_ref, out_ref) in enumerate(((u0_ref, out0_ref), (u1_ref, out1_ref)))
        for r in range(u_ref.shape[1])
    ]
    for copy in copies:
        copy.start()
    for copy in copies:
        copy.wait()


def stage(slot, u0, u1):
    one = jax.ShapeDtypeStruct((1,) + u0.shape[1:], u0.dtype)
    return pl.pallas_call(
        lambda *refs: stage_kernel(slot, *refs),
        out_shape=[one, one],
        in_specs=[ANY] * 2,
        out_specs=[VMEM] * 2,
        scratch_shapes=[pltpu.SemaphoreType.DMA((2, u0.shape[1]))],
        cost_estimate=cost(0, 6_000_000),
        compiler_params=pltpu.CompilerParams(vmem_limit_bytes=24 * 2**20),
        name="stage",
    )(u0, u1)


def last_kernel(core_ref, order_ref, sinks_ref, *refs):
    *others, field_ref, u0_ref, u1_ref, mine_ref, theirs_ref = refs
    slots = order_ref.shape[0]
    deltas = sinks_ref.shape[0] // 2
    share = deltas // 2
    core = core_ref[0]
    sums = [[ref[at] for at in range(4)] for ref in others]
    sums.insert(slots - 2, products(field_ref, (u0_ref, u1_ref), 0))
    for out_ref, owner in ((mine_ref, core), (theirs_ref, 1 - core)):
        lines = [jnp.zeros(sums[0][0].shape, F32) for _ in range(2 * share)]
        for slot in range(slots):
            time = core * slots + order_ref[slot]
            for s in range(2):
                for k in range(share):
                    sink = sinks_ref[s * deltas + owner * share + k]
                    keep = jnp.where(sink == time, F32(1), F32(0))
                    for part in range(2):
                        lines[part * share + k] += keep * sums[slot][2 * s + part]
        table = jnp.concatenate([jnp.sum(line, axis=0, keepdims=True) for line in lines], axis=0)
        table = jnp.sum(table, axis=1, keepdims=True)
        for part in range(2):
            out_ref[part] = table[part * share : (part + 1) * share]


def last(core, order, sinks, others, field, u0, u1):
    share = sinks.shape[0] // 4
    return pl.pallas_call(
        last_kernel,
        out_shape=[jax.ShapeDtypeStruct((2, share, 1), F32)] * 2,
        in_specs=[SMEM] * 3 + [VMEM] * (len(others) + 3),
        out_specs=[VMEM] * 2,
        cost_estimate=cost(4_000_000, 4_000_000),
        compiler_params=pltpu.CompilerParams(vmem_limit_bytes=24 * 2**20),
        name="last",
    )(core, order, sinks, *others, field, u0, u1)


def local(fields, block_cols, sources, deltas, partner):
    assert fields.shape[0] == 1 and lax.axis_size("src") == 2
    del partner
    fields = fields[0]
    times = fields.shape[0]
    core = lax.axis_index("src").reshape(1)
    pairs = one_way_pairs(lax.axis_size("mom"))
    swap = lambda value: lax.ppermute(value, "src", [(0, 1), (1, 0)])
    to_partner = lambda value: lax.ppermute(value, "mom", pairs)

    cols = block_cols.reshape(-1)
    far_cols = to_partner(cols)
    own_field = pick_source(sources, fields)
    far = [to_partner(own_field)]

    other_time = swap(sources)
    order, sinks, active, full = plan(core, sources, other_time, deltas, times)
    others = pick_others(order, fields)
    picked = [own_field, *others]
    *early, late = others
    for field in early:
        if len(far) > 1:
            field, far[-2] = lax.optimization_barrier((field, far[-2]))
        far.append(to_partner(field))

    other_cols = swap(cols)
    far_other_cols = swap(far_cols)
    other_field = swap(own_field)
    far_other = swap(far[0])
    u0 = weights(
        80_000_000_000,
        0,
        order,
        active,
        sources,
        sources,
        far_cols,
        cols,
        far_cols,
        cols,
        far[0],
        own_field,
        picked,
    )
    u1 = weights(
        2_000_000_000,
        1,
        order,
        active,
        other_time,
        other_time,
        far_other_cols,
        other_cols,
        far_cols,
        cols,
        far_other,
        other_field,
        picked,
    )
    sums = [inner(slot, far[slot], u0, u1) for slot in range(times - 2)]

    both = ("mom", "src")

    def with_slot(cores):
        routes = [(2 * a + c, 2 * b + c) for a, b in pairs for c in cores]

        def branch(field, u0, u1):
            field = lax.ppermute(field, both, routes)
            return inner(times - 1, field, u0, u1), *stage(times - 2, u0, u1)

        return branch

    def without_slot(field, u0, u1):
        return jnp.zeros(sums[0].shape, F32), *stage(times - 2, u0, u1)

    branches = [without_slot, with_slot([0]), with_slot([1]), with_slot([0, 1])]
    late, *sums = lax.optimization_barrier((late, *sums))
    late_sums, staged0, staged1 = lax.switch(full[0], branches, late, u0, u1)
    mine, theirs = last(core, order, sinks, [*sums, late_sums], far[-1], staged0, staged1)

    total = mine + swap(theirs)
    back = [(2 * a + c, 2 * b + c) for b, a in pairs for c in range(2)]
    return total + lax.ppermute(total, both, back)


def solution(mesh):
    in_specs = (
        P(("ens", "mom"), "src", None, None, None, None, None),
        P(("ens", "mom"), "src", None, None),
        P("src"),
        P(),
        P("mom"),
    )
    out_specs = P(None, "src", ("ens", "mom"))
    return jax.shard_map(local, mesh=mesh, in_specs=in_specs, out_specs=out_specs, check_vma=False)
```

```python
import jax
import jax.numpy as jnp
from jax import lax
from jax.experimental import pallas as pl
from jax.experimental.pallas import tpu as pltpu
from jax.sharding import PartitionSpec as P

F32 = jnp.float32
BF16 = jnp.bfloat16
I32 = jnp.int32
SMEM = pl.BlockSpec(memory_space=pltpu.SMEM)
VMEM = pl.BlockSpec(memory_space=pltpu.VMEM)
ANY = pl.BlockSpec(memory_space=pl.ANY)


def one_way_pairs(count):
    half = count // 2
    outer = half // 2
    return [(g + half, g) if g < outer else (g, g + half) for g in range(half)]


def cost(flops, size):
    return pl.CostEstimate(flops=flops, bytes_accessed=size, transcendentals=0)


def pick_source_kernel(source_ref, fields_ref, out_ref, sems):
    time = lax.rem(source_ref[0], I32(fields_ref.shape[0]))
    copies = [
        pltpu.make_async_copy(fields_ref.at[time, part, r], out_ref.at[part, r], sems.at[part, r])
        for part in range(fields_ref.shape[1])
        for r in range(fields_ref.shape[2])
    ]
    for copy in copies:
        copy.start()
    for copy in copies:
        copy.wait()


def pick_source(source, fields):
    return pl.pallas_call(
        pick_source_kernel,
        out_shape=jax.ShapeDtypeStruct(fields.shape[1:], fields.dtype),
        in_specs=[SMEM, ANY],
        out_specs=VMEM,
        scratch_shapes=[pltpu.SemaphoreType.DMA(fields.shape[1:3])],
        cost_estimate=cost(0, 1_600_000),
        compiler_params=pltpu.CompilerParams(vmem_limit_bytes=52 * 2**20),
        name="pick_source",
    )(source, fields)


def pick_kernel(pieces, order_ref, fields_ref, *refs):
    *outs, sems = refs
    copies = [
        pltpu.make_async_copy(
            fields_ref.at[order_ref[slot], part, pl.ds(first, rows)], out.at[part], sems.at[at, part]
        )
        for at, ((slot, first, rows), out) in enumerate(zip(pieces, outs))
        for part in range(2)
    ]
    for copy in copies:
        copy.start()
    for copy in copies:
        copy.wait()


def pick_others(order, fields, pieces):
    return pl.pallas_call(
        lambda *refs: pick_kernel(pieces, *refs),
        out_shape=[
            jax.ShapeDtypeStruct((2, rows) + fields.shape[3:], fields.dtype) for _, _, rows in pieces
        ],
        in_specs=[SMEM, ANY],
        out_specs=[VMEM] * len(pieces),
        scratch_shapes=[pltpu.SemaphoreType.DMA((len(pieces), 2))],
        cost_estimate=cost(0, 5_000_000),
        compiler_params=pltpu.CompilerParams(vmem_limit_bytes=58 * 2**20),
        name="pick_others",
    )(order, fields)


def plan_kernel(core_ref, own_ref, other_ref, deltas_ref, order_ref, sinks_ref, active_ref, full_ref):
    times = order_ref.shape[0]
    deltas = deltas_ref.shape[0]
    sinks = []
    for s, ref in enumerate((own_ref, other_ref)):
        for k in range(deltas):
            sink = lax.rem(ref[0] + deltas_ref[k], I32(2 * times))
            sinks_ref[s * deltas + k] = sink
            sinks.append(sink)
    base = core_ref[0] * times
    first = own_ref[0] - base
    keys = []
    for t in range(times):
        needed = sinks[0] == base + t
        for sink in sinks[1:]:
            needed = needed | (sink == base + t)
        key = jnp.where(needed, I32(t), I32(times + t))
        keys.append(jnp.where(first == t, I32(-1), key))
    for t in range(times):
        rank = I32(0)
        for other in range(times):
            if other != t:
                rank += (keys[other] < keys[t]).astype(I32)
        order_ref[rank] = I32(t)
        for s in range(2):
            active = sinks[s * deltas] == base + t
            for k in range(1, deltas):
                active = active | (sinks[s * deltas + k] == base + t)
            active_ref[s * times + rank] = active.astype(I32)
    full = I32(0)
    for c in range(2):
        count = I32(0)
        for t in range(times):
            needed = (own_ref[0] == c * times + t) | (other_ref[0] == c * times + t)
            for sink in sinks:
                needed = needed | (sink == c * times + t)
            count += needed.astype(I32)
        full += jnp.where(count == times, I32(1 << c), I32(0))
    full_ref[0] = full


def plan(core, own, other, deltas, times):
    return pl.pallas_call(
        plan_kernel,
        out_shape=[
            jax.ShapeDtypeStruct((times,), I32),
            jax.ShapeDtypeStruct((2 * deltas.shape[0],), I32),
            jax.ShapeDtypeStruct((2 * times,), I32),
            jax.ShapeDtypeStruct((1,), I32),
        ],
        in_specs=[SMEM] * 4,
        out_specs=[SMEM] * 4,
        cost_estimate=cost(0, 1000),
        name="plan",
    )(core, own, other, deltas)


def weights_kernel(s, pieces, order_ref, active_ref, *refs):
    far_ref, own_ref, far_cols, own_cols, m_cols, b_cols, a_ref, d_ref, *refs = refs
    *b_refs, u_ref, la, ld, bs, yn, held, sems = refs
    slot = pl.program_id(0)
    rows, per_row, size = a_ref.shape[1], a_ref.shape[2], a_ref.shape[3]
    times = order_ref.shape[0]
    step = rows * per_row
    base = order_ref[slot] * step
    a_base = lax.rem(far_ref[0], I32(times)) * step
    d_base = lax.rem(own_ref[0], I32(times)) * step
    lo, hi = pl.ds(0, size), pl.ds(size, size)

    b_copies = [[] for _ in range(times)]
    for at, ((piece_slot, first, count), b_ref) in enumerate(zip(pieces, b_refs)):
        for part in range(2):
            to = held.at[piece_slot % 2, part, pl.ds(first, count)]
            b_copies[piece_slot].append(pltpu.make_async_copy(b_ref.at[part], to, sems.at[at, part]))

    @pl.when(slot == 0)
    def _():
        for copy in b_copies[0]:
            copy.start()
        for r in range(rows):
            for j in range(per_row):
                real, imag = a_ref[0, r, j], a_ref[1, r, j]
                la[r, j, lo, lo] = real
                la[r, j, lo, hi] = -imag
                la[r, j, hi, lo] = imag
                la[r, j, hi, hi] = real
                real, imag = d_ref[0, r, j].T, d_ref[1, r, j].T
                ld[r, j, lo, lo] = real
                ld[r, j, lo, hi] = -imag
                ld[r, j, hi, lo] = imag
                ld[r, j, hi, hi] = real

    for at in range(times):

        @pl.when(slot == at)
        def _():
            for copy in b_copies[at + 1] if at + 1 < times else []:
                copy.start()
            for copy in b_copies[at]:
                copy.wait()

    @pl.when(active_ref[s * times + slot] == 0)
    def _():
        u_ref[...] = jnp.zeros_like(u_ref)

    @pl.when(active_ref[s * times + slot] != 0)
    def _():
        for r in range(rows):
            for j in range(per_row):
                bs[r, lo, pl.ds(j * size, size)] = held[slot % 2, 0, r, j]
                bs[r, hi, pl.ds(j * size, size)] = held[slot % 2, 1, r, j]

        yn[...] = jnp.zeros_like(yn)
        for r in range(rows):
            inners = [far_cols[a_base + r * per_row + j] for j in range(per_row)]
            parts = [
                jnp.dot(la[r, j], bs[inners[j]], preferred_element_type=F32) for j in range(per_row)
            ]
            pieces = []
            for j in range(per_row):
                for k in range(per_row):
                    col = b_cols[base + inners[j] * per_row + k]
                    pieces.append((j, col, parts[j][:, k * size : (k + 1) * size]))
            for at in reversed(range(len(pieces))):
                j, col, value = pieces[at]
                for other_j, other_col, other in pieces:
                    if other_j > j:
                        value = value + jnp.where(other_col == col, 1.0, 0.0) * other
                yn[col, pl.ds(r * size, size), lo] = value[:size].astype(BF16)
                yn[col, pl.ds(r * size, size), hi] = value[size:].astype(BF16)

        trace_real = jnp.zeros((size, size), F32)
        trace_imag = jnp.zeros((size, size), F32)
        for r in range(rows):
            trace_real += yn[r, pl.ds(r * size, size), lo].astype(F32)
            trace_imag += yn[r, pl.ds(r * size, size), hi].astype(F32)
        diagonal = lax.broadcasted_iota(I32, (size, size), 0) == lax.broadcasted_iota(I32, (size, size), 1)
        trace_real = jnp.sum(jnp.where(diagonal, trace_real, 0.0))
        trace_imag = jnp.sum(jnp.where(diagonal, trace_imag, 0.0))

        for r in range(rows):
            for j in range(per_row):
                col = m_cols[base + r * per_row + j]
                pick = I32(0)
                keep = F32(0)
                for k in range(per_row):
                    hit = own_cols[d_base + col * per_row + k] == r
                    pick = jnp.where(hit, I32(k), pick)
                    keep = jnp.where(hit, F32(1), keep)
                real = ld[col, pick, lo, lo].astype(F32)
                imag = ld[col, pick, hi, lo].astype(F32)
                weight_real, weight_imag = trace_real * keep, trace_imag * keep
                u_ref[0, r, j, 0] = weight_real * real - weight_imag * imag
                u_ref[0, r, j, 1] = weight_real * imag + weight_imag * real

        for i in range(rows):
            for j in range(per_row):
                r = own_cols[d_base + i * per_row + j]
                met = [m_cols[base + r * per_row + k] for k in range(per_row)]
                right = jnp.concatenate(
                    [yn[i, pl.ds(pl.multiple_of(col * size, size), size)] for col in met], axis=0
                )
                part = lax.dot_general(
                    ld[i, j], right, (((1,), (1,)), ((), ())), preferred_element_type=F32
                )
                for k in range(per_row):
                    u_ref[0, r, k, 0] -= part[:size, k * size : (k + 1) * size]
                    u_ref[0, r, k, 1] -= part[size:, k * size : (k + 1) * size]


def weights(flops, s, pieces, order, active, far_time, own_time, far_cols, own_cols, m_cols, b_cols, a, d, picked):
    times = order.shape[0]
    _, rows, per_row, size, _ = a.shape
    whole = lambda slot, *_: (0, 0, 0, 0, 0)
    return pl.pallas_call(
        lambda *refs: weights_kernel(s, pieces, *refs),
        out_shape=jax.ShapeDtypeStruct((times, rows, per_row, 2, size, size), F32),
        grid_spec=pltpu.PrefetchScalarGridSpec(
            num_scalar_prefetch=8,
            grid=(times,),
            in_specs=[
                pl.BlockSpec(a.shape, whole),
                pl.BlockSpec(a.shape, whole),
                *[ANY] * len(picked),
            ],
            out_specs=pl.BlockSpec(
                (1, rows, per_row, 2, size, size), lambda slot, *_: (slot, 0, 0, 0, 0, 0)
            ),
            scratch_shapes=[
                pltpu.VMEM((rows, per_row, 2 * size, 2 * size), BF16),
                pltpu.VMEM((rows, per_row, 2 * size, 2 * size), BF16),
                pltpu.VMEM((rows, 2 * size, per_row * size), BF16),
                pltpu.VMEM((rows, rows * size, 2 * size), BF16),
                pltpu.VMEM((2,) + a.shape, a.dtype),
                pltpu.SemaphoreType.DMA((len(picked), 2)),
            ],
        ),
        compiler_params=pltpu.CompilerParams(vmem_limit_bytes=24 * 2**20),
        cost_estimate=cost(flops, times * 1_000_000),
        name="weights",
    )(order, active, far_time, own_time, far_cols, own_cols, m_cols, b_cols, a, d, *picked)


def products(field_ref, u_refs, slot, first):
    _, rows, per_row, size, _ = field_ref.shape
    chunk = min(size, 32)
    fold = lambda x: jnp.sum(x.reshape(chunk // 8, 8, size), axis=0)
    sums = [jnp.zeros((8, size), F32) for _ in range(2 * len(u_refs))]
    for r in range(rows):
        for j in range(per_row):
            for start in range(0, size, chunk):
                at = pl.ds(start, chunk)
                real = field_ref[0, r, j, at].astype(F32)
                imag = field_ref[1, r, j, at].astype(F32)
                for s, u_ref in enumerate(u_refs):
                    u_real, u_imag = u_ref[slot, first + r, j, 0, at], u_ref[slot, first + r, j, 1, at]
                    sums[2 * s] += fold(real * u_real - imag * u_imag)
                    sums[2 * s + 1] += fold(real * u_imag + imag * u_real)
    return sums


def inner_kernel(slot, first, field_ref, u0_ref, u1_ref, *refs):
    *before, out_ref = refs
    for at, value in enumerate(products(field_ref, (u0_ref, u1_ref), slot, first)):
        out_ref[at] = value + before[0][at] if before else value


def inner(slot, first, field, u0, u1, *before):
    return pl.pallas_call(
        lambda *refs: inner_kernel(slot, first, *refs),
        out_shape=jax.ShapeDtypeStruct((4, 8, field.shape[-1]), F32),
        in_specs=[VMEM] * (3 + len(before)),
        out_specs=VMEM,
        cost_estimate=cost(4_000_000, 4_000_000),
        compiler_params=pltpu.CompilerParams(vmem_limit_bytes=24 * 2**20),
        name="inner",
    )(field, u0, u1, *before)


def stage_kernel(slot, u0_ref, u1_ref, out0_ref, out1_ref, sems):
    copies = [
        pltpu.make_async_copy(u_ref.at[slot, r], out_ref.at[0, r], sems.at[s, r])
        for s, (u_ref, out_ref) in enumerate(((u0_ref, out0_ref), (u1_ref, out1_ref)))
        for r in range(u_ref.shape[1])
    ]
    for copy in copies:
        copy.start()
    for copy in copies:
        copy.wait()


def stage(slot, u0, u1):
    one = jax.ShapeDtypeStruct((1,) + u0.shape[1:], u0.dtype)
    return pl.pallas_call(
        lambda *refs: stage_kernel(slot, *refs),
        out_shape=[one, one],
        in_specs=[ANY] * 2,
        out_specs=[VMEM] * 2,
        scratch_shapes=[pltpu.SemaphoreType.DMA((2, u0.shape[1]))],
        cost_estimate=cost(0, 6_000_000),
        compiler_params=pltpu.CompilerParams(vmem_limit_bytes=24 * 2**20),
        name="stage",
    )(u0, u1)


def last_kernel(first, core_ref, order_ref, sinks_ref, *refs):
    *held, field_ref, u0_ref, u1_ref, mine_ref, theirs_ref = refs
    slots = order_ref.shape[0]
    deltas = sinks_ref.shape[0] // 2
    share = deltas // 2
    core = core_ref[0]
    sums = [[ref[at] for at in range(4)] for ref in held]
    for at, value in enumerate(products(field_ref, (u0_ref, u1_ref), 0, first)):
        sums[slots - 2][at] += value
    for out_ref, owner in ((mine_ref, core), (theirs_ref, 1 - core)):
        lines = [jnp.zeros(sums[0][0].shape, F32) for _ in range(2 * share)]
        for slot in range(slots):
            time = core * slots + order_ref[slot]
            for s in range(2):
                for k in range(share):
                    sink = sinks_ref[s * deltas + owner * share + k]
                    keep = jnp.where(sink == time, F32(1), F32(0))
                    for part in range(2):
                        lines[part * share + k] += keep * sums[slot][2 * s + part]
        table = jnp.concatenate([jnp.sum(line, axis=0, keepdims=True) for line in lines], axis=0)
        table = jnp.sum(table, axis=1, keepdims=True)
        for part in range(2):
            out_ref[part] = table[part * share : (part + 1) * share]


def last(first, core, order, sinks, sums, field, u0, u1):
    share = sinks.shape[0] // 4
    return pl.pallas_call(
        lambda *refs: last_kernel(first, *refs),
        out_shape=[jax.ShapeDtypeStruct((2, share, 1), F32)] * 2,
        in_specs=[SMEM] * 3 + [VMEM] * (len(sums) + 3),
        out_specs=[VMEM] * 2,
        cost_estimate=cost(4_000_000, 4_000_000),
        compiler_params=pltpu.CompilerParams(vmem_limit_bytes=24 * 2**20),
        name="last",
    )(core, order, sinks, *sums, field, u0, u1)


def local(fields, block_cols, sources, deltas, partner):
    assert fields.shape[0] == 1 and lax.axis_size("src") == 2
    del partner
    fields = fields[0]
    times = fields.shape[0]
    core = lax.axis_index("src").reshape(1)
    pairs = one_way_pairs(lax.axis_size("mom"))
    swap = lambda value: lax.ppermute(value, "src", [(0, 1), (1, 0)])
    to_partner = lambda value: lax.ppermute(value, "mom", pairs)

    cols = block_cols.reshape(-1)
    far_cols = to_partner(cols)
    own_field = pick_source(sources, fields)
    far = [to_partner(own_field)]

    other_time = swap(sources)
    order, sinks, active, full = plan(core, sources, other_time, deltas, times)
    rows = fields.shape[2]
    half = rows // 2
    halves = [(0, half), (half, rows - half)]
    pieces = [(0, 0, rows), *[(slot, 0, rows) for slot in range(1, times - 2)]]
    pieces += [(slot, *part) for slot in (times - 2, times - 1) for part in halves]
    picked = [own_field, *pick_others(order, fields, pieces[1:])]
    *early, near_low, near_high, late_low, late_high = picked
    far += [to_partner(field) for field in early[1:]]
    near_low, near_high, far[0] = lax.optimization_barrier((near_low, near_high, far[0]))
    near = [to_partner(near_low), to_partner(near_high)]

    other_cols = swap(cols)
    far_other_cols = swap(far_cols)
    other_field = swap(own_field)
    far_other = swap(far[0])
    u0 = weights(
        80_000_000_000,
        0,
        pieces,
        order,
        active,
        sources,
        sources,
        far_cols,
        cols,
        far_cols,
        cols,
        far[0],
        own_field,
        picked,
    )
    u1 = weights(
        2_000_000_000,
        1,
        pieces,
        order,
        active,
        other_time,
        other_time,
        far_other_cols,
        other_cols,
        far_cols,
        cols,
        far_other,
        other_field,
        picked,
    )
    sums = [inner(slot, 0, field, u0, u1) for slot, field in enumerate(far)]

    both = ("mom", "src")

    def with_slot(cores):
        routes = [(2 * a + c, 2 * b + c) for a, b in pairs for c in cores]

        def branch(low, high, u0, u1):
            low, high = lax.ppermute(low, both, routes), lax.ppermute(high, both, routes)
            before = inner(times - 1, 0, low, u0, u1)
            return inner(times - 1, half, high, u0, u1, before), *stage(times - 2, u0, u1)

        return branch

    def without_slot(low, high, u0, u1):
        return jnp.zeros(sums[0].shape, F32), *stage(times - 2, u0, u1)

    branches = [without_slot, with_slot([0]), with_slot([1]), with_slot([0, 1])]
    late_low, late_high, *sums = lax.optimization_barrier((late_low, late_high, *sums))
    late_sums, staged0, staged1 = lax.switch(full[0], branches, late_low, late_high, u0, u1)
    sums += [inner(0, 0, near[0], staged0, staged1), late_sums]
    mine, theirs = last(half, core, order, sinks, sums, near[1], staged0, staged1)

    total = mine + swap(theirs)
    back = [(2 * a + c, 2 * b + c) for b, a in pairs for c in range(2)]
    return total + lax.ppermute(total, both, back)


def solution(mesh):
    in_specs = (
        P(("ens", "mom"), "src", None, None, None, None, None),
        P(("ens", "mom"), "src", None, None),
        P("src"),
        P(),
        P("mom"),
    )
    out_specs = P(None, "src", ("ens", "mom"))
    return jax.shard_map(local, mesh=mesh, in_specs=in_specs, out_specs=out_specs, check_vma=False)
```

```python
import jax
import jax.numpy as jnp
from jax import lax
from jax.experimental import pallas as pl
from jax.experimental.pallas import tpu as pltpu
from jax.sharding import PartitionSpec as P

F32 = jnp.float32
BF16 = jnp.bfloat16
I32 = jnp.int32
SMEM = pl.BlockSpec(memory_space=pltpu.SMEM)
VMEM = pl.BlockSpec(memory_space=pltpu.VMEM)
ANY = pl.BlockSpec(memory_space=pl.ANY)


def one_way_pairs(count):
    half = count // 2
    outer = half // 2
    return [(g + half, g) if g < outer else (g, g + half) for g in range(half)]


def cost(flops, size):
    return pl.CostEstimate(flops=flops, bytes_accessed=size, transcendentals=0)


def pick_source_kernel(source_ref, fields_ref, out_ref, sems):
    time = lax.rem(source_ref[0], I32(fields_ref.shape[0]))
    copies = [
        pltpu.make_async_copy(fields_ref.at[time, part, r], out_ref.at[part, r], sems.at[part, r])
        for part in range(fields_ref.shape[1])
        for r in range(fields_ref.shape[2])
    ]
    for copy in copies:
        copy.start()
    for copy in copies:
        copy.wait()


def pick_source(source, fields):
    return pl.pallas_call(
        pick_source_kernel,
        out_shape=jax.ShapeDtypeStruct(fields.shape[1:], fields.dtype),
        in_specs=[SMEM, ANY],
        out_specs=VMEM,
        scratch_shapes=[pltpu.SemaphoreType.DMA(fields.shape[1:3])],
        cost_estimate=cost(0, 1_600_000),
        compiler_params=pltpu.CompilerParams(vmem_limit_bytes=52 * 2**20),
        name="pick_source",
    )(source, fields)


def pick_kernel(pieces, order_ref, fields_ref, *refs):
    *outs, sems = refs
    copies = [
        pltpu.make_async_copy(
            fields_ref.at[order_ref[slot], part, pl.ds(first, rows)], out.at[part], sems.at[at, part]
        )
        for at, ((slot, first, rows), out) in enumerate(zip(pieces, outs))
        for part in range(2)
    ]
    for copy in copies:
        copy.start()
    for copy in copies:
        copy.wait()


def pick_others(order, fields, pieces):
    return pl.pallas_call(
        lambda *refs: pick_kernel(pieces, *refs),
        out_shape=[
            jax.ShapeDtypeStruct((2, rows) + fields.shape[3:], fields.dtype) for _, _, rows in pieces
        ],
        in_specs=[SMEM, ANY],
        out_specs=[VMEM] * len(pieces),
        scratch_shapes=[pltpu.SemaphoreType.DMA((len(pieces), 2))],
        cost_estimate=cost(0, 5_000_000),
        compiler_params=pltpu.CompilerParams(vmem_limit_bytes=58 * 2**20),
        name="pick_others",
    )(order, fields)


def plan_kernel(core_ref, own_ref, other_ref, deltas_ref, order_ref, sinks_ref, active_ref, full_ref):
    times = order_ref.shape[0]
    deltas = deltas_ref.shape[0]
    sinks = []
    for s, ref in enumerate((own_ref, other_ref)):
        for k in range(deltas):
            sink = lax.rem(ref[0] + deltas_ref[k], I32(2 * times))
            sinks_ref[s * deltas + k] = sink
            sinks.append(sink)
    base = core_ref[0] * times
    first = own_ref[0] - base
    keys = []
    for t in range(times):
        needed = sinks[0] == base + t
        for sink in sinks[1:]:
            needed = needed | (sink == base + t)
        key = jnp.where(needed, I32(t), I32(times + t))
        keys.append(jnp.where(first == t, I32(-1), key))
    for t in range(times):
        rank = I32(0)
        for other in range(times):
            if other != t:
                rank += (keys[other] < keys[t]).astype(I32)
        order_ref[rank] = I32(t)
        for s in range(2):
            active = sinks[s * deltas] == base + t
            for k in range(1, deltas):
                active = active | (sinks[s * deltas + k] == base + t)
            active_ref[s * times + rank] = active.astype(I32)
    full = I32(0)
    for c in range(2):
        count = I32(0)
        for t in range(times):
            needed = (own_ref[0] == c * times + t) | (other_ref[0] == c * times + t)
            for sink in sinks:
                needed = needed | (sink == c * times + t)
            count += needed.astype(I32)
        full += jnp.where(count == times, I32(1 << c), I32(0))
    full_ref[0] = full


def plan(core, own, other, deltas, times):
    return pl.pallas_call(
        plan_kernel,
        out_shape=[
            jax.ShapeDtypeStruct((times,), I32),
            jax.ShapeDtypeStruct((2 * deltas.shape[0],), I32),
            jax.ShapeDtypeStruct((2 * times,), I32),
            jax.ShapeDtypeStruct((1,), I32),
        ],
        in_specs=[SMEM] * 4,
        out_specs=[SMEM] * 4,
        cost_estimate=cost(0, 1000),
        name="plan",
    )(core, own, other, deltas)


def weights_kernel(s, pieces, order_ref, active_ref, *refs):
    far_ref, own_ref, far_cols, own_cols, m_cols, b_cols, a_ref, d_ref, *refs = refs
    *b_refs, u_ref, la, ld, bs, yn, held, sems = refs
    slot = pl.program_id(0)
    rows, per_row, size = a_ref.shape[1], a_ref.shape[2], a_ref.shape[3]
    times = order_ref.shape[0]
    step = rows * per_row
    base = order_ref[slot] * step
    a_base = lax.rem(far_ref[0], I32(times)) * step
    d_base = lax.rem(own_ref[0], I32(times)) * step
    lo, hi = pl.ds(0, size), pl.ds(size, size)

    b_copies = [[] for _ in range(times)]
    for at, ((piece_slot, first, count), b_ref) in enumerate(zip(pieces, b_refs)):
        for part in range(2):
            to = held.at[piece_slot % 2, part, pl.ds(first, count)]
            b_copies[piece_slot].append(pltpu.make_async_copy(b_ref.at[part], to, sems.at[at, part]))

    @pl.when(slot == 0)
    def _():
        for copy in b_copies[0]:
            copy.start()
        for r in range(rows):
            for j in range(per_row):
                real, imag = a_ref[0, r, j], a_ref[1, r, j]
                la[r, j, lo, lo] = real
                la[r, j, lo, hi] = -imag
                la[r, j, hi, lo] = imag
                la[r, j, hi, hi] = real
                real, imag = d_ref[0, r, j].T, d_ref[1, r, j].T
                ld[r, j, lo, lo] = real
                ld[r, j, lo, hi] = -imag
                ld[r, j, hi, lo] = imag
                ld[r, j, hi, hi] = real

    for at in range(times):

        @pl.when(slot == at)
        def _():
            for copy in b_copies[at + 1] if at + 1 < times else []:
                copy.start()
            for copy in b_copies[at]:
                copy.wait()

    @pl.when(active_ref[s * times + slot] == 0)
    def _():
        u_ref[...] = jnp.zeros_like(u_ref)

    @pl.when(active_ref[s * times + slot] != 0)
    def _():
        for r in range(rows):
            for j in range(per_row):
                bs[r, lo, pl.ds(j * size, size)] = held[slot % 2, 0, r, j]
                bs[r, hi, pl.ds(j * size, size)] = held[slot % 2, 1, r, j]

        yn[...] = jnp.zeros_like(yn)
        for r in range(rows):
            inners = [far_cols[a_base + r * per_row + j] for j in range(per_row)]
            parts = [
                jnp.dot(la[r, j], bs[inners[j]], preferred_element_type=F32) for j in range(per_row)
            ]
            pieces = []
            for j in range(per_row):
                for k in range(per_row):
                    col = b_cols[base + inners[j] * per_row + k]
                    pieces.append((j, col, parts[j][:, k * size : (k + 1) * size]))
            for at in reversed(range(len(pieces))):
                j, col, value = pieces[at]
                for other_j, other_col, other in pieces:
                    if other_j > j:
                        value = value + jnp.where(other_col == col, 1.0, 0.0) * other
                yn[col, pl.ds(r * size, size), lo] = value[:size].astype(BF16)
                yn[col, pl.ds(r * size, size), hi] = value[size:].astype(BF16)

        trace_real = jnp.zeros((size, size), F32)
        trace_imag = jnp.zeros((size, size), F32)
        for r in range(rows):
            trace_real += yn[r, pl.ds(r * size, size), lo].astype(F32)
            trace_imag += yn[r, pl.ds(r * size, size), hi].astype(F32)
        diagonal = lax.broadcasted_iota(I32, (size, size), 0) == lax.broadcasted_iota(I32, (size, size), 1)
        trace_real = jnp.sum(jnp.where(diagonal, trace_real, 0.0))
        trace_imag = jnp.sum(jnp.where(diagonal, trace_imag, 0.0))

        for r in range(rows):
            for j in range(per_row):
                col = m_cols[base + r * per_row + j]
                pick = I32(0)
                keep = F32(0)
                for k in range(per_row):
                    hit = own_cols[d_base + col * per_row + k] == r
                    pick = jnp.where(hit, I32(k), pick)
                    keep = jnp.where(hit, F32(1), keep)
                real = ld[col, pick, lo, lo].astype(F32)
                imag = ld[col, pick, hi, lo].astype(F32)
                weight_real, weight_imag = trace_real * keep, trace_imag * keep
                u_ref[0, r, j, 0] = weight_real * real - weight_imag * imag
                u_ref[0, r, j, 1] = weight_real * imag + weight_imag * real

        for i in range(rows):
            for j in range(per_row):
                r = own_cols[d_base + i * per_row + j]
                met = [m_cols[base + r * per_row + k] for k in range(per_row)]
                right = jnp.concatenate(
                    [yn[i, pl.ds(pl.multiple_of(col * size, size), size)] for col in met], axis=0
                )
                part = lax.dot_general(
                    ld[i, j], right, (((1,), (1,)), ((), ())), preferred_element_type=F32
                )
                for k in range(per_row):
                    u_ref[0, r, k, 0] -= part[:size, k * size : (k + 1) * size]
                    u_ref[0, r, k, 1] -= part[size:, k * size : (k + 1) * size]


def weights(flops, s, pieces, order, active, far_time, own_time, far_cols, own_cols, m_cols, b_cols, a, d, picked):
    times = order.shape[0]
    _, rows, per_row, size, _ = a.shape
    whole = lambda slot, *_: (0, 0, 0, 0, 0)
    return pl.pallas_call(
        lambda *refs: weights_kernel(s, pieces, *refs),
        out_shape=jax.ShapeDtypeStruct((times, rows, per_row, 2, size, size), F32),
        grid_spec=pltpu.PrefetchScalarGridSpec(
            num_scalar_prefetch=8,
            grid=(times,),
            in_specs=[
                pl.BlockSpec(a.shape, whole),
                pl.BlockSpec(a.shape, whole),
                *[ANY] * len(picked),
            ],
            out_specs=pl.BlockSpec(
                (1, rows, per_row, 2, size, size), lambda slot, *_: (slot, 0, 0, 0, 0, 0)
            ),
            scratch_shapes=[
                pltpu.VMEM((rows, per_row, 2 * size, 2 * size), BF16),
                pltpu.VMEM((rows, per_row, 2 * size, 2 * size), BF16),
                pltpu.VMEM((rows, 2 * size, per_row * size), BF16),
                pltpu.VMEM((rows, rows * size, 2 * size), BF16),
                pltpu.VMEM((2,) + a.shape, a.dtype),
                pltpu.SemaphoreType.DMA((len(picked), 2)),
            ],
        ),
        compiler_params=pltpu.CompilerParams(vmem_limit_bytes=24 * 2**20),
        cost_estimate=cost(flops, times * 1_000_000),
        name="weights",
    )(order, active, far_time, own_time, far_cols, own_cols, m_cols, b_cols, a, d, *picked)


def products(field_ref, u_refs, slot, first):
    _, rows, per_row, size, _ = field_ref.shape
    chunk = min(size, 32)
    fold = lambda x: jnp.sum(x.reshape(chunk // 8, 8, size), axis=0)
    sums = [jnp.zeros((8, size), F32) for _ in range(2 * len(u_refs))]
    for r in range(rows):
        for j in range(per_row):
            for start in range(0, size, chunk):
                at = pl.ds(start, chunk)
                real = field_ref[0, r, j, at].astype(F32)
                imag = field_ref[1, r, j, at].astype(F32)
                for s, u_ref in enumerate(u_refs):
                    u_real, u_imag = u_ref[slot, first + r, j, 0, at], u_ref[slot, first + r, j, 1, at]
                    sums[2 * s] += fold(real * u_real - imag * u_imag)
                    sums[2 * s + 1] += fold(real * u_imag + imag * u_real)
    return sums


def inner_kernel(slot, first, field_ref, u0_ref, u1_ref, *refs):
    *before, out_ref = refs
    for at, value in enumerate(products(field_ref, (u0_ref, u1_ref), slot, first)):
        out_ref[at] = value + before[0][at] if before else value


def inner(slot, first, field, u0, u1, *before):
    return pl.pallas_call(
        lambda *refs: inner_kernel(slot, first, *refs),
        out_shape=jax.ShapeDtypeStruct((4, 8, field.shape[-1]), F32),
        in_specs=[VMEM] * (3 + len(before)),
        out_specs=VMEM,
        cost_estimate=cost(4_000_000, 4_000_000),
        compiler_params=pltpu.CompilerParams(vmem_limit_bytes=24 * 2**20),
        name="inner",
    )(field, u0, u1, *before)


def stage_kernel(slot, u0_ref, u1_ref, out0_ref, out1_ref, sems):
    copies = [
        pltpu.make_async_copy(u_ref.at[slot, r], out_ref.at[0, r], sems.at[s, r])
        for s, (u_ref, out_ref) in enumerate(((u0_ref, out0_ref), (u1_ref, out1_ref)))
        for r in range(u_ref.shape[1])
    ]
    for copy in copies:
        copy.start()
    for copy in copies:
        copy.wait()


def stage(slot, u0, u1):
    one = jax.ShapeDtypeStruct((1,) + u0.shape[1:], u0.dtype)
    return pl.pallas_call(
        lambda *refs: stage_kernel(slot, *refs),
        out_shape=[one, one],
        in_specs=[ANY] * 2,
        out_specs=[VMEM] * 2,
        scratch_shapes=[pltpu.SemaphoreType.DMA((2, u0.shape[1]))],
        cost_estimate=cost(0, 6_000_000),
        compiler_params=pltpu.CompilerParams(vmem_limit_bytes=24 * 2**20),
        name="stage",
    )(u0, u1)


def last_kernel(first, core_ref, order_ref, sinks_ref, *refs):
    *held, field_ref, u0_ref, u1_ref, mine_ref, theirs_ref = refs
    slots = order_ref.shape[0]
    deltas = sinks_ref.shape[0] // 2
    share = deltas // 2
    core = core_ref[0]
    sums = [[ref[at] for at in range(4)] for ref in held]
    for at, value in enumerate(products(field_ref, (u0_ref, u1_ref), 0, first)):
        sums[slots - 2][at] += value
    for out_ref, owner in ((mine_ref, core), (theirs_ref, 1 - core)):
        lines = [jnp.zeros(sums[0][0].shape, F32) for _ in range(2 * share)]
        for slot in range(slots):
            time = core * slots + order_ref[slot]
            for s in range(2):
                for k in range(share):
                    sink = sinks_ref[s * deltas + owner * share + k]
                    keep = jnp.where(sink == time, F32(1), F32(0))
                    for part in range(2):
                        lines[part * share + k] += keep * sums[slot][2 * s + part]
        table = jnp.concatenate([jnp.sum(line, axis=0, keepdims=True) for line in lines], axis=0)
        table = jnp.sum(table, axis=1, keepdims=True)
        for part in range(2):
            out_ref[part] = table[part * share : (part + 1) * share]


def last(first, core, order, sinks, sums, field, u0, u1):
    share = sinks.shape[0] // 4
    return pl.pallas_call(
        lambda *refs: last_kernel(first, *refs),
        out_shape=[jax.ShapeDtypeStruct((2, share, 1), F32)] * 2,
        in_specs=[SMEM] * 3 + [VMEM] * (len(sums) + 3),
        out_specs=[VMEM] * 2,
        cost_estimate=cost(4_000_000, 4_000_000),
        compiler_params=pltpu.CompilerParams(vmem_limit_bytes=24 * 2**20),
        name="last",
    )(core, order, sinks, *sums, field, u0, u1)


def local(fields, block_cols, sources, deltas, partner):
    assert fields.shape[0] == 1 and lax.axis_size("src") == 2
    del partner
    fields = fields[0]
    times = fields.shape[0]
    core = lax.axis_index("src").reshape(1)
    pairs = one_way_pairs(lax.axis_size("mom"))
    swap = lambda value: lax.ppermute(value, "src", [(0, 1), (1, 0)])
    to_partner = lambda value: lax.ppermute(value, "mom", pairs)
    both = ("mom", "src")
    receivers = [(2 * a + c, 2 * a + 1 - c) for _, a in pairs for c in range(2)]
    swap_received = lambda value: lax.ppermute(value, both, receivers)

    cols = block_cols.reshape(-1)
    far_cols = to_partner(cols)
    own_field = pick_source(sources, fields)
    far = [to_partner(own_field)]

    other_time = swap(sources)
    order, sinks, active, full = plan(core, sources, other_time, deltas, times)
    rows = fields.shape[2]
    half = rows // 2
    halves = [(0, half), (half, rows - half)]
    pieces = [(0, 0, rows), *[(slot, 0, rows) for slot in range(1, times - 2)]]
    pieces += [(slot, *part) for slot in (times - 2, times - 1) for part in halves]
    picked = [own_field, *pick_others(order, fields, pieces[1:])]
    *early, near_low, near_high, late_low, late_high = picked
    far += [to_partner(field) for field in early[1:]]
    near_low, near_high, far[0] = lax.optimization_barrier((near_low, near_high, far[0]))
    near = [to_partner(near_low), to_partner(near_high)]

    other_cols = swap_received(cols)
    far_other_cols = swap_received(far_cols)
    other_field = swap_received(own_field)
    far_other = swap_received(far[0])
    u0 = weights(
        80_000_000_000,
        0,
        pieces,
        order,
        active,
        sources,
        sources,
        far_cols,
        cols,
        far_cols,
        cols,
        far[0],
        own_field,
        picked,
    )
    u1 = weights(
        2_000_000_000,
        1,
        pieces,
        order,
        active,
        other_time,
        other_time,
        far_other_cols,
        other_cols,
        far_cols,
        cols,
        far_other,
        other_field,
        picked,
    )
    sums = [inner(slot, 0, field, u0, u1) for slot, field in enumerate(far)]


    def with_slot(cores):
        routes = [(2 * a + c, 2 * b + c) for a, b in pairs for c in cores]

        def branch(low, high, u0, u1):
            low, high = lax.ppermute(low, both, routes), lax.ppermute(high, both, routes)
            before = inner(times - 1, 0, low, u0, u1)
            return inner(times - 1, half, high, u0, u1, before), *stage(times - 2, u0, u1)

        return branch

    def without_slot(low, high, u0, u1):
        return jnp.zeros(sums[0].shape, F32), *stage(times - 2, u0, u1)

    branches = [without_slot, with_slot([0]), with_slot([1]), with_slot([0, 1])]
    late_low, late_high, *sums = lax.optimization_barrier((late_low, late_high, *sums))
    late_sums, staged0, staged1 = lax.switch(full[0], branches, late_low, late_high, u0, u1)
    sums += [inner(0, 0, near[0], staged0, staged1), late_sums]
    mine, theirs = last(half, core, order, sinks, sums, near[1], staged0, staged1)

    total = mine + swap(theirs)
    back = [(2 * a + c, 2 * b + c) for b, a in pairs for c in range(2)]
    return total + lax.ppermute(total, both, back)


def solution(mesh):
    in_specs = (
        P(("ens", "mom"), "src", None, None, None, None, None),
        P(("ens", "mom"), "src", None, None),
        P("src"),
        P(),
        P("mom"),
    )
    out_specs = P(None, "src", ("ens", "mom"))
    return jax.shard_map(local, mesh=mesh, in_specs=in_specs, out_specs=out_specs, check_vma=False)
```

```python
import jax
import jax.numpy as jnp
from jax import lax
from jax.experimental import pallas as pl
from jax.experimental.pallas import tpu as pltpu
from jax.sharding import PartitionSpec as P

F32 = jnp.float32
BF16 = jnp.bfloat16
I32 = jnp.int32
SMEM = pl.BlockSpec(memory_space=pltpu.SMEM)
VMEM = pl.BlockSpec(memory_space=pltpu.VMEM)
ANY = pl.BlockSpec(memory_space=pl.ANY)


def one_way_pairs(count):
    half = count // 2
    outer = half // 2
    return [(g + half, g) if g < outer else (g, g + half) for g in range(half)]


def cost(flops, size):
    return pl.CostEstimate(flops=flops, bytes_accessed=size, transcendentals=0)


def pick_source_kernel(source_ref, fields_ref, out_ref, sems):
    time = lax.rem(source_ref[0], I32(fields_ref.shape[0]))
    copies = [
        pltpu.make_async_copy(fields_ref.at[time, part, r], out_ref.at[part, r], sems.at[part, r])
        for part in range(fields_ref.shape[1])
        for r in range(fields_ref.shape[2])
    ]
    for copy in copies:
        copy.start()
    for copy in copies:
        copy.wait()


def pick_source(source, fields):
    return pl.pallas_call(
        pick_source_kernel,
        out_shape=jax.ShapeDtypeStruct(fields.shape[1:], fields.dtype),
        in_specs=[SMEM, ANY],
        out_specs=VMEM,
        scratch_shapes=[pltpu.SemaphoreType.DMA(fields.shape[1:3])],
        cost_estimate=cost(0, 1_600_000),
        compiler_params=pltpu.CompilerParams(vmem_limit_bytes=52 * 2**20),
        name="pick_source",
    )(source, fields)


def pick_kernel(pieces, order_ref, fields_ref, *refs):
    *outs, sems = refs
    copies = [
        pltpu.make_async_copy(
            fields_ref.at[order_ref[slot], part, pl.ds(first, rows)], out.at[part], sems.at[at, part]
        )
        for at, ((slot, first, rows), out) in enumerate(zip(pieces, outs))
        for part in range(2)
    ]
    for copy in copies:
        copy.start()
    for copy in copies:
        copy.wait()


def pick_others(order, fields, pieces):
    return pl.pallas_call(
        lambda *refs: pick_kernel(pieces, *refs),
        out_shape=[
            jax.ShapeDtypeStruct((2, rows) + fields.shape[3:], fields.dtype) for _, _, rows in pieces
        ],
        in_specs=[SMEM, ANY],
        out_specs=[VMEM] * len(pieces),
        scratch_shapes=[pltpu.SemaphoreType.DMA((len(pieces), 2))],
        cost_estimate=cost(0, 5_000_000),
        compiler_params=pltpu.CompilerParams(vmem_limit_bytes=51 * 2**20),
        name="pick_others",
    )(order, fields)


def plan_kernel(core_ref, own_ref, other_ref, deltas_ref, order_ref, active_ref, full_ref, masks_ref):
    times = order_ref.shape[0]
    deltas = deltas_ref.shape[0]
    sinks = []
    for s, ref in enumerate((own_ref, other_ref)):
        for k in range(deltas):
            sinks.append(lax.rem(ref[0] + deltas_ref[k], I32(2 * times)))
    base = core_ref[0] * times
    first = own_ref[0] - base
    keys = []
    for t in range(times):
        needed = sinks[0] == base + t
        for sink in sinks[1:]:
            needed = needed | (sink == base + t)
        key = jnp.where(needed, I32(t), I32(times + t))
        keys.append(jnp.where(first == t, I32(-1), key))
    for t in range(times):
        rank = I32(0)
        for other in range(times):
            if other != t:
                rank += (keys[other] < keys[t]).astype(I32)
        order_ref[rank] = I32(t)
        for s in range(2):
            active = sinks[s * deltas] == base + t
            for k in range(1, deltas):
                active = active | (sinks[s * deltas + k] == base + t)
            active_ref[s * times + rank] = active.astype(I32)
    full = I32(0)
    for c in range(2):
        count = I32(0)
        for t in range(times):
            needed = (own_ref[0] == c * times + t) | (other_ref[0] == c * times + t)
            for sink in sinks:
                needed = needed | (sink == c * times + t)
            count += needed.astype(I32)
        full += jnp.where(count == times, I32(1 << c), I32(0))
    full_ref[0] = full
    for slot in range(times):
        time = base + order_ref[slot]
        for s in range(2):
            for k in range(deltas):
                own_first = sinks[s * deltas + (k + deltas // 2) % deltas]
                sink = jnp.where(core_ref[0] == 0, sinks[s * deltas + k], own_first)
                row = jnp.full((1, masks_ref.shape[2]), jnp.where(sink == time, F32(1), F32(0)))
                masks_ref[slot, s * deltas + k : s * deltas + k + 1] = row


def plan(core, own, other, deltas, times):
    return pl.pallas_call(
        plan_kernel,
        out_shape=[
            jax.ShapeDtypeStruct((times,), I32),
            jax.ShapeDtypeStruct((2 * times,), I32),
            jax.ShapeDtypeStruct((1,), I32),
            jax.ShapeDtypeStruct((times, 2 * deltas.shape[0], 128), F32),
        ],
        in_specs=[SMEM] * 4,
        out_specs=[SMEM] * 3 + [VMEM],
        cost_estimate=cost(0, 1000),
        name="plan",
    )(core, own, other, deltas)


def weights_kernel(s, pieces, order_ref, active_ref, *refs):
    far_ref, own_ref, far_cols, own_cols, m_cols, b_cols, a_ref, d_ref, *refs = refs
    *b_refs, u_ref, la, ld, bs, yn, held, sems = refs
    slot = pl.program_id(0)
    rows, per_row, size = a_ref.shape[1], a_ref.shape[2], a_ref.shape[3]
    times = order_ref.shape[0]
    step = rows * per_row
    base = order_ref[slot] * step
    a_base = lax.rem(far_ref[0], I32(times)) * step
    d_base = lax.rem(own_ref[0], I32(times)) * step
    lo, hi = pl.ds(0, size), pl.ds(size, size)

    b_copies = [[] for _ in range(times)]
    for at, ((piece_slot, first, count), b_ref) in enumerate(zip(pieces, b_refs)):
        for part in range(2):
            to = held.at[piece_slot % 2, part, pl.ds(first, count)]
            b_copies[piece_slot].append(pltpu.make_async_copy(b_ref.at[part], to, sems.at[at, part]))

    @pl.when(slot == 0)
    def _():
        for copy in b_copies[0]:
            copy.start()
        for r in range(rows):
            for j in range(per_row):
                real, imag = a_ref[0, r, j], a_ref[1, r, j]
                la[r, j, lo, lo] = real
                la[r, j, lo, hi] = -imag
                la[r, j, hi, lo] = imag
                la[r, j, hi, hi] = real
                real, imag = d_ref[0, r, j].T, d_ref[1, r, j].T
                ld[r, j, lo, lo] = real
                ld[r, j, lo, hi] = -imag
                ld[r, j, hi, lo] = imag
                ld[r, j, hi, hi] = real

    for at in range(times):

        @pl.when(slot == at)
        def _():
            for copy in b_copies[at + 1] if at + 1 < times else []:
                copy.start()
            for copy in b_copies[at]:
                copy.wait()

    @pl.when(active_ref[s * times + slot] == 0)
    def _():
        u_ref[...] = jnp.zeros_like(u_ref)

    @pl.when(active_ref[s * times + slot] != 0)
    def _():
        for r in range(rows):
            for j in range(per_row):
                bs[r, lo, pl.ds(j * size, size)] = held[slot % 2, 0, r, j]
                bs[r, hi, pl.ds(j * size, size)] = held[slot % 2, 1, r, j]

        yn[...] = jnp.zeros_like(yn)
        for r in range(rows):
            inners = [far_cols[a_base + r * per_row + j] for j in range(per_row)]
            parts = [
                jnp.dot(la[r, j], bs[inners[j]], preferred_element_type=F32) for j in range(per_row)
            ]
            pieces = []
            for j in range(per_row):
                for k in range(per_row):
                    col = b_cols[base + inners[j] * per_row + k]
                    pieces.append((j, col, parts[j][:, k * size : (k + 1) * size]))
            for at in reversed(range(len(pieces))):
                j, col, value = pieces[at]
                for other_j, other_col, other in pieces:
                    if other_j > j:
                        value = value + jnp.where(other_col == col, 1.0, 0.0) * other
                yn[col, pl.ds(r * size, size), lo] = value[:size].astype(BF16)
                yn[col, pl.ds(r * size, size), hi] = value[size:].astype(BF16)

        trace_real = jnp.zeros((size, size), F32)
        trace_imag = jnp.zeros((size, size), F32)
        for r in range(rows):
            trace_real += yn[r, pl.ds(r * size, size), lo].astype(F32)
            trace_imag += yn[r, pl.ds(r * size, size), hi].astype(F32)
        diagonal = lax.broadcasted_iota(I32, (size, size), 0) == lax.broadcasted_iota(I32, (size, size), 1)
        trace_real = jnp.sum(jnp.where(diagonal, trace_real, 0.0), axis=(0, 1), keepdims=True)
        trace_imag = jnp.sum(jnp.where(diagonal, trace_imag, 0.0), axis=(0, 1), keepdims=True)

        for r in range(rows):
            for j in range(per_row):
                col = m_cols[base + r * per_row + j]
                pick = I32(0)
                keep = F32(0)
                for k in range(per_row):
                    hit = own_cols[d_base + col * per_row + k] == r
                    pick = jnp.where(hit, I32(k), pick)
                    keep = jnp.where(hit, F32(1), keep)
                real = ld[col, pick, lo, lo].astype(F32)
                imag = ld[col, pick, hi, lo].astype(F32)
                weight_real, weight_imag = trace_real * keep, trace_imag * keep
                u_ref[0, r, j, 0] = weight_real * real - weight_imag * imag
                u_ref[0, r, j, 1] = weight_real * imag + weight_imag * real

        for i in range(rows):
            for j in range(per_row):
                r = own_cols[d_base + i * per_row + j]
                met = [m_cols[base + r * per_row + k] for k in range(per_row)]
                right = jnp.concatenate(
                    [yn[i, pl.ds(pl.multiple_of(col * size, size), size)] for col in met], axis=0
                )
                part = lax.dot_general(
                    ld[i, j], right, (((1,), (1,)), ((), ())), preferred_element_type=F32
                )
                for k in range(per_row):
                    u_ref[0, r, k, 0] -= part[:size, k * size : (k + 1) * size]
                    u_ref[0, r, k, 1] -= part[size:, k * size : (k + 1) * size]


def weights(flops, s, pieces, order, active, far_time, own_time, far_cols, own_cols, m_cols, b_cols, a, d, picked):
    times = order.shape[0]
    _, rows, per_row, size, _ = a.shape
    whole = lambda slot, *_: (0, 0, 0, 0, 0)
    return pl.pallas_call(
        lambda *refs: weights_kernel(s, pieces, *refs),
        out_shape=jax.ShapeDtypeStruct((times, rows, per_row, 2, size, size), F32),
        grid_spec=pltpu.PrefetchScalarGridSpec(
            num_scalar_prefetch=8,
            grid=(times,),
            in_specs=[
                pl.BlockSpec(a.shape, whole),
                pl.BlockSpec(a.shape, whole),
                *[ANY] * len(picked),
            ],
            out_specs=pl.BlockSpec(
                (1, rows, per_row, 2, size, size), lambda slot, *_: (slot, 0, 0, 0, 0, 0)
            ),
            scratch_shapes=[
                pltpu.VMEM((rows, per_row, 2 * size, 2 * size), BF16),
                pltpu.VMEM((rows, per_row, 2 * size, 2 * size), BF16),
                pltpu.VMEM((rows, 2 * size, per_row * size), BF16),
                pltpu.VMEM((rows, rows * size, 2 * size), BF16),
                pltpu.VMEM((2,) + a.shape, a.dtype),
                pltpu.SemaphoreType.DMA((len(picked), 2)),
            ],
        ),
        compiler_params=pltpu.CompilerParams(vmem_limit_bytes=24 * 2**20),
        cost_estimate=cost(flops, times * 1_000_000),
        name="weights",
    )(order, active, far_time, own_time, far_cols, own_cols, m_cols, b_cols, a, d, *picked)


def products(field_ref, u_refs, slot, first):
    _, rows, per_row, size, _ = field_ref.shape
    chunk = min(size, 32)
    fold = lambda x: jnp.sum(x.reshape(chunk // 8, 8, size), axis=0)
    sums = [jnp.zeros((8, size), F32) for _ in range(2 * len(u_refs))]
    for r in range(rows):
        for j in range(per_row):
            for start in range(0, size, chunk):
                at = pl.ds(start, chunk)
                real = field_ref[0, r, j, at].astype(F32)
                imag = field_ref[1, r, j, at].astype(F32)
                for s, u_ref in enumerate(u_refs):
                    u_real, u_imag = u_ref[slot, first + r, j, 0, at], u_ref[slot, first + r, j, 1, at]
                    sums[2 * s] += fold(real * u_real - imag * u_imag)
                    sums[2 * s + 1] += fold(real * u_imag + imag * u_real)
    return sums


def add_lines(slot, first, field_ref, u0_ref, u1_ref, masks_ref, before_ref):
    sums = products(field_ref, (u0_ref, u1_ref), slot, first)
    deltas = masks_ref.shape[1] // 2
    lines = []
    for part in range(2):
        for k in range(deltas):
            line = before_ref[part * deltas + k] if before_ref is not None else 0.0
            for s in range(2):
                at = s * deltas + k
                line = line + masks_ref[slot, at : at + 1] * sums[2 * s + part]
            lines.append(line)
    return lines


def inner_kernel(slot, first, field_ref, u0_ref, u1_ref, masks_ref, *refs):
    *before, out_ref = refs
    lines = add_lines(slot, first, field_ref, u0_ref, u1_ref, masks_ref, before[0] if before else None)
    for at, line in enumerate(lines):
        out_ref[at] = line


def inner(slot, first, field, u0, u1, masks, *before):
    return pl.pallas_call(
        lambda *refs: inner_kernel(slot, first, *refs),
        out_shape=jax.ShapeDtypeStruct((masks.shape[1], 8, field.shape[-1]), F32),
        in_specs=[VMEM] * (4 + len(before)),
        out_specs=VMEM,
        cost_estimate=cost(4_000_000, 4_000_000),
        compiler_params=pltpu.CompilerParams(vmem_limit_bytes=24 * 2**20),
        name="inner",
    )(field, u0, u1, masks, *before)


def stage_kernel(slot, u0_ref, u1_ref, masks_ref, out0_ref, out1_ref, out_masks_ref, sems, masks_sem):
    copies = [
        pltpu.make_async_copy(u_ref.at[slot, r], out_ref.at[0, r], sems.at[s, r])
        for s, (u_ref, out_ref) in enumerate(((u0_ref, out0_ref), (u1_ref, out1_ref)))
        for r in range(u_ref.shape[1])
    ]
    copies.append(pltpu.make_async_copy(masks_ref.at[slot], out_masks_ref.at[0], masks_sem))
    for copy in copies:
        copy.start()
    for copy in copies:
        copy.wait()


def stage(slot, u0, u1, masks):
    one = lambda value: jax.ShapeDtypeStruct((1,) + value.shape[1:], value.dtype)
    return pl.pallas_call(
        lambda *refs: stage_kernel(slot, *refs),
        out_shape=[one(u0), one(u1), one(masks)],
        in_specs=[ANY] * 3,
        out_specs=[VMEM] * 3,
        scratch_shapes=[pltpu.SemaphoreType.DMA((2, u0.shape[1])), pltpu.SemaphoreType.DMA],
        cost_estimate=cost(0, 6_000_000),
        compiler_params=pltpu.CompilerParams(vmem_limit_bytes=24 * 2**20),
        name="stage",
    )(u0, u1, masks)


def last_kernel(field_ref, u0_ref, u1_ref, masks_ref, before_ref, mine_ref, theirs_ref):
    lines = add_lines(0, 0, field_ref, u0_ref, u1_ref, masks_ref, before_ref)
    table = jnp.concatenate([jnp.sum(line, axis=0, keepdims=True) for line in lines], axis=0)
    table = jnp.sum(table, axis=1, keepdims=True)
    share = mine_ref.shape[1]
    for part in range(2):
        at = part * 2 * share
        mine_ref[part] = table[at : at + share]
        theirs_ref[part] = table[at + share : at + 2 * share]


def last(field, u0, u1, masks, lines):
    share = masks.shape[1] // 4
    return pl.pallas_call(
        last_kernel,
        out_shape=[jax.ShapeDtypeStruct((2, share, 1), F32)] * 2,
        in_specs=[VMEM] * 5,
        out_specs=[VMEM] * 2,
        cost_estimate=cost(4_000_000, 4_000_000),
        compiler_params=pltpu.CompilerParams(vmem_limit_bytes=24 * 2**20),
        name="last",
    )(field, u0, u1, masks, lines)


def local(fields, block_cols, sources, deltas, partner):
    assert fields.shape[0] == 1 and lax.axis_size("src") == 2
    del partner
    fields = fields[0]
    times = fields.shape[0]
    core = lax.axis_index("src").reshape(1)
    pairs = one_way_pairs(lax.axis_size("mom"))
    swap = lambda value: lax.ppermute(value, "src", [(0, 1), (1, 0)])
    to_partner = lambda value: lax.ppermute(value, "mom", pairs)

    cols = block_cols.reshape(-1)
    far_cols = to_partner(cols)
    own_field = pick_source(sources, fields)
    far = [to_partner(own_field)]

    other_time = swap(sources)
    order, active, full, masks = plan(core, sources, other_time, deltas, times)
    rows = fields.shape[2]
    half = rows // 2
    pieces = [(slot, 0, rows) for slot in range(times - 1)]
    pieces += [(times - 1, 0, half), (times - 1, half, rows - half)]
    picked = [own_field, *pick_others(order, fields, pieces[1:])]
    *early, near, late_low, late_high = picked
    far += [to_partner(field) for field in early[1:]]
    near, far[0] = lax.optimization_barrier((near, far[0]))
    near = to_partner(near)

    other_cols = swap(cols)
    far_other_cols = swap(far_cols)
    other_field = swap(own_field)
    far_other = swap(far[0])
    u0 = weights(
        80_000_000_000,
        0,
        pieces,
        order,
        active,
        sources,
        sources,
        far_cols,
        cols,
        far_cols,
        cols,
        far[0],
        own_field,
        picked,
    )
    u1 = weights(
        2_000_000_000,
        1,
        pieces,
        order,
        active,
        other_time,
        other_time,
        far_other_cols,
        other_cols,
        far_cols,
        cols,
        far_other,
        other_field,
        picked,
    )
    lines = inner(0, 0, far[0], u0, u1, masks)
    for slot, field in enumerate(far[1:], 1):
        lines = inner(slot, 0, field, u0, u1, masks, lines)

    both = ("mom", "src")

    def with_slot(cores):
        routes = [(2 * a + c, 2 * b + c) for a, b in pairs for c in cores]

        def branch(low, high, u0, u1, masks, lines):
            low, high = lax.ppermute(low, both, routes), lax.ppermute(high, both, routes)
            lines = inner(times - 1, 0, low, u0, u1, masks, lines)
            return inner(times - 1, half, high, u0, u1, masks, lines), *stage(times - 2, u0, u1, masks)

        return branch

    def without_slot(low, high, u0, u1, masks, lines):
        return lines, *stage(times - 2, u0, u1, masks)

    branches = [without_slot, with_slot([0]), with_slot([1]), with_slot([0, 1])]
    late_low, late_high, lines = lax.optimization_barrier((late_low, late_high, lines))
    lines, *staged = lax.switch(full[0], branches, late_low, late_high, u0, u1, masks, lines)
    mine, theirs = last(near, *staged, lines)

    total = mine + swap(theirs)
    back = [(2 * a + c, 2 * b + c) for b, a in pairs for c in range(2)]
    return total + lax.ppermute(total, both, back)


def solution(mesh):
    in_specs = (
        P(("ens", "mom"), "src", None, None, None, None, None),
        P(("ens", "mom"), "src", None, None),
        P("src"),
        P(),
        P("mom"),
    )
    out_specs = P(None, "src", ("ens", "mom"))
    return jax.shard_map(local, mesh=mesh, in_specs=in_specs, out_specs=out_specs, check_vma=False)
```

```python
import jax
import jax.numpy as jnp
from jax import lax
from jax.experimental import pallas as pl
from jax.experimental.pallas import tpu as pltpu
from jax.sharding import PartitionSpec as P

F32 = jnp.float32
BF16 = jnp.bfloat16
I32 = jnp.int32
SMEM = pl.BlockSpec(memory_space=pltpu.SMEM)
VMEM = pl.BlockSpec(memory_space=pltpu.VMEM)
ANY = pl.BlockSpec(memory_space=pl.ANY)


def one_way_pairs(count):
    half = count // 2
    outer = half // 2
    return [(g + half, g) if g < outer else (g, g + half) for g in range(half)]


def cost(flops, size):
    return pl.CostEstimate(flops=flops, bytes_accessed=size, transcendentals=0)


def pick_source_kernel(source_ref, fields_ref, out_ref, sems):
    time = lax.rem(source_ref[0], I32(fields_ref.shape[0]))
    copies = [
        pltpu.make_async_copy(fields_ref.at[time, part, r], out_ref.at[part, r], sems.at[part, r])
        for part in range(fields_ref.shape[1])
        for r in range(fields_ref.shape[2])
    ]
    for copy in copies:
        copy.start()
    for copy in copies:
        copy.wait()


def pick_source(source, fields):
    return pl.pallas_call(
        pick_source_kernel,
        out_shape=jax.ShapeDtypeStruct(fields.shape[1:], fields.dtype),
        in_specs=[SMEM, ANY],
        out_specs=VMEM,
        scratch_shapes=[pltpu.SemaphoreType.DMA(fields.shape[1:3])],
        cost_estimate=cost(0, 1_600_000),
        compiler_params=pltpu.CompilerParams(vmem_limit_bytes=52 * 2**20),
        name="pick_source",
    )(source, fields)


def pick_kernel(pieces, order_ref, fields_ref, *refs):
    *outs, sems = refs
    copies = [
        pltpu.make_async_copy(
            fields_ref.at[order_ref[slot], part, pl.ds(first, rows)], out.at[part], sems.at[at, part]
        )
        for at, ((slot, first, rows), out) in enumerate(zip(pieces, outs))
        for part in range(2)
    ]
    for copy in copies:
        copy.start()
    for copy in copies:
        copy.wait()


def pick_others(order, fields, pieces):
    return pl.pallas_call(
        lambda *refs: pick_kernel(pieces, *refs),
        out_shape=[
            jax.ShapeDtypeStruct((2, rows) + fields.shape[3:], fields.dtype) for _, _, rows in pieces
        ],
        in_specs=[SMEM, ANY],
        out_specs=[VMEM] * len(pieces),
        scratch_shapes=[pltpu.SemaphoreType.DMA((len(pieces), 2))],
        cost_estimate=cost(0, 5_000_000),
        compiler_params=pltpu.CompilerParams(vmem_limit_bytes=51 * 2**20),
        name="pick_others",
    )(order, fields)


def plan_kernel(core_ref, own_ref, other_ref, deltas_ref, order_ref, active_ref, full_ref, masks_ref):
    times = order_ref.shape[0]
    deltas = deltas_ref.shape[0]
    sinks = []
    for s, ref in enumerate((own_ref, other_ref)):
        for k in range(deltas):
            sinks.append(lax.rem(ref[0] + deltas_ref[k], I32(2 * times)))
    base = core_ref[0] * times
    first = own_ref[0] - base
    keys = []
    for t in range(times):
        needed = sinks[0] == base + t
        for sink in sinks[1:]:
            needed = needed | (sink == base + t)
        key = jnp.where(needed, I32(t), I32(times + t))
        keys.append(jnp.where(first == t, I32(-1), key))
    for t in range(times):
        rank = I32(0)
        for other in range(times):
            if other != t:
                rank += (keys[other] < keys[t]).astype(I32)
        order_ref[rank] = I32(t)
        for s in range(2):
            active = sinks[s * deltas] == base + t
            for k in range(1, deltas):
                active = active | (sinks[s * deltas + k] == base + t)
            active_ref[s * times + rank] = active.astype(I32)
    full = I32(0)
    for c in range(2):
        count = I32(0)
        for t in range(times):
            needed = (own_ref[0] == c * times + t) | (other_ref[0] == c * times + t)
            for sink in sinks:
                needed = needed | (sink == c * times + t)
            count += needed.astype(I32)
        full += jnp.where(count == times, I32(1 << c), I32(0))
    full_ref[0] = full
    for slot in range(times):
        time = base + order_ref[slot]
        for s in range(2):
            for k in range(deltas):
                own_first = sinks[s * deltas + (k + deltas // 2) % deltas]
                sink = jnp.where(core_ref[0] == 0, sinks[s * deltas + k], own_first)
                row = jnp.full((1, masks_ref.shape[2]), jnp.where(sink == time, F32(1), F32(0)))
                masks_ref[slot, s * deltas + k : s * deltas + k + 1] = row


def plan(core, own, other, deltas, times):
    return pl.pallas_call(
        plan_kernel,
        out_shape=[
            jax.ShapeDtypeStruct((times,), I32),
            jax.ShapeDtypeStruct((2 * times,), I32),
            jax.ShapeDtypeStruct((1,), I32),
            jax.ShapeDtypeStruct((times, 2 * deltas.shape[0], 128), F32),
        ],
        in_specs=[SMEM] * 4,
        out_specs=[SMEM] * 3 + [VMEM],
        cost_estimate=cost(0, 1000),
        name="plan",
    )(core, own, other, deltas)


def weights_kernel(s, pieces, order_ref, active_ref, *refs):
    far_ref, own_ref, far_cols, own_cols, m_cols, b_cols, a_ref, d_ref, *refs = refs
    *b_refs, u_ref, la, ld, bs, yn, held, sems = refs
    slot = pl.program_id(0)
    rows, per_row, size = a_ref.shape[1], a_ref.shape[2], a_ref.shape[3]
    times = order_ref.shape[0]
    step = rows * per_row
    base = order_ref[slot] * step
    a_base = lax.rem(far_ref[0], I32(times)) * step
    d_base = lax.rem(own_ref[0], I32(times)) * step
    lo, hi = pl.ds(0, size), pl.ds(size, size)

    b_copies = [[] for _ in range(times)]
    for at, ((piece_slot, first, count), b_ref) in enumerate(zip(pieces, b_refs)):
        for part in range(2):
            to = held.at[piece_slot % 2, part, pl.ds(first, count)]
            b_copies[piece_slot].append(pltpu.make_async_copy(b_ref.at[part], to, sems.at[at, part]))

    @pl.when(slot == 0)
    def _():
        for copy in b_copies[0]:
            copy.start()
        for r in range(rows):
            for j in range(per_row):
                real, imag = a_ref[0, r, j], a_ref[1, r, j]
                la[r, j, lo, lo] = real
                la[r, j, lo, hi] = -imag
                la[r, j, hi, lo] = imag
                la[r, j, hi, hi] = real
                real, imag = d_ref[0, r, j].T, d_ref[1, r, j].T
                ld[r, j, lo, lo] = real
                ld[r, j, lo, hi] = -imag
                ld[r, j, hi, lo] = imag
                ld[r, j, hi, hi] = real

    for at in range(times):

        @pl.when(slot == at)
        def _():
            for copy in b_copies[at + 1] if at + 1 < times else []:
                copy.start()
            for copy in b_copies[at]:
                copy.wait()

    @pl.when(active_ref[s * times + slot] == 0)
    def _():
        u_ref[...] = jnp.zeros_like(u_ref)

    @pl.when(active_ref[s * times + slot] != 0)
    def _():
        for r in range(rows):
            for j in range(per_row):
                bs[r, lo, pl.ds(j * size, size)] = held[slot % 2, 0, r, j]
                bs[r, hi, pl.ds(j * size, size)] = held[slot % 2, 1, r, j]

        yn[...] = jnp.zeros_like(yn)
        for r in range(rows):
            inners = [far_cols[a_base + r * per_row + j] for j in range(per_row)]
            parts = [
                jnp.dot(la[r, j], bs[inners[j]], preferred_element_type=F32) for j in range(per_row)
            ]
            pieces = []
            for j in range(per_row):
                for k in range(per_row):
                    col = b_cols[base + inners[j] * per_row + k]
                    pieces.append((j, col, parts[j][:, k * size : (k + 1) * size]))
            for at in reversed(range(len(pieces))):
                j, col, value = pieces[at]
                for other_j, other_col, other in pieces:
                    if other_j > j:
                        value = value + jnp.where(other_col == col, 1.0, 0.0) * other
                yn[col, pl.ds(r * size, size), lo] = value[:size].astype(BF16)
                yn[col, pl.ds(r * size, size), hi] = value[size:].astype(BF16)

        trace_real = jnp.zeros((size, size), F32)
        trace_imag = jnp.zeros((size, size), F32)
        for r in range(rows):
            trace_real += yn[r, pl.ds(r * size, size), lo].astype(F32)
            trace_imag += yn[r, pl.ds(r * size, size), hi].astype(F32)
        diagonal = lax.broadcasted_iota(I32, (size, size), 0) == lax.broadcasted_iota(I32, (size, size), 1)
        trace_real = jnp.sum(jnp.where(diagonal, trace_real, 0.0), axis=(0, 1), keepdims=True)
        trace_imag = jnp.sum(jnp.where(diagonal, trace_imag, 0.0), axis=(0, 1), keepdims=True)

        for r in range(rows):
            for j in range(per_row):
                col = m_cols[base + r * per_row + j]
                pick = I32(0)
                keep = F32(0)
                for k in range(per_row):
                    hit = own_cols[d_base + col * per_row + k] == r
                    pick = jnp.where(hit, I32(k), pick)
                    keep = jnp.where(hit, F32(1), keep)
                real = ld[col, pick, lo, lo].astype(F32)
                imag = ld[col, pick, hi, lo].astype(F32)
                weight_real, weight_imag = trace_real * keep, trace_imag * keep
                u_ref[0, r, j, 0] = weight_real * real - weight_imag * imag
                u_ref[0, r, j, 1] = weight_real * imag + weight_imag * real

        for i in range(rows):
            for j in range(per_row):
                r = own_cols[d_base + i * per_row + j]
                met = [m_cols[base + r * per_row + k] for k in range(per_row)]
                right = jnp.concatenate(
                    [yn[i, pl.ds(pl.multiple_of(col * size, size), size)] for col in met], axis=0
                )
                part = lax.dot_general(
                    ld[i, j], right, (((1,), (1,)), ((), ())), preferred_element_type=F32
                )
                for k in range(per_row):
                    u_ref[0, r, k, 0] -= part[:size, k * size : (k + 1) * size]
                    u_ref[0, r, k, 1] -= part[size:, k * size : (k + 1) * size]


def weights(flops, s, pieces, order, active, far_time, own_time, far_cols, own_cols, m_cols, b_cols, a, d, picked):
    times = order.shape[0]
    _, rows, per_row, size, _ = a.shape
    whole = lambda slot, *_: (0, 0, 0, 0, 0)
    return pl.pallas_call(
        lambda *refs: weights_kernel(s, pieces, *refs),
        out_shape=jax.ShapeDtypeStruct((times, rows, per_row, 2, size, size), F32),
        grid_spec=pltpu.PrefetchScalarGridSpec(
            num_scalar_prefetch=8,
            grid=(times,),
            in_specs=[
                pl.BlockSpec(a.shape, whole),
                pl.BlockSpec(a.shape, whole),
                *[ANY] * len(picked),
            ],
            out_specs=pl.BlockSpec(
                (1, rows, per_row, 2, size, size), lambda slot, *_: (slot, 0, 0, 0, 0, 0)
            ),
            scratch_shapes=[
                pltpu.VMEM((rows, per_row, 2 * size, 2 * size), BF16),
                pltpu.VMEM((rows, per_row, 2 * size, 2 * size), BF16),
                pltpu.VMEM((rows, 2 * size, per_row * size), BF16),
                pltpu.VMEM((rows, rows * size, 2 * size), BF16),
                pltpu.VMEM((2,) + a.shape, a.dtype),
                pltpu.SemaphoreType.DMA((len(picked), 2)),
            ],
        ),
        compiler_params=pltpu.CompilerParams(vmem_limit_bytes=16 * 2**20),
        cost_estimate=cost(flops, times * 1_000_000),
        name="weights",
    )(order, active, far_time, own_time, far_cols, own_cols, m_cols, b_cols, a, d, *picked)


def products(field_ref, u_refs, slot, first):
    _, rows, per_row, size, _ = field_ref.shape
    chunk = min(size, 32)
    fold = lambda x: jnp.sum(x.reshape(chunk // 8, 8, size), axis=0)
    sums = [jnp.zeros((8, size), F32) for _ in range(2 * len(u_refs))]
    for r in range(rows):
        for j in range(per_row):
            for start in range(0, size, chunk):
                at = pl.ds(start, chunk)
                real = field_ref[0, r, j, at].astype(F32)
                imag = field_ref[1, r, j, at].astype(F32)
                for s, u_ref in enumerate(u_refs):
                    u_real, u_imag = u_ref[slot, first + r, j, 0, at], u_ref[slot, first + r, j, 1, at]
                    sums[2 * s] += fold(real * u_real - imag * u_imag)
                    sums[2 * s + 1] += fold(real * u_imag + imag * u_real)
    return sums


def add_lines(slot, first, field_ref, u0_ref, u1_ref, masks_ref, before_ref):
    sums = products(field_ref, (u0_ref, u1_ref), slot, first)
    deltas = masks_ref.shape[1] // 2
    lines = []
    for part in range(2):
        for k in range(deltas):
            line = before_ref[part * deltas + k] if before_ref is not None else 0.0
            for s in range(2):
                at = s * deltas + k
                line = line + masks_ref[slot, at : at + 1] * sums[2 * s + part]
            lines.append(line)
    return lines


def inner_kernel(slot, first, field_ref, u0_ref, u1_ref, masks_ref, *refs):
    *before, out_ref = refs
    lines = add_lines(slot, first, field_ref, u0_ref, u1_ref, masks_ref, before[0] if before else None)
    for at, line in enumerate(lines):
        out_ref[at] = line


def inner(slot, first, field, u0, u1, masks, *before):
    return pl.pallas_call(
        lambda *refs: inner_kernel(slot, first, *refs),
        out_shape=jax.ShapeDtypeStruct((masks.shape[1], 8, field.shape[-1]), F32),
        in_specs=[VMEM] * (4 + len(before)),
        out_specs=VMEM,
        cost_estimate=cost(4_000_000, 4_000_000),
        compiler_params=pltpu.CompilerParams(vmem_limit_bytes=16 * 2**20),
        name="inner",
    )(field, u0, u1, masks, *before)


def stage_kernel(slot, u0_ref, u1_ref, masks_ref, out0_ref, out1_ref, out_masks_ref, sems, masks_sem):
    copies = [
        pltpu.make_async_copy(u_ref.at[slot, r], out_ref.at[0, r], sems.at[s, r])
        for s, (u_ref, out_ref) in enumerate(((u0_ref, out0_ref), (u1_ref, out1_ref)))
        for r in range(u_ref.shape[1])
    ]
    copies.append(pltpu.make_async_copy(masks_ref.at[slot], out_masks_ref.at[0], masks_sem))
    for copy in copies:
        copy.start()
    for copy in copies:
        copy.wait()


def stage(slot, u0, u1, masks):
    one = lambda value: jax.ShapeDtypeStruct((1,) + value.shape[1:], value.dtype)
    return pl.pallas_call(
        lambda *refs: stage_kernel(slot, *refs),
        out_shape=[one(u0), one(u1), one(masks)],
        in_specs=[ANY] * 3,
        out_specs=[VMEM] * 3,
        scratch_shapes=[pltpu.SemaphoreType.DMA((2, u0.shape[1])), pltpu.SemaphoreType.DMA],
        cost_estimate=cost(0, 6_000_000),
        compiler_params=pltpu.CompilerParams(vmem_limit_bytes=8 * 2**20),
        name="stage",
    )(u0, u1, masks)


def last_kernel(field_ref, u0_ref, u1_ref, masks_ref, before_ref, mine_ref, theirs_ref):
    lines = add_lines(0, 0, field_ref, u0_ref, u1_ref, masks_ref, before_ref)
    table = jnp.concatenate([jnp.sum(line, axis=0, keepdims=True) for line in lines], axis=0)
    table = jnp.sum(table, axis=1, keepdims=True)
    share = mine_ref.shape[1]
    for part in range(2):
        at = part * 2 * share
        mine_ref[part] = table[at : at + share]
        theirs_ref[part] = table[at + share : at + 2 * share]


def last(field, u0, u1, masks, lines):
    share = masks.shape[1] // 4
    return pl.pallas_call(
        last_kernel,
        out_shape=[jax.ShapeDtypeStruct((2, share, 1), F32)] * 2,
        in_specs=[VMEM] * 5,
        out_specs=[VMEM] * 2,
        cost_estimate=cost(4_000_000, 4_000_000),
        compiler_params=pltpu.CompilerParams(vmem_limit_bytes=8 * 2**20),
        name="last",
    )(field, u0, u1, masks, lines)


def local(fields, block_cols, sources, deltas, partner):
    assert fields.shape[0] == 1 and lax.axis_size("src") == 2
    del partner
    fields = fields[0]
    times = fields.shape[0]
    core = lax.axis_index("src").reshape(1)
    pairs = one_way_pairs(lax.axis_size("mom"))
    swap = lambda value: lax.ppermute(value, "src", [(0, 1), (1, 0)])
    to_partner = lambda value: lax.ppermute(value, "mom", pairs)

    cols = block_cols.reshape(-1)
    far_cols = to_partner(cols)
    own_field = pick_source(sources, fields)
    far = [to_partner(own_field)]

    other_time = swap(sources)
    order, active, full, masks = plan(core, sources, other_time, deltas, times)
    rows = fields.shape[2]
    half = rows // 2
    pieces = [(slot, 0, rows) for slot in range(times - 1)]
    pieces += [(times - 1, 0, half), (times - 1, half, rows - half)]
    picked = [own_field, *pick_others(order, fields, pieces[1:])]
    *early, near, late_low, late_high = picked
    far += [to_partner(field) for field in early[1:]]
    near, far[0] = lax.optimization_barrier((near, far[0]))
    near = to_partner(near)

    other_cols = swap(cols)
    far_other_cols = swap(far_cols)
    other_field = swap(own_field)
    far_other = swap(far[0])
    u0 = weights(
        80_000_000_000,
        0,
        pieces,
        order,
        active,
        sources,
        sources,
        far_cols,
        cols,
        far_cols,
        cols,
        far[0],
        own_field,
        picked,
    )
    u1 = weights(
        2_000_000_000,
        1,
        pieces,
        order,
        active,
        other_time,
        other_time,
        far_other_cols,
        other_cols,
        far_cols,
        cols,
        far_other,
        other_field,
        picked,
    )
    lines = inner(0, 0, far[0], u0, u1, masks)
    for slot, field in enumerate(far[1:], 1):
        lines = inner(slot, 0, field, u0, u1, masks, lines)

    both = ("mom", "src")

    def with_slot(cores):
        routes = [(2 * a + c, 2 * b + c) for a, b in pairs for c in cores]

        def branch(low, high, u0, u1, masks, lines):
            low, high = lax.ppermute(low, both, routes), lax.ppermute(high, both, routes)
            lines = inner(times - 1, 0, low, u0, u1, masks, lines)
            return inner(times - 1, half, high, u0, u1, masks, lines), *stage(times - 2, u0, u1, masks)

        return branch

    def without_slot(low, high, u0, u1, masks, lines):
        return lines, *stage(times - 2, u0, u1, masks)

    branches = [without_slot, with_slot([0]), with_slot([1]), with_slot([0, 1])]
    late_low, late_high, lines = lax.optimization_barrier((late_low, late_high, lines))
    lines, *staged = lax.switch(full[0], branches, late_low, late_high, u0, u1, masks, lines)
    mine, theirs = last(near, *staged, lines)

    total = mine + swap(theirs)
    back = [(2 * a + c, 2 * b + c) for b, a in pairs for c in range(2)]
    return total + lax.ppermute(total, both, back)


def solution(mesh):
    in_specs = (
        P(("ens", "mom"), "src", None, None, None, None, None),
        P(("ens", "mom"), "src", None, None),
        P("src"),
        P(),
        P("mom"),
    )
    out_specs = P(None, "src", ("ens", "mom"))
    return jax.shard_map(local, mesh=mesh, in_specs=in_specs, out_specs=out_specs, check_vma=False)
```

```python
import jax
import jax.numpy as jnp
from jax import lax
from jax.experimental import pallas as pl
from jax.experimental.pallas import tpu as pltpu
from jax.sharding import PartitionSpec as P

F32 = jnp.float32
BF16 = jnp.bfloat16
I32 = jnp.int32
SMEM = pl.BlockSpec(memory_space=pltpu.SMEM)
VMEM = pl.BlockSpec(memory_space=pltpu.VMEM)
ANY = pl.BlockSpec(memory_space=pl.ANY)


def one_way_pairs(count):
    half = count // 2
    outer = half // 2
    return [(g + half, g) if g < outer else (g, g + half) for g in range(half)]


def cost(flops, size):
    return pl.CostEstimate(flops=flops, bytes_accessed=size, transcendentals=0)


def pick_source_kernel(source_ref, fields_ref, out_ref, sems):
    time = lax.rem(source_ref[0], I32(fields_ref.shape[0]))
    copies = [
        pltpu.make_async_copy(fields_ref.at[time, part, r], out_ref.at[part, r], sems.at[part, r])
        for part in range(fields_ref.shape[1])
        for r in range(fields_ref.shape[2])
    ]
    for copy in copies:
        copy.start()
    for copy in copies:
        copy.wait()


def pick_source(source, fields):
    return pl.pallas_call(
        pick_source_kernel,
        out_shape=jax.ShapeDtypeStruct(fields.shape[1:], fields.dtype),
        in_specs=[SMEM, ANY],
        out_specs=VMEM,
        scratch_shapes=[pltpu.SemaphoreType.DMA(fields.shape[1:3])],
        cost_estimate=cost(0, 1_600_000),
        compiler_params=pltpu.CompilerParams(vmem_limit_bytes=52 * 2**20),
        name="pick_source",
    )(source, fields)


def pick_kernel(pieces, order_ref, fields_ref, *refs):
    *outs, sems = refs
    copies = [
        pltpu.make_async_copy(
            fields_ref.at[order_ref[slot], part, pl.ds(first, rows)], out.at[part], sems.at[at, part]
        )
        for at, ((slot, first, rows), out) in enumerate(zip(pieces, outs))
        for part in range(2)
    ]
    for copy in copies:
        copy.start()
    for copy in copies:
        copy.wait()


def pick_others(order, fields, pieces):
    return pl.pallas_call(
        lambda *refs: pick_kernel(pieces, *refs),
        out_shape=[
            jax.ShapeDtypeStruct((2, rows) + fields.shape[3:], fields.dtype) for _, _, rows in pieces
        ],
        in_specs=[SMEM, ANY],
        out_specs=[VMEM] * len(pieces),
        scratch_shapes=[pltpu.SemaphoreType.DMA((len(pieces), 2))],
        cost_estimate=cost(0, 5_000_000),
        compiler_params=pltpu.CompilerParams(vmem_limit_bytes=51 * 2**20),
        name="pick_others",
    )(order, fields)


def plan_kernel(core_ref, own_ref, other_ref, deltas_ref, order_ref, active_ref, full_ref, masks_ref):
    times = order_ref.shape[0]
    deltas = deltas_ref.shape[0]
    sinks = []
    for s, ref in enumerate((own_ref, other_ref)):
        for k in range(deltas):
            sinks.append(lax.rem(ref[0] + deltas_ref[k], I32(2 * times)))
    base = core_ref[0] * times
    first = own_ref[0] - base
    keys = []
    for t in range(times):
        needed = sinks[0] == base + t
        for sink in sinks[1:]:
            needed = needed | (sink == base + t)
        key = jnp.where(needed, I32(t), I32(times + t))
        keys.append(jnp.where(first == t, I32(-1), key))
    for t in range(times):
        rank = I32(0)
        for other in range(times):
            if other != t:
                rank += (keys[other] < keys[t]).astype(I32)
        order_ref[rank] = I32(t)
        for s in range(2):
            active = sinks[s * deltas] == base + t
            for k in range(1, deltas):
                active = active | (sinks[s * deltas + k] == base + t)
            active_ref[s * times + rank] = active.astype(I32)
    full = I32(0)
    for c in range(2):
        count = I32(0)
        for t in range(times):
            needed = (own_ref[0] == c * times + t) | (other_ref[0] == c * times + t)
            for sink in sinks:
                needed = needed | (sink == c * times + t)
            count += needed.astype(I32)
        full += jnp.where(count == times, I32(1 << c), I32(0))
    full_ref[0] = full
    for slot in range(times):
        time = base + order_ref[slot]
        for s in range(2):
            for k in range(deltas):
                own_first = sinks[s * deltas + (k + deltas // 2) % deltas]
                sink = jnp.where(core_ref[0] == 0, sinks[s * deltas + k], own_first)
                row = jnp.full((1, masks_ref.shape[2]), jnp.where(sink == time, F32(1), F32(0)))
                masks_ref[slot, s * deltas + k : s * deltas + k + 1] = row


def plan(core, own, other, deltas, times):
    return pl.pallas_call(
        plan_kernel,
        out_shape=[
            jax.ShapeDtypeStruct((times,), I32),
            jax.ShapeDtypeStruct((2 * times,), I32),
            jax.ShapeDtypeStruct((1,), I32),
            jax.ShapeDtypeStruct((times, 2 * deltas.shape[0], 128), F32),
        ],
        in_specs=[SMEM] * 4,
        out_specs=[SMEM] * 3 + [VMEM],
        cost_estimate=cost(0, 1000),
        name="plan",
    )(core, own, other, deltas)


def weights_kernel(s, pieces, order_ref, active_ref, *refs):
    far_ref, own_ref, far_cols, own_cols, m_cols, b_cols, a_ref, d_ref, *refs = refs
    *b_refs, u_ref, la, ld, bs, yn, held, sems = refs
    slot = pl.program_id(0)
    rows, per_row, size = a_ref.shape[1], a_ref.shape[2], a_ref.shape[3]
    times = order_ref.shape[0]
    step = rows * per_row
    base = order_ref[slot] * step
    a_base = lax.rem(far_ref[0], I32(times)) * step
    d_base = lax.rem(own_ref[0], I32(times)) * step
    lo, hi = pl.ds(0, size), pl.ds(size, size)

    b_copies = [[] for _ in range(times)]
    for at, ((piece_slot, first, count), b_ref) in enumerate(zip(pieces, b_refs)):
        for part in range(2):
            to = held.at[piece_slot % 2, part, pl.ds(first, count)]
            b_copies[piece_slot].append(pltpu.make_async_copy(b_ref.at[part], to, sems.at[at, part]))

    @pl.when(slot == 0)
    def _():
        for copy in b_copies[0]:
            copy.start()
        for r in range(rows):
            for j in range(per_row):
                real, imag = a_ref[0, r, j], a_ref[1, r, j]
                la[r, j, lo, lo] = real
                la[r, j, lo, hi] = -imag
                la[r, j, hi, lo] = imag
                la[r, j, hi, hi] = real
                real, imag = d_ref[0, r, j].T, d_ref[1, r, j].T
                ld[r, j, lo, lo] = real
                ld[r, j, lo, hi] = -imag
                ld[r, j, hi, lo] = imag
                ld[r, j, hi, hi] = real

    for at in range(times):

        @pl.when(slot == at)
        def _():
            for copy in b_copies[at + 1] if at + 1 < times else []:
                copy.start()
            for copy in b_copies[at]:
                copy.wait()

    @pl.when(active_ref[s * times + slot] == 0)
    def _():
        u_ref[...] = jnp.zeros_like(u_ref)

    @pl.when(active_ref[s * times + slot] != 0)
    def _():
        for r in range(rows):
            for j in range(per_row):
                bs[r, lo, pl.ds(j * size, size)] = held[slot % 2, 0, r, j]
                bs[r, hi, pl.ds(j * size, size)] = held[slot % 2, 1, r, j]

        yn[...] = jnp.zeros_like(yn)
        for r in range(rows):
            inners = [far_cols[a_base + r * per_row + j] for j in range(per_row)]
            parts = [
                jnp.dot(la[r, j], bs[inners[j]], preferred_element_type=F32) for j in range(per_row)
            ]
            pieces = []
            for j in range(per_row):
                for k in range(per_row):
                    col = b_cols[base + inners[j] * per_row + k]
                    pieces.append((j, col, parts[j][:, k * size : (k + 1) * size]))
            for at in reversed(range(len(pieces))):
                j, col, value = pieces[at]
                for other_j, other_col, other in pieces:
                    if other_j > j:
                        value = value + jnp.where(other_col == col, 1.0, 0.0) * other
                yn[col, pl.ds(r * size, size), lo] = value[:size].astype(BF16)
                yn[col, pl.ds(r * size, size), hi] = value[size:].astype(BF16)

        trace_real = jnp.zeros((size, size), F32)
        trace_imag = jnp.zeros((size, size), F32)
        for r in range(rows):
            trace_real += yn[r, pl.ds(r * size, size), lo].astype(F32)
            trace_imag += yn[r, pl.ds(r * size, size), hi].astype(F32)
        diagonal = lax.broadcasted_iota(I32, (size, size), 0) == lax.broadcasted_iota(I32, (size, size), 1)
        trace_real = jnp.sum(jnp.where(diagonal, trace_real, 0.0), axis=(0, 1), keepdims=True)
        trace_imag = jnp.sum(jnp.where(diagonal, trace_imag, 0.0), axis=(0, 1), keepdims=True)

        for r in range(rows):
            for j in range(per_row):
                col = m_cols[base + r * per_row + j]
                pick = I32(0)
                keep = F32(0)
                for k in range(per_row):
                    hit = own_cols[d_base + col * per_row + k] == r
                    pick = jnp.where(hit, I32(k), pick)
                    keep = jnp.where(hit, F32(1), keep)
                real = ld[col, pick, lo, lo].astype(F32)
                imag = ld[col, pick, hi, lo].astype(F32)
                weight_real, weight_imag = trace_real * keep, trace_imag * keep
                u_ref[0, r, j, 0] = weight_real * real - weight_imag * imag
                u_ref[0, r, j, 1] = weight_real * imag + weight_imag * real

        for i in range(rows):
            for j in range(per_row):
                r = own_cols[d_base + i * per_row + j]
                met = [m_cols[base + r * per_row + k] for k in range(per_row)]
                right = jnp.concatenate(
                    [yn[i, pl.ds(pl.multiple_of(col * size, size), size)] for col in met], axis=0
                )
                part = lax.dot_general(
                    ld[i, j], right, (((1,), (1,)), ((), ())), preferred_element_type=F32
                )
                for k in range(per_row):
                    u_ref[0, r, k, 0] -= part[:size, k * size : (k + 1) * size]
                    u_ref[0, r, k, 1] -= part[size:, k * size : (k + 1) * size]


def weights(flops, s, pieces, order, active, far_time, own_time, far_cols, own_cols, m_cols, b_cols, a, d, picked):
    times = order.shape[0]
    _, rows, per_row, size, _ = a.shape
    whole = lambda slot, *_: (0, 0, 0, 0, 0)
    return pl.pallas_call(
        lambda *refs: weights_kernel(s, pieces, *refs),
        out_shape=jax.ShapeDtypeStruct((times, rows, per_row, 2, size, size), F32),
        grid_spec=pltpu.PrefetchScalarGridSpec(
            num_scalar_prefetch=8,
            grid=(times,),
            in_specs=[
                pl.BlockSpec(a.shape, whole),
                pl.BlockSpec(a.shape, whole),
                *[ANY] * len(picked),
            ],
            out_specs=pl.BlockSpec(
                (1, rows, per_row, 2, size, size), lambda slot, *_: (slot, 0, 0, 0, 0, 0)
            ),
            scratch_shapes=[
                pltpu.VMEM((rows, per_row, 2 * size, 2 * size), BF16),
                pltpu.VMEM((rows, per_row, 2 * size, 2 * size), BF16),
                pltpu.VMEM((rows, 2 * size, per_row * size), BF16),
                pltpu.VMEM((rows, rows * size, 2 * size), BF16),
                pltpu.VMEM((2,) + a.shape, a.dtype),
                pltpu.SemaphoreType.DMA((len(picked), 2)),
            ],
        ),
        compiler_params=pltpu.CompilerParams(vmem_limit_bytes=16 * 2**20),
        cost_estimate=cost(flops, times * 1_000_000),
        name="weights",
    )(order, active, far_time, own_time, far_cols, own_cols, m_cols, b_cols, a, d, *picked)


def products(field_ref, u_refs, slot, first):
    _, rows, per_row, size, _ = field_ref.shape
    chunk = min(size, 32)
    fold = lambda x: jnp.sum(x.reshape(chunk // 8, 8, size), axis=0)
    sums = [jnp.zeros((8, size), F32) for _ in range(2 * len(u_refs))]
    for r in range(rows):
        for j in range(per_row):
            for start in range(0, size, chunk):
                at = pl.ds(start, chunk)
                real = field_ref[0, r, j, at].astype(F32)
                imag = field_ref[1, r, j, at].astype(F32)
                for s, u_ref in enumerate(u_refs):
                    u_real, u_imag = u_ref[slot, first + r, j, 0, at], u_ref[slot, first + r, j, 1, at]
                    sums[2 * s] += fold(real * u_real - imag * u_imag)
                    sums[2 * s + 1] += fold(real * u_imag + imag * u_real)
    return sums


def add_lines(slot, first, field_ref, u0_ref, u1_ref, masks_ref, before_ref):
    sums = products(field_ref, (u0_ref, u1_ref), slot, first)
    deltas = masks_ref.shape[1] // 2
    lines = []
    for part in range(2):
        for k in range(deltas):
            line = before_ref[part * deltas + k] if before_ref is not None else 0.0
            for s in range(2):
                at = s * deltas + k
                line = line + masks_ref[slot, at : at + 1] * sums[2 * s + part]
            lines.append(line)
    return lines


def inner_kernel(slot, first, field_ref, u0_ref, u1_ref, masks_ref, *refs):
    *before, out_ref = refs
    lines = add_lines(slot, first, field_ref, u0_ref, u1_ref, masks_ref, before[0] if before else None)
    for at, line in enumerate(lines):
        out_ref[at] = line


def inner(slot, first, field, u0, u1, masks, *before):
    return pl.pallas_call(
        lambda *refs: inner_kernel(slot, first, *refs),
        out_shape=jax.ShapeDtypeStruct((masks.shape[1], 8, field.shape[-1]), F32),
        in_specs=[VMEM] * (4 + len(before)),
        out_specs=VMEM,
        cost_estimate=cost(4_000_000, 4_000_000),
        compiler_params=pltpu.CompilerParams(vmem_limit_bytes=16 * 2**20),
        name="inner",
    )(field, u0, u1, masks, *before)


def stage_kernel(slot, u0_ref, u1_ref, masks_ref, out0_ref, out1_ref, out_masks_ref, sems, masks_sem):
    copies = [
        pltpu.make_async_copy(u_ref.at[slot, r], out_ref.at[0, r], sems.at[s, r])
        for s, (u_ref, out_ref) in enumerate(((u0_ref, out0_ref), (u1_ref, out1_ref)))
        for r in range(u_ref.shape[1])
    ]
    copies.append(pltpu.make_async_copy(masks_ref.at[slot], out_masks_ref.at[0], masks_sem))
    for copy in copies:
        copy.start()
    for copy in copies:
        copy.wait()


def stage(slot, u0, u1, masks):
    one = lambda value: jax.ShapeDtypeStruct((1,) + value.shape[1:], value.dtype)
    return pl.pallas_call(
        lambda *refs: stage_kernel(slot, *refs),
        out_shape=[one(u0), one(u1), one(masks)],
        in_specs=[ANY] * 3,
        out_specs=[VMEM] * 3,
        scratch_shapes=[pltpu.SemaphoreType.DMA((2, u0.shape[1])), pltpu.SemaphoreType.DMA],
        cost_estimate=cost(0, 6_000_000),
        compiler_params=pltpu.CompilerParams(vmem_limit_bytes=8 * 2**20),
        name="stage",
    )(u0, u1, masks)


def last_kernel(first, field_ref, u0_ref, u1_ref, masks_ref, before_ref, mine_ref, theirs_ref):
    lines = add_lines(0, first, field_ref, u0_ref, u1_ref, masks_ref, before_ref)
    table = jnp.concatenate([jnp.sum(line, axis=0, keepdims=True) for line in lines], axis=0)
    table = jnp.sum(table, axis=1, keepdims=True)
    share = mine_ref.shape[1]
    for part in range(2):
        at = part * 2 * share
        mine_ref[part] = table[at : at + share]
        theirs_ref[part] = table[at + share : at + 2 * share]


def last(first, field, u0, u1, masks, lines):
    share = masks.shape[1] // 4
    return pl.pallas_call(
        lambda *refs: last_kernel(first, *refs),
        out_shape=[jax.ShapeDtypeStruct((2, share, 1), F32)] * 2,
        in_specs=[VMEM] * 5,
        out_specs=[VMEM] * 2,
        cost_estimate=cost(4_000_000, 4_000_000),
        compiler_params=pltpu.CompilerParams(vmem_limit_bytes=8 * 2**20),
        name="last",
    )(field, u0, u1, masks, lines)


def local(fields, block_cols, sources, deltas, partner):
    assert fields.shape[0] == 1 and lax.axis_size("src") == 2
    del partner
    fields = fields[0]
    times = fields.shape[0]
    core = lax.axis_index("src").reshape(1)
    pairs = one_way_pairs(lax.axis_size("mom"))
    swap = lambda value: lax.ppermute(value, "src", [(0, 1), (1, 0)])
    to_partner = lambda value: lax.ppermute(value, "mom", pairs)

    cols = block_cols.reshape(-1)
    far_cols = to_partner(cols)
    own_field = pick_source(sources, fields)
    far = [to_partner(own_field)]

    other_time = swap(sources)
    order, active, full, masks = plan(core, sources, other_time, deltas, times)
    rows = fields.shape[2]
    half = rows // 2
    halves = [(0, half), (half, rows - half)]
    pieces = [(slot, 0, rows) for slot in range(times - 2)]
    pieces += [(slot, *part) for slot in (times - 2, times - 1) for part in halves]
    picked = [own_field, *pick_others(order, fields, pieces[1:])]
    *early, near_low, near_high, late_low, late_high = picked
    far += [to_partner(field) for field in early[1:]]
    other_cols = swap(cols)
    far_other_cols = swap(far_cols)
    other_field = swap(own_field)
    far_other = swap(far[0])
    near_low, far[0] = lax.optimization_barrier((near_low, far[0]))
    near_high, far_other = lax.optimization_barrier((near_high, far_other))
    near_low, near_high = to_partner(near_low), to_partner(near_high)
    u0 = weights(
        80_000_000_000,
        0,
        pieces,
        order,
        active,
        sources,
        sources,
        far_cols,
        cols,
        far_cols,
        cols,
        far[0],
        own_field,
        picked,
    )
    u1 = weights(
        2_000_000_000,
        1,
        pieces,
        order,
        active,
        other_time,
        other_time,
        far_other_cols,
        other_cols,
        far_cols,
        cols,
        far_other,
        other_field,
        picked,
    )
    lines = inner(0, 0, far[0], u0, u1, masks)
    for slot, field in enumerate(far[1:], 1):
        lines = inner(slot, 0, field, u0, u1, masks, lines)

    both = ("mom", "src")

    def with_slot(cores):
        routes = [(2 * a + c, 2 * b + c) for a, b in pairs for c in cores]

        def branch(low, high, u0, u1, masks, lines):
            low, high = lax.ppermute(low, both, routes), lax.ppermute(high, both, routes)
            lines = inner(times - 1, 0, low, u0, u1, masks, lines)
            return inner(times - 1, half, high, u0, u1, masks, lines), *stage(times - 2, u0, u1, masks)

        return branch

    def without_slot(low, high, u0, u1, masks, lines):
        return lines, *stage(times - 2, u0, u1, masks)

    branches = [without_slot, with_slot([0]), with_slot([1]), with_slot([0, 1])]
    late_low, late_high, lines = lax.optimization_barrier((late_low, late_high, lines))
    lines, *staged = lax.switch(full[0], branches, late_low, late_high, u0, u1, masks, lines)
    lines = inner(0, 0, near_low, *staged, lines)
    mine, theirs = last(half, near_high, *staged, lines)

    total = mine + swap(theirs)
    back = [(2 * a + c, 2 * b + c) for b, a in pairs for c in range(2)]
    return total + lax.ppermute(total, both, back)


def solution(mesh):
    in_specs = (
        P(("ens", "mom"), "src", None, None, None, None, None),
        P(("ens", "mom"), "src", None, None),
        P("src"),
        P(),
        P("mom"),
    )
    out_specs = P(None, "src", ("ens", "mom"))
    return jax.shard_map(local, mesh=mesh, in_specs=in_specs, out_specs=out_specs, check_vma=False)
```

```python
import jax
import jax.numpy as jnp
from jax import lax
from jax.experimental import pallas as pl
from jax.experimental.pallas import tpu as pltpu
from jax.sharding import PartitionSpec as P

F32 = jnp.float32
BF16 = jnp.bfloat16
I32 = jnp.int32
SMEM = pl.BlockSpec(memory_space=pltpu.SMEM)
VMEM = pl.BlockSpec(memory_space=pltpu.VMEM)
ANY = pl.BlockSpec(memory_space=pl.ANY)


def one_way_pairs(count):
    half = count // 2
    outer = half // 2
    return [(g + half, g) if g < outer else (g, g + half) for g in range(half)]


def cost(flops, size):
    return pl.CostEstimate(flops=flops, bytes_accessed=size, transcendentals=0)


def pick_source_kernel(senders, source_ref, fields_ref, out_ref, sems):
    first, last = senders
    group = lax.axis_index("mom")
    sends = (group >= first) & (group < last)

    @pl.when(sends)
    def _():
        time = lax.rem(source_ref[0], I32(fields_ref.shape[0]))
        copies = [
            pltpu.make_async_copy(fields_ref.at[time, part, r], out_ref.at[part, r], sems.at[part, r])
            for part in range(fields_ref.shape[1])
            for r in range(fields_ref.shape[2])
        ]
        for copy in copies:
            copy.start()
        for copy in copies:
            copy.wait()

    @pl.when(jnp.logical_not(sends))
    def _():
        out_ref[...] = jnp.zeros_like(out_ref)


def pick_source(source, fields, senders):
    return pl.pallas_call(
        lambda *refs: pick_source_kernel(senders, *refs),
        out_shape=jax.ShapeDtypeStruct(fields.shape[1:], fields.dtype),
        in_specs=[SMEM, ANY],
        out_specs=VMEM,
        scratch_shapes=[pltpu.SemaphoreType.DMA(fields.shape[1:3])],
        cost_estimate=cost(0, 1_600_000),
        compiler_params=pltpu.CompilerParams(vmem_limit_bytes=52 * 2**20),
        name="pick_source",
    )(source, fields)


def pick_kernel(pieces, order_ref, fields_ref, *refs):
    *outs, sems = refs
    copies = [
        pltpu.make_async_copy(
            fields_ref.at[order_ref[slot], part, pl.ds(first, rows)], out.at[part], sems.at[at, part]
        )
        for at, ((slot, first, rows), out) in enumerate(zip(pieces, outs))
        for part in range(2)
    ]
    for copy in copies:
        copy.start()
    for copy in copies:
        copy.wait()


def pick_others(order, fields, pieces):
    return pl.pallas_call(
        lambda *refs: pick_kernel(pieces, *refs),
        out_shape=[
            jax.ShapeDtypeStruct((2, rows) + fields.shape[3:], fields.dtype) for _, _, rows in pieces
        ],
        in_specs=[SMEM, ANY],
        out_specs=[VMEM] * len(pieces),
        scratch_shapes=[pltpu.SemaphoreType.DMA((len(pieces), 2))],
        cost_estimate=cost(0, 5_000_000),
        compiler_params=pltpu.CompilerParams(vmem_limit_bytes=51 * 2**20),
        name="pick_others",
    )(order, fields)


def plan_kernel(core_ref, own_ref, other_ref, deltas_ref, order_ref, active_ref, full_ref, masks_ref):
    times = order_ref.shape[0]
    deltas = deltas_ref.shape[0]
    sinks = []
    for s, ref in enumerate((own_ref, other_ref)):
        for k in range(deltas):
            sinks.append(lax.rem(ref[0] + deltas_ref[k], I32(2 * times)))
    base = core_ref[0] * times
    first = own_ref[0] - base
    keys = []
    for t in range(times):
        needed = sinks[0] == base + t
        for sink in sinks[1:]:
            needed = needed | (sink == base + t)
        key = jnp.where(needed, I32(t), I32(times + t))
        keys.append(jnp.where(first == t, I32(-1), key))
    for t in range(times):
        rank = I32(0)
        for other in range(times):
            if other != t:
                rank += (keys[other] < keys[t]).astype(I32)
        order_ref[rank] = I32(t)
        for s in range(2):
            active = sinks[s * deltas] == base + t
            for k in range(1, deltas):
                active = active | (sinks[s * deltas + k] == base + t)
            active_ref[s * times + rank] = active.astype(I32)
    full = I32(0)
    for c in range(2):
        count = I32(0)
        for t in range(times):
            needed = (own_ref[0] == c * times + t) | (other_ref[0] == c * times + t)
            for sink in sinks:
                needed = needed | (sink == c * times + t)
            count += needed.astype(I32)
        full += jnp.where(count == times, I32(1 << c), I32(0))
    full_ref[0] = full
    for slot in range(times):
        time = base + order_ref[slot]
        for s in range(2):
            for k in range(deltas):
                own_first = sinks[s * deltas + (k + deltas // 2) % deltas]
                sink = jnp.where(core_ref[0] == 0, sinks[s * deltas + k], own_first)
                row = jnp.full((1, masks_ref.shape[2]), jnp.where(sink == time, F32(1), F32(0)))
                masks_ref[slot, s * deltas + k : s * deltas + k + 1] = row


def plan(core, own, other, deltas, times):
    return pl.pallas_call(
        plan_kernel,
        out_shape=[
            jax.ShapeDtypeStruct((times,), I32),
            jax.ShapeDtypeStruct((2 * times,), I32),
            jax.ShapeDtypeStruct((1,), I32),
            jax.ShapeDtypeStruct((times, 2 * deltas.shape[0], 128), F32),
        ],
        in_specs=[SMEM] * 4,
        out_specs=[SMEM] * 3 + [VMEM],
        cost_estimate=cost(0, 1000),
        name="plan",
    )(core, own, other, deltas)


def weights_kernel(s, pieces, order_ref, active_ref, *refs):
    far_ref, own_ref, far_cols, own_cols, m_cols, b_cols, a_ref, d_ref, *refs = refs
    *b_refs, u_ref, la, ld, bs, yn, held, sems = refs
    slot = pl.program_id(0)
    rows, per_row, size = a_ref.shape[1], a_ref.shape[2], a_ref.shape[3]
    times = order_ref.shape[0]
    step = rows * per_row
    base = order_ref[slot] * step
    a_base = lax.rem(far_ref[0], I32(times)) * step
    d_base = lax.rem(own_ref[0], I32(times)) * step
    lo, hi = pl.ds(0, size), pl.ds(size, size)

    b_copies = [[] for _ in range(times)]
    for at, ((piece_slot, first, count), b_ref) in enumerate(zip(pieces, b_refs)):
        for part in range(2):
            to = held.at[piece_slot % 2, part, pl.ds(first, count)]
            b_copies[piece_slot].append(pltpu.make_async_copy(b_ref.at[part], to, sems.at[at, part]))

    @pl.when(slot == 0)
    def _():
        for copy in b_copies[0]:
            copy.start()
        for r in range(rows):
            for j in range(per_row):
                real, imag = a_ref[0, r, j], a_ref[1, r, j]
                la[r, j, lo, lo] = real
                la[r, j, lo, hi] = -imag
                la[r, j, hi, lo] = imag
                la[r, j, hi, hi] = real
                real, imag = d_ref[0, r, j].T, d_ref[1, r, j].T
                ld[r, j, lo, lo] = real
                ld[r, j, lo, hi] = -imag
                ld[r, j, hi, lo] = imag
                ld[r, j, hi, hi] = real

    for at in range(times):

        @pl.when(slot == at)
        def _():
            for copy in b_copies[at + 1] if at + 1 < times else []:
                copy.start()
            for copy in b_copies[at]:
                copy.wait()

    @pl.when(active_ref[s * times + slot] == 0)
    def _():
        u_ref[...] = jnp.zeros_like(u_ref)

    @pl.when(active_ref[s * times + slot] != 0)
    def _():
        for r in range(rows):
            for j in range(per_row):
                bs[r, lo, pl.ds(j * size, size)] = held[slot % 2, 0, r, j]
                bs[r, hi, pl.ds(j * size, size)] = held[slot % 2, 1, r, j]

        yn[...] = jnp.zeros_like(yn)
        for r in range(rows):
            inners = [far_cols[a_base + r * per_row + j] for j in range(per_row)]
            parts = [
                jnp.dot(la[r, j], bs[inners[j]], preferred_element_type=F32) for j in range(per_row)
            ]
            pieces = []
            for j in range(per_row):
                for k in range(per_row):
                    col = b_cols[base + inners[j] * per_row + k]
                    pieces.append((j, col, parts[j][:, k * size : (k + 1) * size]))
            for at in reversed(range(len(pieces))):
                j, col, value = pieces[at]
                for other_j, other_col, other in pieces:
                    if other_j > j:
                        value = value + jnp.where(other_col == col, 1.0, 0.0) * other
                yn[col, pl.ds(r * size, size), lo] = value[:size].astype(BF16)
                yn[col, pl.ds(r * size, size), hi] = value[size:].astype(BF16)

        trace_real = jnp.zeros((size, size), F32)
        trace_imag = jnp.zeros((size, size), F32)
        for r in range(rows):
            trace_real += yn[r, pl.ds(r * size, size), lo].astype(F32)
            trace_imag += yn[r, pl.ds(r * size, size), hi].astype(F32)
        diagonal = lax.broadcasted_iota(I32, (size, size), 0) == lax.broadcasted_iota(I32, (size, size), 1)
        trace_real = jnp.sum(jnp.where(diagonal, trace_real, 0.0), axis=(0, 1), keepdims=True)
        trace_imag = jnp.sum(jnp.where(diagonal, trace_imag, 0.0), axis=(0, 1), keepdims=True)

        for r in range(rows):
            for j in range(per_row):
                col = m_cols[base + r * per_row + j]
                pick = I32(0)
                keep = F32(0)
                for k in range(per_row):
                    hit = own_cols[d_base + col * per_row + k] == r
                    pick = jnp.where(hit, I32(k), pick)
                    keep = jnp.where(hit, F32(1), keep)
                real = ld[col, pick, lo, lo].astype(F32)
                imag = ld[col, pick, hi, lo].astype(F32)
                weight_real, weight_imag = trace_real * keep, trace_imag * keep
                u_ref[0, r, j, 0] = weight_real * real - weight_imag * imag
                u_ref[0, r, j, 1] = weight_real * imag + weight_imag * real

        for i in range(rows):
            for j in range(per_row):
                r = own_cols[d_base + i * per_row + j]
                met = [m_cols[base + r * per_row + k] for k in range(per_row)]
                right = jnp.concatenate(
                    [yn[i, pl.ds(pl.multiple_of(col * size, size), size)] for col in met], axis=0
                )
                part = lax.dot_general(
                    ld[i, j], right, (((1,), (1,)), ((), ())), preferred_element_type=F32
                )
                for k in range(per_row):
                    u_ref[0, r, k, 0] -= part[:size, k * size : (k + 1) * size]
                    u_ref[0, r, k, 1] -= part[size:, k * size : (k + 1) * size]


def weights(flops, s, pieces, order, active, far_time, own_time, far_cols, own_cols, m_cols, b_cols, a, d, picked):
    times = order.shape[0]
    _, rows, per_row, size, _ = a.shape
    whole = lambda slot, *_: (0, 0, 0, 0, 0)
    return pl.pallas_call(
        lambda *refs: weights_kernel(s, pieces, *refs),
        out_shape=jax.ShapeDtypeStruct((times, rows, per_row, 2, size, size), F32),
        grid_spec=pltpu.PrefetchScalarGridSpec(
            num_scalar_prefetch=8,
            grid=(times,),
            in_specs=[
                pl.BlockSpec(a.shape, whole),
                pl.BlockSpec(a.shape, whole),
                *[ANY] * len(picked),
            ],
            out_specs=pl.BlockSpec(
                (1, rows, per_row, 2, size, size), lambda slot, *_: (slot, 0, 0, 0, 0, 0)
            ),
            scratch_shapes=[
                pltpu.VMEM((rows, per_row, 2 * size, 2 * size), BF16),
                pltpu.VMEM((rows, per_row, 2 * size, 2 * size), BF16),
                pltpu.VMEM((rows, 2 * size, per_row * size), BF16),
                pltpu.VMEM((rows, rows * size, 2 * size), BF16),
                pltpu.VMEM((2,) + a.shape, a.dtype),
                pltpu.SemaphoreType.DMA((len(picked), 2)),
            ],
        ),
        compiler_params=pltpu.CompilerParams(vmem_limit_bytes=16 * 2**20),
        cost_estimate=cost(flops, times * 1_000_000),
        name="weights",
    )(order, active, far_time, own_time, far_cols, own_cols, m_cols, b_cols, a, d, *picked)


def products(field_ref, u_refs, slot, first):
    _, rows, per_row, size, _ = field_ref.shape
    chunk = min(size, 32)
    fold = lambda x: jnp.sum(x.reshape(chunk // 8, 8, size), axis=0)
    sums = [jnp.zeros((8, size), F32) for _ in range(2 * len(u_refs))]
    for r in range(rows):
        for j in range(per_row):
            for start in range(0, size, chunk):
                at = pl.ds(start, chunk)
                real = field_ref[0, r, j, at].astype(F32)
                imag = field_ref[1, r, j, at].astype(F32)
                for s, u_ref in enumerate(u_refs):
                    u_real, u_imag = u_ref[slot, first + r, j, 0, at], u_ref[slot, first + r, j, 1, at]
                    sums[2 * s] += fold(real * u_real - imag * u_imag)
                    sums[2 * s + 1] += fold(real * u_imag + imag * u_real)
    return sums


def add_lines(slot, first, field_ref, u0_ref, u1_ref, masks_ref, before_ref):
    sums = products(field_ref, (u0_ref, u1_ref), slot, first)
    deltas = masks_ref.shape[1] // 2
    lines = []
    for part in range(2):
        for k in range(deltas):
            line = before_ref[part * deltas + k] if before_ref is not None else 0.0
            for s in range(2):
                at = s * deltas + k
                line = line + masks_ref[slot, at : at + 1] * sums[2 * s + part]
            lines.append(line)
    return lines


def inner_kernel(slot, first, field_ref, u0_ref, u1_ref, masks_ref, *refs):
    *before, out_ref = refs
    lines = add_lines(slot, first, field_ref, u0_ref, u1_ref, masks_ref, before[0] if before else None)
    for at, line in enumerate(lines):
        out_ref[at] = line


def inner(slot, first, field, u0, u1, masks, *before):
    return pl.pallas_call(
        lambda *refs: inner_kernel(slot, first, *refs),
        out_shape=jax.ShapeDtypeStruct((masks.shape[1], 8, field.shape[-1]), F32),
        in_specs=[VMEM] * (4 + len(before)),
        out_specs=VMEM,
        cost_estimate=cost(4_000_000, 4_000_000),
        compiler_params=pltpu.CompilerParams(vmem_limit_bytes=16 * 2**20),
        name="inner",
    )(field, u0, u1, masks, *before)


def stage_kernel(slot, u0_ref, u1_ref, masks_ref, out0_ref, out1_ref, out_masks_ref, sems, masks_sem):
    copies = [
        pltpu.make_async_copy(u_ref.at[slot, r], out_ref.at[0, r], sems.at[s, r])
        for s, (u_ref, out_ref) in enumerate(((u0_ref, out0_ref), (u1_ref, out1_ref)))
        for r in range(u_ref.shape[1])
    ]
    copies.append(pltpu.make_async_copy(masks_ref.at[slot], out_masks_ref.at[0], masks_sem))
    for copy in copies:
        copy.start()
    for copy in copies:
        copy.wait()


def stage(slot, u0, u1, masks):
    one = lambda value: jax.ShapeDtypeStruct((1,) + value.shape[1:], value.dtype)
    return pl.pallas_call(
        lambda *refs: stage_kernel(slot, *refs),
        out_shape=[one(u0), one(u1), one(masks)],
        in_specs=[ANY] * 3,
        out_specs=[VMEM] * 3,
        scratch_shapes=[pltpu.SemaphoreType.DMA((2, u0.shape[1])), pltpu.SemaphoreType.DMA],
        cost_estimate=cost(0, 6_000_000),
        compiler_params=pltpu.CompilerParams(vmem_limit_bytes=8 * 2**20),
        name="stage",
    )(u0, u1, masks)


def last_kernel(field_ref, u0_ref, u1_ref, masks_ref, before_ref, mine_ref, theirs_ref):
    lines = add_lines(0, 0, field_ref, u0_ref, u1_ref, masks_ref, before_ref)
    table = jnp.concatenate([jnp.sum(line, axis=0, keepdims=True) for line in lines], axis=0)
    table = jnp.sum(table, axis=1, keepdims=True)
    share = mine_ref.shape[1]
    for part in range(2):
        at = part * 2 * share
        mine_ref[part] = table[at : at + share]
        theirs_ref[part] = table[at + share : at + 2 * share]


def last(field, u0, u1, masks, lines):
    share = masks.shape[1] // 4
    return pl.pallas_call(
        last_kernel,
        out_shape=[jax.ShapeDtypeStruct((2, share, 1), F32)] * 2,
        in_specs=[VMEM] * 5,
        out_specs=[VMEM] * 2,
        cost_estimate=cost(4_000_000, 4_000_000),
        compiler_params=pltpu.CompilerParams(vmem_limit_bytes=8 * 2**20),
        name="last",
    )(field, u0, u1, masks, lines)


def local(fields, block_cols, sources, deltas, partner):
    assert fields.shape[0] == 1 and lax.axis_size("src") == 2
    del partner
    fields = fields[0]
    times = fields.shape[0]
    core = lax.axis_index("src").reshape(1)
    pairs = one_way_pairs(lax.axis_size("mom"))
    swap = lambda value: lax.ppermute(value, "src", [(0, 1), (1, 0)])
    to_partner = lambda value: lax.ppermute(value, "mom", pairs)

    cols = block_cols.reshape(-1)
    far_cols = to_partner(cols)
    senders = min(source for source, _ in pairs), max(source for source, _ in pairs) + 1
    far = [to_partner(pick_source(sources, fields, senders))]

    other_time = swap(sources)
    order, active, full, masks = plan(core, sources, other_time, deltas, times)
    rows = fields.shape[2]
    half = rows // 2
    pieces = [(slot, 0, rows) for slot in range(times - 1)]
    pieces += [(times - 1, 0, half), (times - 1, half, rows - half)]
    picked = pick_others(order, fields, pieces)
    own_field = picked[0]
    *early, near, late_low, late_high = picked
    far += [to_partner(field) for field in early[1:]]
    near, far[0] = lax.optimization_barrier((near, far[0]))
    near = to_partner(near)

    other_cols = swap(cols)
    far_other_cols = swap(far_cols)
    other_field = swap(own_field)
    far_other = swap(far[0])
    u0 = weights(
        80_000_000_000,
        0,
        pieces,
        order,
        active,
        sources,
        sources,
        far_cols,
        cols,
        far_cols,
        cols,
        far[0],
        own_field,
        picked,
    )
    u1 = weights(
        2_000_000_000,
        1,
        pieces,
        order,
        active,
        other_time,
        other_time,
        far_other_cols,
        other_cols,
        far_cols,
        cols,
        far_other,
        other_field,
        picked,
    )
    lines = inner(0, 0, far[0], u0, u1, masks)
    for slot, field in enumerate(far[1:], 1):
        lines = inner(slot, 0, field, u0, u1, masks, lines)

    both = ("mom", "src")

    def with_slot(cores):
        routes = [(2 * a + c, 2 * b + c) for a, b in pairs for c in cores]

        def branch(low, high, u0, u1, masks, lines):
            low, high = lax.ppermute(low, both, routes), lax.ppermute(high, both, routes)
            lines = inner(times - 1, 0, low, u0, u1, masks, lines)
            return inner(times - 1, half, high, u0, u1, masks, lines), *stage(times - 2, u0, u1, masks)

        return branch

    def without_slot(low, high, u0, u1, masks, lines):
        return lines, *stage(times - 2, u0, u1, masks)

    branches = [without_slot, with_slot([0]), with_slot([1]), with_slot([0, 1])]
    late_low, late_high, lines = lax.optimization_barrier((late_low, late_high, lines))
    lines, *staged = lax.switch(full[0], branches, late_low, late_high, u0, u1, masks, lines)
    mine, theirs = last(near, *staged, lines)

    total = mine + swap(theirs)
    back = [(2 * a + c, 2 * b + c) for b, a in pairs for c in range(2)]
    return total + lax.ppermute(total, both, back)


def solution(mesh):
    in_specs = (
        P(("ens", "mom"), "src", None, None, None, None, None),
        P(("ens", "mom"), "src", None, None),
        P("src"),
        P(),
        P("mom"),
    )
    out_specs = P(None, "src", ("ens", "mom"))
    return jax.shard_map(local, mesh=mesh, in_specs=in_specs, out_specs=out_specs, check_vma=False)
```

```python
import jax
import jax.numpy as jnp
from jax import lax
from jax.experimental import pallas as pl
from jax.experimental.pallas import tpu as pltpu
from jax.sharding import PartitionSpec as P

F32 = jnp.float32
BF16 = jnp.bfloat16
I32 = jnp.int32
SMEM = pl.BlockSpec(memory_space=pltpu.SMEM)
VMEM = pl.BlockSpec(memory_space=pltpu.VMEM)
ANY = pl.BlockSpec(memory_space=pl.ANY)


def one_way_pairs(count):
    half = count // 2
    outer = half // 2
    return [(g + half, g) if g < outer else (g, g + half) for g in range(half)]


def cost(flops, size):
    return pl.CostEstimate(flops=flops, bytes_accessed=size, transcendentals=0)


def pick_source_kernel(senders, halves, source_ref, fields_ref, *refs):
    *out_refs, sems = refs
    first, last = senders
    group = lax.axis_index("mom")
    sends = (group >= first) & (group < last)

    @pl.when(sends)
    def _():
        time = lax.rem(source_ref[0], I32(fields_ref.shape[0]))
        copies = [
            pltpu.make_async_copy(
                fields_ref.at[time, part, first + r], out_ref.at[part, r], sems.at[part, first + r]
            )
            for part in range(fields_ref.shape[1])
            for (first, rows), out_ref in zip(halves, out_refs)
            for r in range(rows)
        ]
        for copy in copies:
            copy.start()
        for copy in copies:
            copy.wait()

    @pl.when(jnp.logical_not(sends))
    def _():
        for out_ref in out_refs:
            out_ref[...] = jnp.zeros_like(out_ref)


def pick_source(source, fields, senders, halves):
    return pl.pallas_call(
        lambda *refs: pick_source_kernel(senders, halves, *refs),
        out_shape=[
            jax.ShapeDtypeStruct((2, rows) + fields.shape[3:], fields.dtype) for _, rows in halves
        ],
        in_specs=[SMEM, ANY],
        out_specs=[VMEM] * len(halves),
        scratch_shapes=[pltpu.SemaphoreType.DMA(fields.shape[1:3])],
        cost_estimate=cost(0, 1_600_000),
        compiler_params=pltpu.CompilerParams(vmem_limit_bytes=52 * 2**20),
        name="pick_source",
    )(source, fields)


def pick_kernel(pieces, order_ref, fields_ref, *refs):
    *outs, sems = refs
    copies = [
        pltpu.make_async_copy(
            fields_ref.at[order_ref[slot], part, pl.ds(first, rows)], out.at[part], sems.at[at, part]
        )
        for at, ((slot, first, rows), out) in enumerate(zip(pieces, outs))
        for part in range(2)
    ]
    for copy in copies:
        copy.start()
    for copy in copies:
        copy.wait()


def pick_others(order, fields, pieces):
    return pl.pallas_call(
        lambda *refs: pick_kernel(pieces, *refs),
        out_shape=[
            jax.ShapeDtypeStruct((2, rows) + fields.shape[3:], fields.dtype) for _, _, rows in pieces
        ],
        in_specs=[SMEM, ANY],
        out_specs=[VMEM] * len(pieces),
        scratch_shapes=[pltpu.SemaphoreType.DMA((len(pieces), 2))],
        cost_estimate=cost(0, 5_000_000),
        compiler_params=pltpu.CompilerParams(vmem_limit_bytes=51 * 2**20),
        name="pick_others",
    )(order, fields)


def plan_kernel(core_ref, own_ref, other_ref, deltas_ref, order_ref, active_ref, full_ref, masks_ref):
    times = order_ref.shape[0]
    deltas = deltas_ref.shape[0]
    sinks = []
    for s, ref in enumerate((own_ref, other_ref)):
        for k in range(deltas):
            sinks.append(lax.rem(ref[0] + deltas_ref[k], I32(2 * times)))
    base = core_ref[0] * times
    first = own_ref[0] - base
    keys = []
    for t in range(times):
        needed = sinks[0] == base + t
        for sink in sinks[1:]:
            needed = needed | (sink == base + t)
        key = jnp.where(needed, I32(t), I32(times + t))
        keys.append(jnp.where(first == t, I32(-1), key))
    for t in range(times):
        rank = I32(0)
        for other in range(times):
            if other != t:
                rank += (keys[other] < keys[t]).astype(I32)
        order_ref[rank] = I32(t)
        for s in range(2):
            active = sinks[s * deltas] == base + t
            for k in range(1, deltas):
                active = active | (sinks[s * deltas + k] == base + t)
            active_ref[s * times + rank] = active.astype(I32)
    full = I32(0)
    for c in range(2):
        count = I32(0)
        for t in range(times):
            needed = (own_ref[0] == c * times + t) | (other_ref[0] == c * times + t)
            for sink in sinks:
                needed = needed | (sink == c * times + t)
            count += needed.astype(I32)
        full += jnp.where(count == times, I32(1 << c), I32(0))
    full_ref[0] = full
    for slot in range(times):
        time = base + order_ref[slot]
        for s in range(2):
            for k in range(deltas):
                own_first = sinks[s * deltas + (k + deltas // 2) % deltas]
                sink = jnp.where(core_ref[0] == 0, sinks[s * deltas + k], own_first)
                row = jnp.full((1, masks_ref.shape[2]), jnp.where(sink == time, F32(1), F32(0)))
                masks_ref[slot, s * deltas + k : s * deltas + k + 1] = row


def plan(core, own, other, deltas, times):
    return pl.pallas_call(
        plan_kernel,
        out_shape=[
            jax.ShapeDtypeStruct((times,), I32),
            jax.ShapeDtypeStruct((2 * times,), I32),
            jax.ShapeDtypeStruct((1,), I32),
            jax.ShapeDtypeStruct((times, 2 * deltas.shape[0], 128), F32),
        ],
        in_specs=[SMEM] * 4,
        out_specs=[SMEM] * 3 + [VMEM],
        cost_estimate=cost(0, 1000),
        name="plan",
    )(core, own, other, deltas)


def weights_kernel(s, pieces, order_ref, active_ref, *refs):
    far_ref, own_ref, far_cols, own_cols, m_cols, b_cols, a_low, a_high, d_ref, *refs = refs
    *b_refs, u_ref, la, ld, bs, yn, held, sems = refs
    slot = pl.program_id(0)
    rows, per_row, size = d_ref.shape[1], d_ref.shape[2], d_ref.shape[3]
    times = order_ref.shape[0]
    step = rows * per_row
    base = order_ref[slot] * step
    a_base = lax.rem(far_ref[0], I32(times)) * step
    d_base = lax.rem(own_ref[0], I32(times)) * step
    lo, hi = pl.ds(0, size), pl.ds(size, size)

    b_copies = [[] for _ in range(times)]
    for at, ((piece_slot, first, count), b_ref) in enumerate(zip(pieces, b_refs)):
        for part in range(2):
            to = held.at[piece_slot % 2, part, pl.ds(first, count)]
            b_copies[piece_slot].append(pltpu.make_async_copy(b_ref.at[part], to, sems.at[at, part]))

    @pl.when(slot == 0)
    def _():
        for copy in b_copies[0]:
            copy.start()
        for r in range(rows):
            for j in range(per_row):
                a_ref, at = (a_low, r) if r < a_low.shape[1] else (a_high, r - a_low.shape[1])
                real, imag = a_ref[0, at, j], a_ref[1, at, j]
                la[r, j, lo, lo] = real
                la[r, j, lo, hi] = -imag
                la[r, j, hi, lo] = imag
                la[r, j, hi, hi] = real
                real, imag = d_ref[0, r, j].T, d_ref[1, r, j].T
                ld[r, j, lo, lo] = real
                ld[r, j, lo, hi] = -imag
                ld[r, j, hi, lo] = imag
                ld[r, j, hi, hi] = real

    for at in range(times):

        @pl.when(slot == at)
        def _():
            for copy in b_copies[at + 1] if at + 1 < times else []:
                copy.start()
            for copy in b_copies[at]:
                copy.wait()

    @pl.when(active_ref[s * times + slot] == 0)
    def _():
        u_ref[...] = jnp.zeros_like(u_ref)

    @pl.when(active_ref[s * times + slot] != 0)
    def _():
        for r in range(rows):
            for j in range(per_row):
                bs[r, lo, pl.ds(j * size, size)] = held[slot % 2, 0, r, j]
                bs[r, hi, pl.ds(j * size, size)] = held[slot % 2, 1, r, j]

        yn[...] = jnp.zeros_like(yn)
        for r in range(rows):
            inners = [far_cols[a_base + r * per_row + j] for j in range(per_row)]
            parts = [
                jnp.dot(la[r, j], bs[inners[j]], preferred_element_type=F32) for j in range(per_row)
            ]
            pieces = []
            for j in range(per_row):
                for k in range(per_row):
                    col = b_cols[base + inners[j] * per_row + k]
                    pieces.append((j, col, parts[j][:, k * size : (k + 1) * size]))
            for at in reversed(range(len(pieces))):
                j, col, value = pieces[at]
                for other_j, other_col, other in pieces:
                    if other_j > j:
                        value = value + jnp.where(other_col == col, 1.0, 0.0) * other
                yn[col, pl.ds(r * size, size), lo] = value[:size].astype(BF16)
                yn[col, pl.ds(r * size, size), hi] = value[size:].astype(BF16)

        trace_real = jnp.zeros((size, size), F32)
        trace_imag = jnp.zeros((size, size), F32)
        for r in range(rows):
            trace_real += yn[r, pl.ds(r * size, size), lo].astype(F32)
            trace_imag += yn[r, pl.ds(r * size, size), hi].astype(F32)
        diagonal = lax.broadcasted_iota(I32, (size, size), 0) == lax.broadcasted_iota(I32, (size, size), 1)
        trace_real = jnp.sum(jnp.where(diagonal, trace_real, 0.0), axis=(0, 1), keepdims=True)
        trace_imag = jnp.sum(jnp.where(diagonal, trace_imag, 0.0), axis=(0, 1), keepdims=True)

        for r in range(rows):
            for j in range(per_row):
                col = m_cols[base + r * per_row + j]
                pick = I32(0)
                keep = F32(0)
                for k in range(per_row):
                    hit = own_cols[d_base + col * per_row + k] == r
                    pick = jnp.where(hit, I32(k), pick)
                    keep = jnp.where(hit, F32(1), keep)
                real = ld[col, pick, lo, lo].astype(F32)
                imag = ld[col, pick, hi, lo].astype(F32)
                weight_real, weight_imag = trace_real * keep, trace_imag * keep
                u_ref[0, r, j, 0] = weight_real * real - weight_imag * imag
                u_ref[0, r, j, 1] = weight_real * imag + weight_imag * real

        for i in range(rows):
            for j in range(per_row):
                r = own_cols[d_base + i * per_row + j]
                met = [m_cols[base + r * per_row + k] for k in range(per_row)]
                right = jnp.concatenate(
                    [yn[i, pl.ds(pl.multiple_of(col * size, size), size)] for col in met], axis=0
                )
                part = lax.dot_general(
                    ld[i, j], right, (((1,), (1,)), ((), ())), preferred_element_type=F32
                )
                for k in range(per_row):
                    u_ref[0, r, k, 0] -= part[:size, k * size : (k + 1) * size]
                    u_ref[0, r, k, 1] -= part[size:, k * size : (k + 1) * size]


def weights(flops, s, pieces, order, active, far_time, own_time, far_cols, own_cols, m_cols, b_cols, a, d, picked):
    times = order.shape[0]
    _, rows, per_row, size, _ = d.shape
    whole = lambda slot, *_: (0, 0, 0, 0, 0)
    return pl.pallas_call(
        lambda *refs: weights_kernel(s, pieces, *refs),
        out_shape=jax.ShapeDtypeStruct((times, rows, per_row, 2, size, size), F32),
        grid_spec=pltpu.PrefetchScalarGridSpec(
            num_scalar_prefetch=8,
            grid=(times,),
            in_specs=[
                *[pl.BlockSpec(half.shape, whole) for half in a],
                pl.BlockSpec(d.shape, whole),
                *[ANY] * len(picked),
            ],
            out_specs=pl.BlockSpec(
                (1, rows, per_row, 2, size, size), lambda slot, *_: (slot, 0, 0, 0, 0, 0)
            ),
            scratch_shapes=[
                pltpu.VMEM((rows, per_row, 2 * size, 2 * size), BF16),
                pltpu.VMEM((rows, per_row, 2 * size, 2 * size), BF16),
                pltpu.VMEM((rows, 2 * size, per_row * size), BF16),
                pltpu.VMEM((rows, rows * size, 2 * size), BF16),
                pltpu.VMEM((2,) + d.shape, d.dtype),
                pltpu.SemaphoreType.DMA((len(picked), 2)),
            ],
        ),
        compiler_params=pltpu.CompilerParams(vmem_limit_bytes=16 * 2**20),
        cost_estimate=cost(flops, times * 1_000_000),
        name="weights",
    )(order, active, far_time, own_time, far_cols, own_cols, m_cols, b_cols, *a, d, *picked)


def products(field_ref, u_refs, slot, first):
    _, rows, per_row, size, _ = field_ref.shape
    chunk = min(size, 32)
    fold = lambda x: jnp.sum(x.reshape(chunk // 8, 8, size), axis=0)
    sums = [jnp.zeros((8, size), F32) for _ in range(2 * len(u_refs))]
    for r in range(rows):
        for j in range(per_row):
            for start in range(0, size, chunk):
                at = pl.ds(start, chunk)
                real = field_ref[0, r, j, at].astype(F32)
                imag = field_ref[1, r, j, at].astype(F32)
                for s, u_ref in enumerate(u_refs):
                    u_real, u_imag = u_ref[slot, first + r, j, 0, at], u_ref[slot, first + r, j, 1, at]
                    sums[2 * s] += fold(real * u_real - imag * u_imag)
                    sums[2 * s + 1] += fold(real * u_imag + imag * u_real)
    return sums


def add_lines(slot, first, field_ref, u0_ref, u1_ref, masks_ref, before_ref):
    sums = products(field_ref, (u0_ref, u1_ref), slot, first)
    deltas = masks_ref.shape[1] // 2
    lines = []
    for part in range(2):
        for k in range(deltas):
            line = before_ref[part * deltas + k] if before_ref is not None else 0.0
            for s in range(2):
                at = s * deltas + k
                line = line + masks_ref[slot, at : at + 1] * sums[2 * s + part]
            lines.append(line)
    return lines


def inner_kernel(slot, first, field_ref, u0_ref, u1_ref, masks_ref, *refs):
    *before, out_ref = refs
    lines = add_lines(slot, first, field_ref, u0_ref, u1_ref, masks_ref, before[0] if before else None)
    for at, line in enumerate(lines):
        out_ref[at] = line


def inner(slot, first, field, u0, u1, masks, *before):
    return pl.pallas_call(
        lambda *refs: inner_kernel(slot, first, *refs),
        out_shape=jax.ShapeDtypeStruct((masks.shape[1], 8, field.shape[-1]), F32),
        in_specs=[VMEM] * (4 + len(before)),
        out_specs=VMEM,
        cost_estimate=cost(4_000_000, 4_000_000),
        compiler_params=pltpu.CompilerParams(vmem_limit_bytes=16 * 2**20),
        name="inner",
    )(field, u0, u1, masks, *before)


def stage_kernel(slot, u0_ref, u1_ref, masks_ref, out0_ref, out1_ref, out_masks_ref, sems, masks_sem):
    copies = [
        pltpu.make_async_copy(u_ref.at[slot, r], out_ref.at[0, r], sems.at[s, r])
        for s, (u_ref, out_ref) in enumerate(((u0_ref, out0_ref), (u1_ref, out1_ref)))
        for r in range(u_ref.shape[1])
    ]
    copies.append(pltpu.make_async_copy(masks_ref.at[slot], out_masks_ref.at[0], masks_sem))
    for copy in copies:
        copy.start()
    for copy in copies:
        copy.wait()


def stage(slot, u0, u1, masks):
    one = lambda value: jax.ShapeDtypeStruct((1,) + value.shape[1:], value.dtype)
    return pl.pallas_call(
        lambda *refs: stage_kernel(slot, *refs),
        out_shape=[one(u0), one(u1), one(masks)],
        in_specs=[ANY] * 3,
        out_specs=[VMEM] * 3,
        scratch_shapes=[pltpu.SemaphoreType.DMA((2, u0.shape[1])), pltpu.SemaphoreType.DMA],
        cost_estimate=cost(0, 6_000_000),
        compiler_params=pltpu.CompilerParams(vmem_limit_bytes=8 * 2**20),
        name="stage",
    )(u0, u1, masks)


def last_kernel(field_ref, u0_ref, u1_ref, masks_ref, before_ref, mine_ref, theirs_ref):
    lines = add_lines(0, 0, field_ref, u0_ref, u1_ref, masks_ref, before_ref)
    table = jnp.concatenate([jnp.sum(line, axis=0, keepdims=True) for line in lines], axis=0)
    table = jnp.sum(table, axis=1, keepdims=True)
    share = mine_ref.shape[1]
    for part in range(2):
        at = part * 2 * share
        mine_ref[part] = table[at : at + share]
        theirs_ref[part] = table[at + share : at + 2 * share]


def last(field, u0, u1, masks, lines):
    share = masks.shape[1] // 4
    return pl.pallas_call(
        last_kernel,
        out_shape=[jax.ShapeDtypeStruct((2, share, 1), F32)] * 2,
        in_specs=[VMEM] * 5,
        out_specs=[VMEM] * 2,
        cost_estimate=cost(4_000_000, 4_000_000),
        compiler_params=pltpu.CompilerParams(vmem_limit_bytes=8 * 2**20),
        name="last",
    )(field, u0, u1, masks, lines)


def local(fields, block_cols, sources, deltas, partner):
    assert fields.shape[0] == 1 and lax.axis_size("src") == 2
    del partner
    fields = fields[0]
    times = fields.shape[0]
    core = lax.axis_index("src").reshape(1)
    pairs = one_way_pairs(lax.axis_size("mom"))
    swap = lambda value: lax.ppermute(value, "src", [(0, 1), (1, 0)])
    to_partner = lambda value: lax.ppermute(value, "mom", pairs)

    cols = block_cols.reshape(-1)
    far_cols = to_partner(cols)
    senders = min(source for source, _ in pairs), max(source for source, _ in pairs) + 1
    rows = fields.shape[2]
    half = rows // 2
    halves = [(0, half), (half, rows - half)]
    far_source = [to_partner(part) for part in pick_source(sources, fields, senders, halves)]

    other_time = swap(sources)
    order, active, full, masks = plan(core, sources, other_time, deltas, times)
    pieces = [(slot, 0, rows) for slot in range(times - 1)]
    pieces += [(times - 1, *part) for part in halves]
    picked = pick_others(order, fields, pieces)
    own_field = picked[0]
    *early, near, late_low, late_high = picked
    far = [to_partner(field) for field in early[1:]]
    near, far_source = lax.optimization_barrier((near, far_source))
    near = to_partner(near)

    other_cols = swap(cols)
    far_other_cols = swap(far_cols)
    other_field = swap(own_field)
    far_other = [swap(part) for part in far_source]
    u0 = weights(
        80_000_000_000,
        0,
        pieces,
        order,
        active,
        sources,
        sources,
        far_cols,
        cols,
        far_cols,
        cols,
        far_source,
        own_field,
        picked,
    )
    u1 = weights(
        2_000_000_000,
        1,
        pieces,
        order,
        active,
        other_time,
        other_time,
        far_other_cols,
        other_cols,
        far_cols,
        cols,
        far_other,
        other_field,
        picked,
    )
    lines = inner(0, 0, far_source[0], u0, u1, masks)
    lines = inner(0, half, far_source[1], u0, u1, masks, lines)
    for slot, field in enumerate(far, 1):
        lines = inner(slot, 0, field, u0, u1, masks, lines)

    both = ("mom", "src")

    def with_slot(cores):
        routes = [(2 * a + c, 2 * b + c) for a, b in pairs for c in cores]

        def branch(low, high, u0, u1, masks, lines):
            low, high = lax.ppermute(low, both, routes), lax.ppermute(high, both, routes)
            lines = inner(times - 1, 0, low, u0, u1, masks, lines)
            return inner(times - 1, half, high, u0, u1, masks, lines), *stage(times - 2, u0, u1, masks)

        return branch

    def without_slot(low, high, u0, u1, masks, lines):
        return lines, *stage(times - 2, u0, u1, masks)

    branches = [without_slot, with_slot([0]), with_slot([1]), with_slot([0, 1])]
    late_low, late_high, lines = lax.optimization_barrier((late_low, late_high, lines))
    lines, *staged = lax.switch(full[0], branches, late_low, late_high, u0, u1, masks, lines)
    mine, theirs = last(near, *staged, lines)

    total = mine + swap(theirs)
    back = [(2 * a + c, 2 * b + c) for b, a in pairs for c in range(2)]
    return total + lax.ppermute(total, both, back)


def solution(mesh):
    in_specs = (
        P(("ens", "mom"), "src", None, None, None, None, None),
        P(("ens", "mom"), "src", None, None),
        P("src"),
        P(),
        P("mom"),
    )
    out_specs = P(None, "src", ("ens", "mom"))
    return jax.shard_map(local, mesh=mesh, in_specs=in_specs, out_specs=out_specs, check_vma=False)
```

```python
import jax
import jax.numpy as jnp
from jax import lax
from jax.experimental import pallas as pl
from jax.experimental.pallas import tpu as pltpu
from jax.sharding import PartitionSpec as P

F32 = jnp.float32
BF16 = jnp.bfloat16
I32 = jnp.int32
SMEM = pl.BlockSpec(memory_space=pltpu.SMEM)
VMEM = pl.BlockSpec(memory_space=pltpu.VMEM)
ANY = pl.BlockSpec(memory_space=pl.ANY)


def one_way_pairs(count):
    half = count // 2
    outer = half // 2
    return [(g + half, g) if g < outer else (g, g + half) for g in range(half)]


def cost(flops, size):
    return pl.CostEstimate(flops=flops, bytes_accessed=size, transcendentals=0)


def pick_source_kernel(source_ref, fields_ref, out_ref, sems):
    time = lax.rem(source_ref[0], I32(fields_ref.shape[0]))
    copies = [
        pltpu.make_async_copy(fields_ref.at[time, part, r], out_ref.at[part, r], sems.at[part, r])
        for part in range(fields_ref.shape[1])
        for r in range(fields_ref.shape[2])
    ]
    for copy in copies:
        copy.start()
    for copy in copies:
        copy.wait()


def pick_source(source, fields):
    return pl.pallas_call(
        pick_source_kernel,
        out_shape=jax.ShapeDtypeStruct(fields.shape[1:], fields.dtype),
        in_specs=[SMEM, ANY],
        out_specs=VMEM,
        scratch_shapes=[pltpu.SemaphoreType.DMA(fields.shape[1:3])],
        cost_estimate=cost(0, 1_600_000),
        compiler_params=pltpu.CompilerParams(vmem_limit_bytes=52 * 2**20),
        name="pick_source",
    )(source, fields)


def no_field_kernel(out_ref):
    out_ref[...] = jnp.zeros_like(out_ref)


def no_field(fields):
    return pl.pallas_call(
        no_field_kernel,
        out_shape=jax.ShapeDtypeStruct(fields.shape[1:], fields.dtype),
        out_specs=VMEM,
        cost_estimate=cost(0, 800_000),
        name="no_field",
    )()


def pick_kernel(pieces, order_ref, fields_ref, *refs):
    *outs, sems = refs
    copies = [
        pltpu.make_async_copy(
            fields_ref.at[order_ref[slot], part, pl.ds(first, rows)], out.at[part], sems.at[at, part]
        )
        for at, ((slot, first, rows), out) in enumerate(zip(pieces, outs))
        for part in range(2)
    ]
    for copy in copies:
        copy.start()
    for copy in copies:
        copy.wait()


def pick_others(order, fields, pieces):
    return pl.pallas_call(
        lambda *refs: pick_kernel(pieces, *refs),
        out_shape=[
            jax.ShapeDtypeStruct((2, rows) + fields.shape[3:], fields.dtype) for _, _, rows in pieces
        ],
        in_specs=[SMEM, ANY],
        out_specs=[VMEM] * len(pieces),
        scratch_shapes=[pltpu.SemaphoreType.DMA((len(pieces), 2))],
        cost_estimate=cost(0, 5_000_000),
        compiler_params=pltpu.CompilerParams(vmem_limit_bytes=51 * 2**20),
        name="pick_others",
    )(order, fields)


def plan_kernel(core_ref, own_ref, other_ref, deltas_ref, order_ref, active_ref, full_ref, masks_ref):
    times = order_ref.shape[0]
    deltas = deltas_ref.shape[0]
    sinks = []
    for s, ref in enumerate((own_ref, other_ref)):
        for k in range(deltas):
            sinks.append(lax.rem(ref[0] + deltas_ref[k], I32(2 * times)))
    base = core_ref[0] * times
    first = own_ref[0] - base
    keys = []
    for t in range(times):
        needed = sinks[0] == base + t
        for sink in sinks[1:]:
            needed = needed | (sink == base + t)
        key = jnp.where(needed, I32(t), I32(times + t))
        keys.append(jnp.where(first == t, I32(-1), key))
    for t in range(times):
        rank = I32(0)
        for other in range(times):
            if other != t:
                rank += (keys[other] < keys[t]).astype(I32)
        order_ref[rank] = I32(t)
        for s in range(2):
            active = sinks[s * deltas] == base + t
            for k in range(1, deltas):
                active = active | (sinks[s * deltas + k] == base + t)
            active_ref[s * times + rank] = active.astype(I32)
    full = I32(0)
    for c in range(2):
        count = I32(0)
        for t in range(times):
            needed = (own_ref[0] == c * times + t) | (other_ref[0] == c * times + t)
            for sink in sinks:
                needed = needed | (sink == c * times + t)
            count += needed.astype(I32)
        full += jnp.where(count == times, I32(1 << c), I32(0))
    full_ref[0] = full
    for slot in range(times):
        time = base + order_ref[slot]
        for s in range(2):
            for k in range(deltas):
                own_first = sinks[s * deltas + (k + deltas // 2) % deltas]
                sink = jnp.where(core_ref[0] == 0, sinks[s * deltas + k], own_first)
                row = jnp.full((1, masks_ref.shape[2]), jnp.where(sink == time, F32(1), F32(0)))
                masks_ref[slot, s * deltas + k : s * deltas + k + 1] = row


def plan(core, own, other, deltas, times):
    return pl.pallas_call(
        plan_kernel,
        out_shape=[
            jax.ShapeDtypeStruct((times,), I32),
            jax.ShapeDtypeStruct((2 * times,), I32),
            jax.ShapeDtypeStruct((1,), I32),
            jax.ShapeDtypeStruct((times, 2 * deltas.shape[0], 128), F32),
        ],
        in_specs=[SMEM] * 4,
        out_specs=[SMEM] * 3 + [VMEM],
        cost_estimate=cost(0, 1000),
        name="plan",
    )(core, own, other, deltas)


def weights_kernel(s, pieces, order_ref, active_ref, *refs):
    far_ref, own_ref, far_cols, own_cols, m_cols, b_cols, a_ref, d_ref, *refs = refs
    *b_refs, u_ref, la, ld, bs, yn, held, sems = refs
    slot = pl.program_id(0)
    rows, per_row, size = a_ref.shape[1], a_ref.shape[2], a_ref.shape[3]
    times = order_ref.shape[0]
    step = rows * per_row
    base = order_ref[slot] * step
    a_base = lax.rem(far_ref[0], I32(times)) * step
    d_base = lax.rem(own_ref[0], I32(times)) * step
    lo, hi = pl.ds(0, size), pl.ds(size, size)

    b_copies = [[] for _ in range(times)]
    for at, ((piece_slot, first, count), b_ref) in enumerate(zip(pieces, b_refs)):
        for part in range(2):
            to = held.at[piece_slot % 2, part, pl.ds(first, count)]
            b_copies[piece_slot].append(pltpu.make_async_copy(b_ref.at[part], to, sems.at[at, part]))

    @pl.when(slot == 0)
    def _():
        for copy in b_copies[0]:
            copy.start()
        for r in range(rows):
            for j in range(per_row):
                real, imag = a_ref[0, r, j], a_ref[1, r, j]
                la[r, j, lo, lo] = real
                la[r, j, lo, hi] = -imag
                la[r, j, hi, lo] = imag
                la[r, j, hi, hi] = real
                real, imag = d_ref[0, r, j].T, d_ref[1, r, j].T
                ld[r, j, lo, lo] = real
                ld[r, j, lo, hi] = -imag
                ld[r, j, hi, lo] = imag
                ld[r, j, hi, hi] = real

    for at in range(times):

        @pl.when(slot == at)
        def _():
            for copy in b_copies[at + 1] if at + 1 < times else []:
                copy.start()
            for copy in b_copies[at]:
                copy.wait()

    @pl.when(active_ref[s * times + slot] == 0)
    def _():
        u_ref[...] = jnp.zeros_like(u_ref)

    @pl.when(active_ref[s * times + slot] != 0)
    def _():
        for r in range(rows):
            for j in range(per_row):
                bs[r, lo, pl.ds(j * size, size)] = held[slot % 2, 0, r, j]
                bs[r, hi, pl.ds(j * size, size)] = held[slot % 2, 1, r, j]

        yn[...] = jnp.zeros_like(yn)
        for r in range(rows):
            inners = [far_cols[a_base + r * per_row + j] for j in range(per_row)]
            parts = [
                jnp.dot(la[r, j], bs[inners[j]], preferred_element_type=F32) for j in range(per_row)
            ]
            pieces = []
            for j in range(per_row):
                for k in range(per_row):
                    col = b_cols[base + inners[j] * per_row + k]
                    pieces.append((j, col, parts[j][:, k * size : (k + 1) * size]))
            for at in reversed(range(len(pieces))):
                j, col, value = pieces[at]
                for other_j, other_col, other in pieces:
                    if other_j > j:
                        value = value + jnp.where(other_col == col, 1.0, 0.0) * other
                yn[col, pl.ds(r * size, size), lo] = value[:size].astype(BF16)
                yn[col, pl.ds(r * size, size), hi] = value[size:].astype(BF16)

        trace_real = jnp.zeros((size, size), F32)
        trace_imag = jnp.zeros((size, size), F32)
        for r in range(rows):
            trace_real += yn[r, pl.ds(r * size, size), lo].astype(F32)
            trace_imag += yn[r, pl.ds(r * size, size), hi].astype(F32)
        diagonal = lax.broadcasted_iota(I32, (size, size), 0) == lax.broadcasted_iota(I32, (size, size), 1)
        trace_real = jnp.sum(jnp.where(diagonal, trace_real, 0.0), axis=(0, 1), keepdims=True)
        trace_imag = jnp.sum(jnp.where(diagonal, trace_imag, 0.0), axis=(0, 1), keepdims=True)

        for r in range(rows):
            for j in range(per_row):
                col = m_cols[base + r * per_row + j]
                pick = I32(0)
                keep = F32(0)
                for k in range(per_row):
                    hit = own_cols[d_base + col * per_row + k] == r
                    pick = jnp.where(hit, I32(k), pick)
                    keep = jnp.where(hit, F32(1), keep)
                real = ld[col, pick, lo, lo].astype(F32)
                imag = ld[col, pick, hi, lo].astype(F32)
                weight_real, weight_imag = trace_real * keep, trace_imag * keep
                u_ref[0, r, j, 0] = weight_real * real - weight_imag * imag
                u_ref[0, r, j, 1] = weight_real * imag + weight_imag * real

        for i in range(rows):
            for j in range(per_row):
                r = own_cols[d_base + i * per_row + j]
                met = [m_cols[base + r * per_row + k] for k in range(per_row)]
                right = jnp.concatenate(
                    [yn[i, pl.ds(pl.multiple_of(col * size, size), size)] for col in met], axis=0
                )
                part = lax.dot_general(
                    ld[i, j], right, (((1,), (1,)), ((), ())), preferred_element_type=F32
                )
                for k in range(per_row):
                    u_ref[0, r, k, 0] -= part[:size, k * size : (k + 1) * size]
                    u_ref[0, r, k, 1] -= part[size:, k * size : (k + 1) * size]


def weights(flops, s, pieces, order, active, far_time, own_time, far_cols, own_cols, m_cols, b_cols, a, d, picked):
    times = order.shape[0]
    _, rows, per_row, size, _ = a.shape
    whole = lambda slot, *_: (0, 0, 0, 0, 0)
    return pl.pallas_call(
        lambda *refs: weights_kernel(s, pieces, *refs),
        out_shape=jax.ShapeDtypeStruct((times, rows, per_row, 2, size, size), F32),
        grid_spec=pltpu.PrefetchScalarGridSpec(
            num_scalar_prefetch=8,
            grid=(times,),
            in_specs=[
                pl.BlockSpec(a.shape, whole),
                pl.BlockSpec(a.shape, whole),
                *[ANY] * len(picked),
            ],
            out_specs=pl.BlockSpec(
                (1, rows, per_row, 2, size, size), lambda slot, *_: (slot, 0, 0, 0, 0, 0)
            ),
            scratch_shapes=[
                pltpu.VMEM((rows, per_row, 2 * size, 2 * size), BF16),
                pltpu.VMEM((rows, per_row, 2 * size, 2 * size), BF16),
                pltpu.VMEM((rows, 2 * size, per_row * size), BF16),
                pltpu.VMEM((rows, rows * size, 2 * size), BF16),
                pltpu.VMEM((2,) + a.shape, a.dtype),
                pltpu.SemaphoreType.DMA((len(picked), 2)),
            ],
        ),
        compiler_params=pltpu.CompilerParams(vmem_limit_bytes=16 * 2**20),
        cost_estimate=cost(flops, times * 1_000_000),
        name="weights",
    )(order, active, far_time, own_time, far_cols, own_cols, m_cols, b_cols, a, d, *picked)


def products(field_ref, u_refs, slot, first):
    _, rows, per_row, size, _ = field_ref.shape
    chunk = min(size, 32)
    fold = lambda x: jnp.sum(x.reshape(chunk // 8, 8, size), axis=0)
    sums = [jnp.zeros((8, size), F32) for _ in range(2 * len(u_refs))]
    for r in range(rows):
        for j in range(per_row):
            for start in range(0, size, chunk):
                at = pl.ds(start, chunk)
                real = field_ref[0, r, j, at].astype(F32)
                imag = field_ref[1, r, j, at].astype(F32)
                for s, u_ref in enumerate(u_refs):
                    u_real, u_imag = u_ref[slot, first + r, j, 0, at], u_ref[slot, first + r, j, 1, at]
                    sums[2 * s] += fold(real * u_real - imag * u_imag)
                    sums[2 * s + 1] += fold(real * u_imag + imag * u_real)
    return sums


def add_lines(slot, first, field_ref, u0_ref, u1_ref, masks_ref, before_ref):
    sums = products(field_ref, (u0_ref, u1_ref), slot, first)
    deltas = masks_ref.shape[1] // 2
    lines = []
    for part in range(2):
        for k in range(deltas):
            line = before_ref[part * deltas + k] if before_ref is not None else 0.0
            for s in range(2):
                at = s * deltas + k
                line = line + masks_ref[slot, at : at + 1] * sums[2 * s + part]
            lines.append(line)
    return lines


def inner_kernel(slot, first, field_ref, u0_ref, u1_ref, masks_ref, *refs):
    *before, out_ref = refs
    lines = add_lines(slot, first, field_ref, u0_ref, u1_ref, masks_ref, before[0] if before else None)
    for at, line in enumerate(lines):
        out_ref[at] = line


def inner(slot, first, field, u0, u1, masks, *before):
    return pl.pallas_call(
        lambda *refs: inner_kernel(slot, first, *refs),
        out_shape=jax.ShapeDtypeStruct((masks.shape[1], 8, field.shape[-1]), F32),
        in_specs=[VMEM] * (4 + len(before)),
        out_specs=VMEM,
        cost_estimate=cost(4_000_000, 4_000_000),
        compiler_params=pltpu.CompilerParams(vmem_limit_bytes=16 * 2**20),
        name="inner",
    )(field, u0, u1, masks, *before)


def stage_kernel(slot, u0_ref, u1_ref, masks_ref, out0_ref, out1_ref, out_masks_ref, sems, masks_sem):
    copies = [
        pltpu.make_async_copy(u_ref.at[slot, r], out_ref.at[0, r], sems.at[s, r])
        for s, (u_ref, out_ref) in enumerate(((u0_ref, out0_ref), (u1_ref, out1_ref)))
        for r in range(u_ref.shape[1])
    ]
    copies.append(pltpu.make_async_copy(masks_ref.at[slot], out_masks_ref.at[0], masks_sem))
    for copy in copies:
        copy.start()
    for copy in copies:
        copy.wait()


def stage(slot, u0, u1, masks):
    one = lambda value: jax.ShapeDtypeStruct((1,) + value.shape[1:], value.dtype)
    return pl.pallas_call(
        lambda *refs: stage_kernel(slot, *refs),
        out_shape=[one(u0), one(u1), one(masks)],
        in_specs=[ANY] * 3,
        out_specs=[VMEM] * 3,
        scratch_shapes=[pltpu.SemaphoreType.DMA((2, u0.shape[1])), pltpu.SemaphoreType.DMA],
        cost_estimate=cost(0, 6_000_000),
        compiler_params=pltpu.CompilerParams(vmem_limit_bytes=8 * 2**20),
        name="stage",
    )(u0, u1, masks)


def last_kernel(field_ref, u0_ref, u1_ref, masks_ref, before_ref, mine_ref, theirs_ref):
    lines = add_lines(0, 0, field_ref, u0_ref, u1_ref, masks_ref, before_ref)
    table = jnp.concatenate([jnp.sum(line, axis=0, keepdims=True) for line in lines], axis=0)
    table = jnp.sum(table, axis=1, keepdims=True)
    share = mine_ref.shape[1]
    for part in range(2):
        at = part * 2 * share
        mine_ref[part] = table[at : at + share]
        theirs_ref[part] = table[at + share : at + 2 * share]


def last(field, u0, u1, masks, lines):
    share = masks.shape[1] // 4
    return pl.pallas_call(
        last_kernel,
        out_shape=[jax.ShapeDtypeStruct((2, share, 1), F32)] * 2,
        in_specs=[VMEM] * 5,
        out_specs=[VMEM] * 2,
        cost_estimate=cost(4_000_000, 4_000_000),
        compiler_params=pltpu.CompilerParams(vmem_limit_bytes=8 * 2**20),
        name="last",
    )(field, u0, u1, masks, lines)


def local(fields, block_cols, sources, deltas, partner):
    assert fields.shape[0] == 1 and lax.axis_size("src") == 2
    del partner
    fields = fields[0]
    times = fields.shape[0]
    core = lax.axis_index("src").reshape(1)
    pairs = one_way_pairs(lax.axis_size("mom"))
    swap = lambda value: lax.ppermute(value, "src", [(0, 1), (1, 0)])
    to_partner = lambda value: lax.ppermute(value, "mom", pairs)

    cols = block_cols.reshape(-1)
    far_cols = to_partner(cols)
    group = lax.axis_index("mom")
    sends = (group >= min(a for a, _ in pairs)) & (group <= max(a for a, _ in pairs))
    picked = lax.cond(sends, pick_source, lambda _, fields: no_field(fields), sources, fields)
    far = [to_partner(picked)]

    other_time = swap(sources)
    order, active, full, masks = plan(core, sources, other_time, deltas, times)
    rows = fields.shape[2]
    half = rows // 2
    pieces = [(slot, 0, rows) for slot in range(times - 1)]
    pieces += [(times - 1, 0, half), (times - 1, half, rows - half)]
    picked = pick_others(order, fields, pieces)
    own_field = picked[0]
    *early, near, late_low, late_high = picked
    far += [to_partner(field) for field in early[1:]]
    near, far[0] = lax.optimization_barrier((near, far[0]))
    near = to_partner(near)

    other_cols = swap(cols)
    far_other_cols = swap(far_cols)
    other_field = swap(own_field)
    far_other = swap(far[0])
    u0 = weights(
        80_000_000_000,
        0,
        pieces,
        order,
        active,
        sources,
        sources,
        far_cols,
        cols,
        far_cols,
        cols,
        far[0],
        own_field,
        picked,
    )
    u1 = weights(
        2_000_000_000,
        1,
        pieces,
        order,
        active,
        other_time,
        other_time,
        far_other_cols,
        other_cols,
        far_cols,
        cols,
        far_other,
        other_field,
        picked,
    )
    lines = inner(0, 0, far[0], u0, u1, masks)
    for slot, field in enumerate(far[1:], 1):
        lines = inner(slot, 0, field, u0, u1, masks, lines)

    both = ("mom", "src")

    def with_slot(cores):
        routes = [(2 * a + c, 2 * b + c) for a, b in pairs for c in cores]

        def branch(low, high, u0, u1, masks, lines):
            low, high = lax.ppermute(low, both, routes), lax.ppermute(high, both, routes)
            lines = inner(times - 1, 0, low, u0, u1, masks, lines)
            return inner(times - 1, half, high, u0, u1, masks, lines), *stage(times - 2, u0, u1, masks)

        return branch

    def without_slot(low, high, u0, u1, masks, lines):
        return lines, *stage(times - 2, u0, u1, masks)

    branches = [without_slot, with_slot([0]), with_slot([1]), with_slot([0, 1])]
    late_low, late_high, lines = lax.optimization_barrier((late_low, late_high, lines))
    lines, *staged = lax.switch(full[0], branches, late_low, late_high, u0, u1, masks, lines)
    mine, theirs = last(near, *staged, lines)

    total = mine + swap(theirs)
    back = [(2 * a + c, 2 * b + c) for b, a in pairs for c in range(2)]
    return total + lax.ppermute(total, both, back)


def solution(mesh):
    in_specs = (
        P(("ens", "mom"), "src", None, None, None, None, None),
        P(("ens", "mom"), "src", None, None),
        P("src"),
        P(),
        P("mom"),
    )
    out_specs = P(None, "src", ("ens", "mom"))
    return jax.shard_map(local, mesh=mesh, in_specs=in_specs, out_specs=out_specs, check_vma=False)
```

```python
import jax
import jax.numpy as jnp
from jax import lax
from jax.experimental import pallas as pl
from jax.experimental.pallas import tpu as pltpu
from jax.sharding import PartitionSpec as P

F32 = jnp.float32
BF16 = jnp.bfloat16
I32 = jnp.int32
SMEM = pl.BlockSpec(memory_space=pltpu.SMEM)
VMEM = pl.BlockSpec(memory_space=pltpu.VMEM)
ANY = pl.BlockSpec(memory_space=pl.ANY)


def one_way_pairs(count):
    half = count // 2
    outer = half // 2
    return [(g + half, g) if g < outer else (g, g + half) for g in range(half)]


def cost(flops, size):
    return pl.CostEstimate(flops=flops, bytes_accessed=size, transcendentals=0)


def pick_source_kernel(source_ref, fields_ref, out_ref, sems):
    time = lax.rem(source_ref[0], I32(fields_ref.shape[0]))
    copies = [
        pltpu.make_async_copy(fields_ref.at[time, part, r], out_ref.at[part, r], sems.at[part, r])
        for part in range(fields_ref.shape[1])
        for r in range(fields_ref.shape[2])
    ]
    for copy in copies:
        copy.start()
    for copy in copies:
        copy.wait()


def pick_source(source, fields):
    return pl.pallas_call(
        pick_source_kernel,
        out_shape=jax.ShapeDtypeStruct(fields.shape[1:], fields.dtype),
        in_specs=[SMEM, ANY],
        out_specs=VMEM,
        scratch_shapes=[pltpu.SemaphoreType.DMA(fields.shape[1:3])],
        cost_estimate=cost(0, 1_600_000),
        compiler_params=pltpu.CompilerParams(vmem_limit_bytes=52 * 2**20),
        name="pick_source",
    )(source, fields)


def no_field_kernel(out_ref):
    out_ref[...] = jnp.zeros_like(out_ref)


def no_field(fields):
    return pl.pallas_call(
        no_field_kernel,
        out_shape=jax.ShapeDtypeStruct(fields.shape[1:], fields.dtype),
        out_specs=VMEM,
        cost_estimate=cost(0, 800_000),
        name="no_field",
    )()


def pick_kernel(pieces, order_ref, fields_ref, *refs):
    *outs, sems = refs
    copies = [
        pltpu.make_async_copy(
            fields_ref.at[order_ref[slot], part, pl.ds(first, rows)], out.at[part], sems.at[at, part]
        )
        for at, ((slot, first, rows), out) in enumerate(zip(pieces, outs))
        for part in range(2)
    ]
    for copy in copies:
        copy.start()
    for copy in copies:
        copy.wait()


def pick_others(order, fields, pieces):
    return pl.pallas_call(
        lambda *refs: pick_kernel(pieces, *refs),
        out_shape=[
            jax.ShapeDtypeStruct((2, rows) + fields.shape[3:], fields.dtype) for _, _, rows in pieces
        ],
        in_specs=[SMEM, ANY],
        out_specs=[VMEM] * len(pieces),
        scratch_shapes=[pltpu.SemaphoreType.DMA((len(pieces), 2))],
        cost_estimate=cost(0, 5_000_000),
        compiler_params=pltpu.CompilerParams(vmem_limit_bytes=51 * 2**20),
        name="pick_others",
    )(order, fields)


def plan_kernel(core_ref, own_ref, other_ref, deltas_ref, order_ref, active_ref, full_ref, masks_ref):
    times = order_ref.shape[0]
    deltas = deltas_ref.shape[0]
    sinks = []
    for s, ref in enumerate((own_ref, other_ref)):
        for k in range(deltas):
            sinks.append(lax.rem(ref[0] + deltas_ref[k], I32(2 * times)))
    base = core_ref[0] * times
    first = own_ref[0] - base
    keys = []
    for t in range(times):
        needed = sinks[0] == base + t
        for sink in sinks[1:]:
            needed = needed | (sink == base + t)
        key = jnp.where(needed, I32(t), I32(times + t))
        keys.append(jnp.where(first == t, I32(-1), key))
    for t in range(times):
        rank = I32(0)
        for other in range(times):
            if other != t:
                rank += (keys[other] < keys[t]).astype(I32)
        order_ref[rank] = I32(t)
        for s in range(2):
            active = sinks[s * deltas] == base + t
            for k in range(1, deltas):
                active = active | (sinks[s * deltas + k] == base + t)
            active_ref[s * times + rank] = active.astype(I32)
    full = I32(0)
    for c in range(2):
        count = I32(0)
        for t in range(times):
            needed = (own_ref[0] == c * times + t) | (other_ref[0] == c * times + t)
            for sink in sinks:
                needed = needed | (sink == c * times + t)
            count += needed.astype(I32)
        full += jnp.where(count == times, I32(1 << c), I32(0))
    full_ref[0] = full
    for slot in range(times):
        time = base + order_ref[slot]
        for s in range(2):
            for k in range(deltas):
                own_first = sinks[s * deltas + (k + deltas // 2) % deltas]
                sink = jnp.where(core_ref[0] == 0, sinks[s * deltas + k], own_first)
                row = jnp.full((1, masks_ref.shape[2]), jnp.where(sink == time, F32(1), F32(0)))
                masks_ref[slot, s * deltas + k : s * deltas + k + 1] = row


def plan(core, own, other, deltas, times):
    return pl.pallas_call(
        plan_kernel,
        out_shape=[
            jax.ShapeDtypeStruct((times,), I32),
            jax.ShapeDtypeStruct((2 * times,), I32),
            jax.ShapeDtypeStruct((1,), I32),
            jax.ShapeDtypeStruct((times, 2 * deltas.shape[0], 128), F32),
        ],
        in_specs=[SMEM] * 4,
        out_specs=[SMEM] * 3 + [VMEM],
        cost_estimate=cost(0, 1000),
        name="plan",
    )(core, own, other, deltas)


def weights_kernel(s, pieces, order_ref, active_ref, *refs):
    far_ref, own_ref, far_cols, own_cols, m_cols, b_cols, a_ref, d_ref, *refs = refs
    *b_refs, u_ref, la, ld, bs, yn, held, sems = refs
    slot = pl.program_id(0)
    rows, per_row, size = a_ref.shape[1], a_ref.shape[2], a_ref.shape[3]
    times = order_ref.shape[0]
    step = rows * per_row
    base = order_ref[slot] * step
    a_base = lax.rem(far_ref[0], I32(times)) * step
    d_base = lax.rem(own_ref[0], I32(times)) * step
    lo, hi = pl.ds(0, size), pl.ds(size, size)

    b_copies = [[] for _ in range(times)]
    for at, ((piece_slot, first, count), b_ref) in enumerate(zip(pieces, b_refs)):
        for part in range(2):
            to = held.at[piece_slot % 2, part, pl.ds(first, count)]
            b_copies[piece_slot].append(pltpu.make_async_copy(b_ref.at[part], to, sems.at[at, part]))

    @pl.when(slot == 0)
    def _():
        for copy in b_copies[0]:
            copy.start()
        for r in range(rows):
            for j in range(per_row):
                real, imag = a_ref[0, r, j], a_ref[1, r, j]
                la[r, j, lo, lo] = real
                la[r, j, lo, hi] = -imag
                la[r, j, hi, lo] = imag
                la[r, j, hi, hi] = real
                real, imag = d_ref[0, r, j].T, d_ref[1, r, j].T
                ld[r, j, lo, lo] = real
                ld[r, j, lo, hi] = -imag
                ld[r, j, hi, lo] = imag
                ld[r, j, hi, hi] = real

    for at in range(times):

        @pl.when(slot == at)
        def _():
            for copy in b_copies[at + 1] if at + 1 < times else []:
                copy.start()
            for copy in b_copies[at]:
                copy.wait()

    @pl.when(active_ref[s * times + slot] == 0)
    def _():
        u_ref[...] = jnp.zeros_like(u_ref)

    @pl.when(active_ref[s * times + slot] != 0)
    def _():
        for r in range(rows):
            for j in range(per_row):
                bs[r, lo, pl.ds(j * size, size)] = held[slot % 2, 0, r, j]
                bs[r, hi, pl.ds(j * size, size)] = held[slot % 2, 1, r, j]

        yn[...] = jnp.zeros_like(yn)
        for r in range(rows):
            inners = [far_cols[a_base + r * per_row + j] for j in range(per_row)]
            parts = [
                jnp.dot(la[r, j], bs[inners[j]], preferred_element_type=F32) for j in range(per_row)
            ]
            pieces = []
            for j in range(per_row):
                for k in range(per_row):
                    col = b_cols[base + inners[j] * per_row + k]
                    pieces.append((j, col, parts[j][:, k * size : (k + 1) * size]))
            for at in reversed(range(len(pieces))):
                j, col, value = pieces[at]
                for other_j, other_col, other in pieces:
                    if other_j > j:
                        value = value + jnp.where(other_col == col, 1.0, 0.0) * other
                yn[col, pl.ds(r * size, size), lo] = value[:size].astype(BF16)
                yn[col, pl.ds(r * size, size), hi] = value[size:].astype(BF16)

        trace_real = jnp.zeros((size, size), F32)
        trace_imag = jnp.zeros((size, size), F32)
        for r in range(rows):
            trace_real += yn[r, pl.ds(r * size, size), lo].astype(F32)
            trace_imag += yn[r, pl.ds(r * size, size), hi].astype(F32)
        diagonal = lax.broadcasted_iota(I32, (size, size), 0) == lax.broadcasted_iota(I32, (size, size), 1)
        trace_real = jnp.sum(jnp.where(diagonal, trace_real, 0.0), axis=(0, 1), keepdims=True)
        trace_imag = jnp.sum(jnp.where(diagonal, trace_imag, 0.0), axis=(0, 1), keepdims=True)

        for r in range(rows):
            for j in range(per_row):
                col = m_cols[base + r * per_row + j]
                pick = I32(0)
                keep = F32(0)
                for k in range(per_row):
                    hit = own_cols[d_base + col * per_row + k] == r
                    pick = jnp.where(hit, I32(k), pick)
                    keep = jnp.where(hit, F32(1), keep)
                real = ld[col, pick, lo, lo].astype(F32)
                imag = ld[col, pick, hi, lo].astype(F32)
                weight_real, weight_imag = trace_real * keep, trace_imag * keep
                u_ref[0, r, j, 0] = weight_real * real - weight_imag * imag
                u_ref[0, r, j, 1] = weight_real * imag + weight_imag * real

        for i in range(rows):
            for j in range(per_row):
                r = own_cols[d_base + i * per_row + j]
                met = [m_cols[base + r * per_row + k] for k in range(per_row)]
                right = jnp.concatenate(
                    [yn[i, pl.ds(pl.multiple_of(col * size, size), size)] for col in met], axis=0
                )
                part = lax.dot_general(
                    ld[i, j], right, (((1,), (1,)), ((), ())), preferred_element_type=F32
                )
                for k in range(per_row):
                    u_ref[0, r, k, 0] -= part[:size, k * size : (k + 1) * size]
                    u_ref[0, r, k, 1] -= part[size:, k * size : (k + 1) * size]


def weights(flops, s, pieces, order, active, far_time, own_time, far_cols, own_cols, m_cols, b_cols, a, d, picked):
    times = order.shape[0]
    _, rows, per_row, size, _ = a.shape
    whole = lambda slot, *_: (0, 0, 0, 0, 0)
    return pl.pallas_call(
        lambda *refs: weights_kernel(s, pieces, *refs),
        out_shape=jax.ShapeDtypeStruct((times, rows, per_row, 2, size, size), F32),
        grid_spec=pltpu.PrefetchScalarGridSpec(
            num_scalar_prefetch=8,
            grid=(times,),
            in_specs=[
                pl.BlockSpec(a.shape, whole),
                pl.BlockSpec(a.shape, whole),
                *[ANY] * len(picked),
            ],
            out_specs=pl.BlockSpec(
                (1, rows, per_row, 2, size, size), lambda slot, *_: (slot, 0, 0, 0, 0, 0)
            ),
            scratch_shapes=[
                pltpu.VMEM((rows, per_row, 2 * size, 2 * size), BF16),
                pltpu.VMEM((rows, per_row, 2 * size, 2 * size), BF16),
                pltpu.VMEM((rows, 2 * size, per_row * size), BF16),
                pltpu.VMEM((rows, rows * size, 2 * size), BF16),
                pltpu.VMEM((2,) + a.shape, a.dtype),
                pltpu.SemaphoreType.DMA((len(picked), 2)),
            ],
        ),
        compiler_params=pltpu.CompilerParams(vmem_limit_bytes=16 * 2**20),
        cost_estimate=cost(flops, times * 1_000_000),
        name="weights",
    )(order, active, far_time, own_time, far_cols, own_cols, m_cols, b_cols, a, d, *picked)


def products(field_ref, u_refs, slot, first):
    _, rows, per_row, size, _ = field_ref.shape
    chunk = min(size, 32)
    fold = lambda x: jnp.sum(x.reshape(chunk // 8, 8, size), axis=0)
    sums = [jnp.zeros((8, size), F32) for _ in range(2 * len(u_refs))]
    for r in range(rows):
        for j in range(per_row):
            for start in range(0, size, chunk):
                at = pl.ds(start, chunk)
                real = field_ref[0, r, j, at].astype(F32)
                imag = field_ref[1, r, j, at].astype(F32)
                for s, u_ref in enumerate(u_refs):
                    u_real, u_imag = u_ref[slot, first + r, j, 0, at], u_ref[slot, first + r, j, 1, at]
                    sums[2 * s] += fold(real * u_real - imag * u_imag)
                    sums[2 * s + 1] += fold(real * u_imag + imag * u_real)
    return sums


def add_lines(slot, first, field_ref, u0_ref, u1_ref, masks_ref, before_ref):
    sums = products(field_ref, (u0_ref, u1_ref), slot, first)
    deltas = masks_ref.shape[1] // 2
    lines = []
    for part in range(2):
        for k in range(deltas):
            line = before_ref[part * deltas + k] if before_ref is not None else 0.0
            for s in range(2):
                at = s * deltas + k
                line = line + masks_ref[slot, at : at + 1] * sums[2 * s + part]
            lines.append(line)
    return lines


def inner_kernel(slot, first, field_ref, u0_ref, u1_ref, masks_ref, *refs):
    *before, out_ref = refs
    lines = add_lines(slot, first, field_ref, u0_ref, u1_ref, masks_ref, before[0] if before else None)
    for at, line in enumerate(lines):
        out_ref[at] = line


def inner(slot, first, field, u0, u1, masks, *before):
    return pl.pallas_call(
        lambda *refs: inner_kernel(slot, first, *refs),
        out_shape=jax.ShapeDtypeStruct((masks.shape[1], 8, field.shape[-1]), F32),
        in_specs=[VMEM] * (4 + len(before)),
        out_specs=VMEM,
        cost_estimate=cost(4_000_000, 4_000_000),
        compiler_params=pltpu.CompilerParams(vmem_limit_bytes=16 * 2**20),
        name="inner",
    )(field, u0, u1, masks, *before)


def stage_kernel(slot, u0_ref, u1_ref, masks_ref, out0_ref, out1_ref, out_masks_ref, sems, masks_sem):
    copies = [
        pltpu.make_async_copy(u_ref.at[slot, r], out_ref.at[0, r], sems.at[s, r])
        for s, (u_ref, out_ref) in enumerate(((u0_ref, out0_ref), (u1_ref, out1_ref)))
        for r in range(u_ref.shape[1])
    ]
    copies.append(pltpu.make_async_copy(masks_ref.at[slot], out_masks_ref.at[0], masks_sem))
    for copy in copies:
        copy.start()
    for copy in copies:
        copy.wait()


def stage(slot, u0, u1, masks):
    one = lambda value: jax.ShapeDtypeStruct((1,) + value.shape[1:], value.dtype)
    return pl.pallas_call(
        lambda *refs: stage_kernel(slot, *refs),
        out_shape=[one(u0), one(u1), one(masks)],
        in_specs=[ANY] * 3,
        out_specs=[VMEM] * 3,
        scratch_shapes=[pltpu.SemaphoreType.DMA((2, u0.shape[1])), pltpu.SemaphoreType.DMA],
        cost_estimate=cost(0, 6_000_000),
        compiler_params=pltpu.CompilerParams(vmem_limit_bytes=8 * 2**20),
        name="stage",
    )(u0, u1, masks)


def last_kernel(field_ref, u0_ref, u1_ref, masks_ref, before_ref, out_ref):
    lines = add_lines(0, 0, field_ref, u0_ref, u1_ref, masks_ref, before_ref)
    table = jnp.concatenate([jnp.sum(line, axis=0, keepdims=True) for line in lines], axis=0)
    table = jnp.sum(table, axis=1, keepdims=True)
    share = out_ref.shape[2]
    for part in range(2):
        for owner in range(2):
            at = (2 * part + owner) * share
            out_ref[owner, part] = table[at : at + share]


def last(field, u0, u1, masks, lines):
    return pl.pallas_call(
        last_kernel,
        out_shape=jax.ShapeDtypeStruct((2, 2, masks.shape[1] // 4, 1), F32),
        in_specs=[VMEM] * 5,
        out_specs=VMEM,
        cost_estimate=cost(4_000_000, 4_000_000),
        compiler_params=pltpu.CompilerParams(vmem_limit_bytes=8 * 2**20),
        name="last",
    )(field, u0, u1, masks, lines)


def local(fields, block_cols, sources, deltas, partner):
    assert fields.shape[0] == 1 and lax.axis_size("src") == 2
    del partner
    fields = fields[0]
    times = fields.shape[0]
    core = lax.axis_index("src").reshape(1)
    pairs = one_way_pairs(lax.axis_size("mom"))
    swap = lambda value: lax.ppermute(value, "src", [(0, 1), (1, 0)])
    to_partner = lambda value: lax.ppermute(value, "mom", pairs)

    cols = block_cols.reshape(-1)
    far_cols = to_partner(cols)
    group = lax.axis_index("mom")
    sends = (group >= min(a for a, _ in pairs)) & (group <= max(a for a, _ in pairs))
    picked = lax.cond(sends, pick_source, lambda _, fields: no_field(fields), sources, fields)
    far = [to_partner(picked)]

    other_time = swap(sources)
    order, active, full, masks = plan(core, sources, other_time, deltas, times)
    rows = fields.shape[2]
    half = rows // 2
    pieces = [(slot, 0, rows) for slot in range(times - 1)]
    pieces += [(times - 1, 0, half), (times - 1, half, rows - half)]
    picked = pick_others(order, fields, pieces)
    own_field = picked[0]
    *early, near, late_low, late_high = picked
    far += [to_partner(field) for field in early[1:]]
    near, far[0] = lax.optimization_barrier((near, far[0]))
    near = to_partner(near)

    other_cols = swap(cols)
    far_other_cols = swap(far_cols)
    other_field = swap(own_field)
    far_other = swap(far[0])
    u0 = weights(
        80_000_000_000,
        0,
        pieces,
        order,
        active,
        sources,
        sources,
        far_cols,
        cols,
        far_cols,
        cols,
        far[0],
        own_field,
        picked,
    )
    u1 = weights(
        2_000_000_000,
        1,
        pieces,
        order,
        active,
        other_time,
        other_time,
        far_other_cols,
        other_cols,
        far_cols,
        cols,
        far_other,
        other_field,
        picked,
    )
    lines = inner(0, 0, far[0], u0, u1, masks)
    for slot, field in enumerate(far[1:], 1):
        lines = inner(slot, 0, field, u0, u1, masks, lines)

    both = ("mom", "src")

    def with_slot(cores):
        routes = [(2 * a + c, 2 * b + c) for a, b in pairs for c in cores]

        def branch(low, high, u0, u1, masks, lines):
            low, high = lax.ppermute(low, both, routes), lax.ppermute(high, both, routes)
            lines = inner(times - 1, 0, low, u0, u1, masks, lines)
            return inner(times - 1, half, high, u0, u1, masks, lines), *stage(times - 2, u0, u1, masks)

        return branch

    def without_slot(low, high, u0, u1, masks, lines):
        return lines, *stage(times - 2, u0, u1, masks)

    branches = [without_slot, with_slot([0]), with_slot([1]), with_slot([0, 1])]
    late_low, late_high, lines = lax.optimization_barrier((late_low, late_high, lines))
    lines, *staged = lax.switch(full[0], branches, late_low, late_high, u0, u1, masks, lines)
    sums = last(near, *staged, lines)

    back = [(2 * a + c, 2 * b + c) for b, a in pairs for c in range(2)]
    sums = sums + lax.ppermute(sums, both, back)
    return sums[0] + swap(sums[1])


def solution(mesh):
    in_specs = (
        P(("ens", "mom"), "src", None, None, None, None, None),
        P(("ens", "mom"), "src", None, None),
        P("src"),
        P(),
        P("mom"),
    )
    out_specs = P(None, "src", ("ens", "mom"))
    return jax.shard_map(local, mesh=mesh, in_specs=in_specs, out_specs=out_specs, check_vma=False)
```

```python
import jax
import jax.numpy as jnp
from jax import lax
from jax.experimental import pallas as pl
from jax.experimental.pallas import tpu as pltpu
from jax.sharding import PartitionSpec as P

F32 = jnp.float32
BF16 = jnp.bfloat16
I32 = jnp.int32
SMEM = pl.BlockSpec(memory_space=pltpu.SMEM)
VMEM = pl.BlockSpec(memory_space=pltpu.VMEM)
ANY = pl.BlockSpec(memory_space=pl.ANY)


def one_way_pairs(count):
    half = count // 2
    outer = half // 2
    return [(g + half, g) if g < outer else (g, g + half) for g in range(half)]


def cost(flops, size):
    return pl.CostEstimate(flops=flops, bytes_accessed=size, transcendentals=0)


def pick_source_kernel(source_ref, cols_ref, fields_ref, out_ref, sems):
    _, _, rows, per_row, size, _ = fields_ref.shape
    time = lax.rem(source_ref[0], I32(fields_ref.shape[0]))
    copies = [
        pltpu.make_async_copy(
            fields_ref.at[time, part, r], out_ref.at[pl.ds((part * rows + r) * per_row, per_row)], sems.at[part, r]
        )
        for part in range(2)
        for r in range(rows)
    ]
    for copy in copies:
        copy.start()
    lane = lax.broadcasted_iota(I32, (16, size), 1)
    line = jnp.zeros((16, size), F32)
    for at in range(cols_ref.shape[0]):
        line = jnp.where(lane == at, cols_ref[at].astype(F32), line)
    out_ref[2 * rows * per_row] = jnp.zeros((size, size), BF16)
    out_ref[2 * rows * per_row, 0:16] = line.astype(BF16)
    for copy in copies:
        copy.wait()


def message_shape(fields):
    _, _, rows, per_row, size, _ = fields.shape
    return jax.ShapeDtypeStruct((2 * rows * per_row + 1, size, size), fields.dtype)


def pick_source(source, cols, fields):
    return pl.pallas_call(
        pick_source_kernel,
        out_shape=message_shape(fields),
        in_specs=[SMEM, SMEM, ANY],
        out_specs=VMEM,
        scratch_shapes=[pltpu.SemaphoreType.DMA(fields.shape[1:3])],
        cost_estimate=cost(0, 1_600_000),
        compiler_params=pltpu.CompilerParams(vmem_limit_bytes=52 * 2**20),
        name="pick_source",
    )(source, cols, fields)


def no_field_kernel(out_ref):
    out_ref[...] = jnp.zeros_like(out_ref)


def no_field(fields):
    return pl.pallas_call(
        no_field_kernel,
        out_shape=message_shape(fields),
        out_specs=VMEM,
        cost_estimate=cost(0, 800_000),
        name="no_field",
    )()


def pick_kernel(pieces, order_ref, fields_ref, *refs):
    *outs, sems = refs
    copies = [
        pltpu.make_async_copy(
            fields_ref.at[order_ref[slot], part, pl.ds(first, rows)], out.at[part], sems.at[at, part]
        )
        for at, ((slot, first, rows), out) in enumerate(zip(pieces, outs))
        for part in range(2)
    ]
    for copy in copies:
        copy.start()
    for copy in copies:
        copy.wait()


def pick_others(order, fields, pieces):
    return pl.pallas_call(
        lambda *refs: pick_kernel(pieces, *refs),
        out_shape=[
            jax.ShapeDtypeStruct((2, rows) + fields.shape[3:], fields.dtype) for _, _, rows in pieces
        ],
        in_specs=[SMEM, ANY],
        out_specs=[VMEM] * len(pieces),
        scratch_shapes=[pltpu.SemaphoreType.DMA((len(pieces), 2))],
        cost_estimate=cost(0, 5_000_000),
        compiler_params=pltpu.CompilerParams(vmem_limit_bytes=51 * 2**20),
        name="pick_others",
    )(order, fields)


def plan_kernel(core_ref, own_ref, other_ref, deltas_ref, order_ref, active_ref, counts_ref, masks_ref):
    times = order_ref.shape[0]
    deltas = deltas_ref.shape[0]
    sinks = []
    for s, ref in enumerate((own_ref, other_ref)):
        for k in range(deltas):
            sinks.append(lax.rem(ref[0] + deltas_ref[k], I32(2 * times)))
    base = core_ref[0] * times
    first = own_ref[0] - base
    keys = []
    for t in range(times):
        needed = sinks[0] == base + t
        for sink in sinks[1:]:
            needed = needed | (sink == base + t)
        key = jnp.where(needed, I32(t), I32(times + t))
        keys.append(jnp.where(first == t, I32(-1), key))
    for t in range(times):
        rank = I32(0)
        for other in range(times):
            if other != t:
                rank += (keys[other] < keys[t]).astype(I32)
        order_ref[rank] = I32(t)
        for s in range(2):
            active = sinks[s * deltas] == base + t
            for k in range(1, deltas):
                active = active | (sinks[s * deltas + k] == base + t)
            active_ref[s * times + rank] = active.astype(I32)
    counts = I32(0)
    for c in range(2):
        count = I32(0)
        for t in range(times):
            needed = (own_ref[0] == c * times + t) | (other_ref[0] == c * times + t)
            for sink in sinks:
                needed = needed | (sink == c * times + t)
            count += needed.astype(I32)
        counts += 3**c * jnp.maximum(count - (times - 2), I32(0))
    counts_ref[0] = counts
    for slot in range(times):
        time = base + order_ref[slot]
        for s in range(2):
            for k in range(deltas):
                own_first = sinks[s * deltas + (k + deltas // 2) % deltas]
                sink = jnp.where(core_ref[0] == 0, sinks[s * deltas + k], own_first)
                row = jnp.full((1, masks_ref.shape[2]), jnp.where(sink == time, F32(1), F32(0)))
                masks_ref[slot, s * deltas + k : s * deltas + k + 1] = row


def plan(core, own, other, deltas, times):
    return pl.pallas_call(
        plan_kernel,
        out_shape=[
            jax.ShapeDtypeStruct((times,), I32),
            jax.ShapeDtypeStruct((2 * times,), I32),
            jax.ShapeDtypeStruct((1,), I32),
            jax.ShapeDtypeStruct((times, 2 * deltas.shape[0], 128), F32),
        ],
        in_specs=[SMEM] * 4,
        out_specs=[SMEM] * 3 + [VMEM],
        cost_estimate=cost(0, 1000),
        name="plan",
    )(core, own, other, deltas)


def weights_kernel(s, pieces, order_ref, active_ref, *refs):
    far_ref, own_ref, far_cols, own_cols, m_cols, b_cols, a_ref, d_ref, *refs = refs
    *b_refs, u_ref, la, ld, bs, yn, held, sems = refs
    slot = pl.program_id(0)
    rows, per_row, size = a_ref.shape[1], a_ref.shape[2], a_ref.shape[3]
    times = order_ref.shape[0]
    step = rows * per_row
    base = order_ref[slot] * step
    a_base = lax.rem(far_ref[0], I32(times)) * step
    d_base = lax.rem(own_ref[0], I32(times)) * step
    lo, hi = pl.ds(0, size), pl.ds(size, size)

    b_copies = [[] for _ in range(times)]
    for at, ((piece_slot, first, count), b_ref) in enumerate(zip(pieces, b_refs)):
        for part in range(2):
            to = held.at[piece_slot % 2, part, pl.ds(first, count)]
            b_copies[piece_slot].append(pltpu.make_async_copy(b_ref.at[part], to, sems.at[at, part]))

    @pl.when(slot == 0)
    def _():
        for copy in b_copies[0]:
            copy.start()
        for r in range(rows):
            for j in range(per_row):
                real, imag = a_ref[0, r, j], a_ref[1, r, j]
                la[r, j, lo, lo] = real
                la[r, j, lo, hi] = -imag
                la[r, j, hi, lo] = imag
                la[r, j, hi, hi] = real
                real, imag = d_ref[0, r, j].T, d_ref[1, r, j].T
                ld[r, j, lo, lo] = real
                ld[r, j, lo, hi] = -imag
                ld[r, j, hi, lo] = imag
                ld[r, j, hi, hi] = real

    for at in range(times):

        @pl.when(slot == at)
        def _():
            for copy in b_copies[at + 1] if at + 1 < times else []:
                copy.start()
            for copy in b_copies[at]:
                copy.wait()

    @pl.when(active_ref[s * times + slot] == 0)
    def _():
        u_ref[...] = jnp.zeros_like(u_ref)

    @pl.when(active_ref[s * times + slot] != 0)
    def _():
        for r in range(rows):
            for j in range(per_row):
                bs[r, lo, pl.ds(j * size, size)] = held[slot % 2, 0, r, j]
                bs[r, hi, pl.ds(j * size, size)] = held[slot % 2, 1, r, j]

        yn[...] = jnp.zeros_like(yn)
        for r in range(rows):
            inners = [far_cols[a_base + r * per_row + j] for j in range(per_row)]
            parts = [
                jnp.dot(la[r, j], bs[inners[j]], preferred_element_type=F32) for j in range(per_row)
            ]
            pieces = []
            for j in range(per_row):
                for k in range(per_row):
                    col = b_cols[base + inners[j] * per_row + k]
                    pieces.append((j, col, parts[j][:, k * size : (k + 1) * size]))
            for at in reversed(range(len(pieces))):
                j, col, value = pieces[at]
                for other_j, other_col, other in pieces:
                    if other_j > j:
                        value = value + jnp.where(other_col == col, 1.0, 0.0) * other
                yn[col, pl.ds(r * size, size), lo] = value[:size].astype(BF16)
                yn[col, pl.ds(r * size, size), hi] = value[size:].astype(BF16)

        trace_real = jnp.zeros((size, size), F32)
        trace_imag = jnp.zeros((size, size), F32)
        for r in range(rows):
            trace_real += yn[r, pl.ds(r * size, size), lo].astype(F32)
            trace_imag += yn[r, pl.ds(r * size, size), hi].astype(F32)
        diagonal = lax.broadcasted_iota(I32, (size, size), 0) == lax.broadcasted_iota(I32, (size, size), 1)
        trace_real = jnp.sum(jnp.where(diagonal, trace_real, 0.0), axis=(0, 1), keepdims=True)
        trace_imag = jnp.sum(jnp.where(diagonal, trace_imag, 0.0), axis=(0, 1), keepdims=True)

        for r in range(rows):
            for j in range(per_row):
                col = m_cols[base + r * per_row + j]
                pick = I32(0)
                keep = F32(0)
                for k in range(per_row):
                    hit = own_cols[d_base + col * per_row + k] == r
                    pick = jnp.where(hit, I32(k), pick)
                    keep = jnp.where(hit, F32(1), keep)
                real = ld[col, pick, lo, lo].astype(F32)
                imag = ld[col, pick, hi, lo].astype(F32)
                weight_real, weight_imag = trace_real * keep, trace_imag * keep
                u_ref[0, r, j, 0] = weight_real * real - weight_imag * imag
                u_ref[0, r, j, 1] = weight_real * imag + weight_imag * real

        for i in range(rows):
            for j in range(per_row):
                r = own_cols[d_base + i * per_row + j]
                met = [m_cols[base + r * per_row + k] for k in range(per_row)]
                right = jnp.concatenate(
                    [yn[i, pl.ds(pl.multiple_of(col * size, size), size)] for col in met], axis=0
                )
                part = lax.dot_general(
                    ld[i, j], right, (((1,), (1,)), ((), ())), preferred_element_type=F32
                )
                for k in range(per_row):
                    u_ref[0, r, k, 0] -= part[:size, k * size : (k + 1) * size]
                    u_ref[0, r, k, 1] -= part[size:, k * size : (k + 1) * size]


def weights(flops, s, pieces, order, active, far_time, own_time, far_cols, own_cols, m_cols, b_cols, a, d, picked):
    times = order.shape[0]
    _, rows, per_row, size, _ = a.shape
    whole = lambda slot, *_: (0, 0, 0, 0, 0)
    return pl.pallas_call(
        lambda *refs: weights_kernel(s, pieces, *refs),
        out_shape=jax.ShapeDtypeStruct((times, rows, per_row, 2, size, size), F32),
        grid_spec=pltpu.PrefetchScalarGridSpec(
            num_scalar_prefetch=8,
            grid=(times,),
            in_specs=[
                pl.BlockSpec(a.shape, whole),
                pl.BlockSpec(a.shape, whole),
                *[ANY] * len(picked),
            ],
            out_specs=pl.BlockSpec(
                (1, rows, per_row, 2, size, size), lambda slot, *_: (slot, 0, 0, 0, 0, 0)
            ),
            scratch_shapes=[
                pltpu.VMEM((rows, per_row, 2 * size, 2 * size), BF16),
                pltpu.VMEM((rows, per_row, 2 * size, 2 * size), BF16),
                pltpu.VMEM((rows, 2 * size, per_row * size), BF16),
                pltpu.VMEM((rows, rows * size, 2 * size), BF16),
                pltpu.VMEM((2,) + a.shape, a.dtype),
                pltpu.SemaphoreType.DMA((len(picked), 2)),
            ],
        ),
        compiler_params=pltpu.CompilerParams(vmem_limit_bytes=16 * 2**20),
        cost_estimate=cost(flops, times * 1_000_000),
        name="weights",
    )(order, active, far_time, own_time, far_cols, own_cols, m_cols, b_cols, a, d, *picked)


def products(field_ref, u_refs, slot, first):
    _, rows, per_row, size, _ = field_ref.shape
    chunk = min(size, 32)
    fold = lambda x: jnp.sum(x.reshape(chunk // 8, 8, size), axis=0)
    sums = [jnp.zeros((8, size), F32) for _ in range(2 * len(u_refs))]
    for r in range(rows):
        for j in range(per_row):
            for start in range(0, size, chunk):
                at = pl.ds(start, chunk)
                real = field_ref[0, r, j, at].astype(F32)
                imag = field_ref[1, r, j, at].astype(F32)
                for s, u_ref in enumerate(u_refs):
                    u_real, u_imag = u_ref[slot, first + r, j, 0, at], u_ref[slot, first + r, j, 1, at]
                    sums[2 * s] += fold(real * u_real - imag * u_imag)
                    sums[2 * s + 1] += fold(real * u_imag + imag * u_real)
    return sums


def add_lines(slot, first, field_ref, u0_ref, u1_ref, masks_ref, before_ref):
    sums = products(field_ref, (u0_ref, u1_ref), slot, first)
    deltas = masks_ref.shape[1] // 2
    lines = []
    for part in range(2):
        for k in range(deltas):
            line = before_ref[part * deltas + k] if before_ref is not None else 0.0
            for s in range(2):
                at = s * deltas + k
                line = line + masks_ref[slot, at : at + 1] * sums[2 * s + part]
            lines.append(line)
    return lines


def inner_kernel(slot, first, field_ref, u0_ref, u1_ref, masks_ref, *refs):
    *before, out_ref = refs
    lines = add_lines(slot, first, field_ref, u0_ref, u1_ref, masks_ref, before[0] if before else None)
    for at, line in enumerate(lines):
        out_ref[at] = line


def inner(slot, first, field, u0, u1, masks, *before):
    return pl.pallas_call(
        lambda *refs: inner_kernel(slot, first, *refs),
        out_shape=jax.ShapeDtypeStruct((masks.shape[1], 8, field.shape[-1]), F32),
        in_specs=[VMEM] * (4 + len(before)),
        out_specs=VMEM,
        cost_estimate=cost(4_000_000, 4_000_000),
        compiler_params=pltpu.CompilerParams(vmem_limit_bytes=16 * 2**20),
        name="inner",
    )(field, u0, u1, masks, *before)


def stage_kernel(slot, u0_ref, u1_ref, masks_ref, out0_ref, out1_ref, out_masks_ref, sems, masks_sem):
    copies = [
        pltpu.make_async_copy(u_ref.at[slot, r], out_ref.at[0, r], sems.at[s, r])
        for s, (u_ref, out_ref) in enumerate(((u0_ref, out0_ref), (u1_ref, out1_ref)))
        for r in range(u_ref.shape[1])
    ]
    copies.append(pltpu.make_async_copy(masks_ref.at[slot], out_masks_ref.at[0], masks_sem))
    for copy in copies:
        copy.start()
    for copy in copies:
        copy.wait()


def stage(slot, u0, u1, masks):
    one = lambda value: jax.ShapeDtypeStruct((1,) + value.shape[1:], value.dtype)
    return pl.pallas_call(
        lambda *refs: stage_kernel(slot, *refs),
        out_shape=[one(u0), one(u1), one(masks)],
        in_specs=[ANY] * 3,
        out_specs=[VMEM] * 3,
        scratch_shapes=[pltpu.SemaphoreType.DMA((2, u0.shape[1])), pltpu.SemaphoreType.DMA],
        cost_estimate=cost(0, 6_000_000),
        compiler_params=pltpu.CompilerParams(vmem_limit_bytes=8 * 2**20),
        name="stage",
    )(u0, u1, masks)


def last_kernel(field_ref, u0_ref, u1_ref, masks_ref, before_ref, out_ref):
    lines = add_lines(0, 0, field_ref, u0_ref, u1_ref, masks_ref, before_ref)
    table = jnp.concatenate([jnp.sum(line, axis=0, keepdims=True) for line in lines], axis=0)
    table = jnp.sum(table, axis=1, keepdims=True)
    share = out_ref.shape[2]
    for part in range(2):
        for owner in range(2):
            at = (2 * part + owner) * share
            out_ref[owner, part] = table[at : at + share]


def last(field, u0, u1, masks, lines):
    return pl.pallas_call(
        last_kernel,
        out_shape=jax.ShapeDtypeStruct((2, 2, masks.shape[1] // 4, 1), F32),
        in_specs=[VMEM] * 5,
        out_specs=VMEM,
        cost_estimate=cost(4_000_000, 4_000_000),
        compiler_params=pltpu.CompilerParams(vmem_limit_bytes=8 * 2**20),
        name="last",
    )(field, u0, u1, masks, lines)


def local(fields, block_cols, sources, deltas, partner):
    assert fields.shape[0] == 1 and fields.shape[1] == 4 and lax.axis_size("src") == 2
    del partner
    fields = fields[0]
    times = fields.shape[0]
    core = lax.axis_index("src").reshape(1)
    pairs = one_way_pairs(lax.axis_size("mom"))
    swap = lambda value: lax.ppermute(value, "src", [(0, 1), (1, 0)])
    to_partner = lambda value: lax.ppermute(value, "mom", pairs)

    cols = block_cols.reshape(-1)
    assert cols.shape[0] <= fields.shape[-1]
    group = lax.axis_index("mom")
    sends = (group >= min(a for a, _ in pairs)) & (group <= max(a for a, _ in pairs))
    send = lambda sources, cols, fields: pick_source(sources, cols.reshape(-1), fields)
    message = lax.cond(sends, send, lambda _, __, fields: no_field(fields), sources, block_cols, fields)
    message = to_partner(message)
    far_source = message[:-1].reshape(fields.shape[1:])
    far_cols = message[-1, 0, : cols.shape[0]].astype(I32)

    other_time = swap(sources)
    order, active, counts, masks = plan(core, sources, other_time, deltas, times)
    pieces = [(slot, 0, fields.shape[2]) for slot in range(times)]
    picked = pick_others(order, fields, pieces)
    other_cols = swap(cols)
    second = to_partner(picked[1])
    other_field = swap(picked[0])

    both = ("mom", "src")

    def make_branch(needs):
        def branch(source, far_cols, other_field, *picked):
            arrived = []
            for slot in range(2, 2 + max(needs)):
                cores = [c for c in range(2) if needs[c] >= slot - 1]
                routes = [(2 * a + c, 2 * b + c) for a, b in pairs for c in cores]
                arrived.append(lax.ppermute(picked[slot], both, routes))
            far_other = swap(source)
            far_other_cols = swap(far_cols)
            u0 = weights(
                80_000_000_000, 0, pieces, order, active, sources, sources,
                far_cols, cols, far_cols, cols, source, picked[0], picked,
            )
            u1 = weights(
                80_000_000_000, 1, pieces, order, active, other_time, other_time,
                far_other_cols, other_cols, far_cols, cols, far_other, other_field, picked,
            )
            lines = inner(0, 0, source, u0, u1, masks)
            for slot, field in enumerate(arrived, 2):
                lines = inner(slot, 0, field, u0, u1, masks, lines)
            return lines, *stage(1, u0, u1, masks)

        return branch

    branches = [make_branch((at % 3, at // 3)) for at in range(9)]
    operands = far_source, far_cols, other_field, *picked
    lines, *staged = lax.switch(counts[0], branches, *operands)
    sums = last(second, *staged, lines)

    back = [(2 * a + c, 2 * b + c) for b, a in pairs for c in range(2)]
    sums = sums + lax.ppermute(sums, both, back)
    return sums[0] + swap(sums[1])


def solution(mesh):
    in_specs = (
        P(("ens", "mom"), "src", None, None, None, None, None),
        P(("ens", "mom"), "src", None, None),
        P("src"),
        P(),
        P("mom"),
    )
    out_specs = P(None, "src", ("ens", "mom"))
    return jax.shard_map(local, mesh=mesh, in_specs=in_specs, out_specs=out_specs, check_vma=False)
```

```python
import jax
import jax.numpy as jnp
from jax import lax
from jax.experimental import pallas as pl
from jax.experimental.pallas import tpu as pltpu
from jax.sharding import PartitionSpec as P

F32 = jnp.float32
BF16 = jnp.bfloat16
I32 = jnp.int32
SMEM = pl.BlockSpec(memory_space=pltpu.SMEM)
VMEM = pl.BlockSpec(memory_space=pltpu.VMEM)
ANY = pl.BlockSpec(memory_space=pl.ANY)


def one_way_pairs(count):
    half = count // 2
    outer = half // 2
    return [(g + half, g) if g < outer else (g, g + half) for g in range(half)]


def cost(flops, size):
    return pl.CostEstimate(flops=flops, bytes_accessed=size, transcendentals=0)


def pick_source_kernel(source_ref, fields_ref, out_ref, sems):
    time = lax.rem(source_ref[0], I32(fields_ref.shape[0]))
    copies = [
        pltpu.make_async_copy(fields_ref.at[time, part, r], out_ref.at[part, r], sems.at[part, r])
        for part in range(fields_ref.shape[1])
        for r in range(fields_ref.shape[2])
    ]
    for copy in copies:
        copy.start()
    for copy in copies:
        copy.wait()


def pick_source(source, fields):
    return pl.pallas_call(
        pick_source_kernel,
        out_shape=jax.ShapeDtypeStruct(fields.shape[1:], fields.dtype),
        in_specs=[SMEM, ANY],
        out_specs=VMEM,
        scratch_shapes=[pltpu.SemaphoreType.DMA(fields.shape[1:3])],
        cost_estimate=cost(0, 1_600_000),
        compiler_params=pltpu.CompilerParams(vmem_limit_bytes=52 * 2**20),
        name="pick_source",
    )(source, fields)


def no_field_kernel(out_ref):
    out_ref[...] = jnp.zeros_like(out_ref)


def no_field(fields):
    return pl.pallas_call(
        no_field_kernel,
        out_shape=jax.ShapeDtypeStruct(fields.shape[1:], fields.dtype),
        out_specs=VMEM,
        cost_estimate=cost(0, 800_000),
        name="no_field",
    )()


def pick_kernel(pieces, order_ref, fields_ref, *refs):
    *outs, sems = refs
    copies = [
        pltpu.make_async_copy(
            fields_ref.at[order_ref[slot], part, pl.ds(first, rows)], out.at[part], sems.at[at, part]
        )
        for at, ((slot, first, rows), out) in enumerate(zip(pieces, outs))
        for part in range(2)
    ]
    for copy in copies:
        copy.start()
    for copy in copies:
        copy.wait()


def pick_others(order, fields, pieces):
    return pl.pallas_call(
        lambda *refs: pick_kernel(pieces, *refs),
        out_shape=[
            jax.ShapeDtypeStruct((2, rows) + fields.shape[3:], fields.dtype) for _, _, rows in pieces
        ],
        in_specs=[SMEM, ANY],
        out_specs=[VMEM] * len(pieces),
        scratch_shapes=[pltpu.SemaphoreType.DMA((len(pieces), 2))],
        cost_estimate=cost(0, 5_000_000),
        compiler_params=pltpu.CompilerParams(vmem_limit_bytes=51 * 2**20),
        name="pick_others",
    )(order, fields)


def plan_kernel(core_ref, own_ref, other_ref, deltas_ref, order_ref, active_ref, full_ref, masks_ref):
    times = order_ref.shape[0]
    deltas = deltas_ref.shape[0]
    sinks = []
    for s, ref in enumerate((own_ref, other_ref)):
        for k in range(deltas):
            sinks.append(lax.rem(ref[0] + deltas_ref[k], I32(2 * times)))
    base = core_ref[0] * times
    first = own_ref[0] - base
    keys = []
    for t in range(times):
        needed = sinks[0] == base + t
        for sink in sinks[1:]:
            needed = needed | (sink == base + t)
        key = jnp.where(needed, I32(t), I32(times + t))
        keys.append(jnp.where(first == t, I32(-1), key))
    for t in range(times):
        rank = I32(0)
        for other in range(times):
            if other != t:
                rank += (keys[other] < keys[t]).astype(I32)
        order_ref[rank] = I32(t)
        for s in range(2):
            active = sinks[s * deltas] == base + t
            for k in range(1, deltas):
                active = active | (sinks[s * deltas + k] == base + t)
            active_ref[s * times + rank] = active.astype(I32)
    full = I32(0)
    for c in range(2):
        count = I32(0)
        for t in range(times):
            needed = (own_ref[0] == c * times + t) | (other_ref[0] == c * times + t)
            for sink in sinks:
                needed = needed | (sink == c * times + t)
            count += needed.astype(I32)
        full += jnp.where(count == times, I32(1 << c), I32(0))
    full_ref[0] = full
    for slot in range(times):
        time = base + order_ref[slot]
        for s in range(2):
            for k in range(deltas):
                own_first = sinks[s * deltas + (k + deltas // 2) % deltas]
                sink = jnp.where(core_ref[0] == 0, sinks[s * deltas + k], own_first)
                row = jnp.full((1, masks_ref.shape[2]), jnp.where(sink == time, F32(1), F32(0)))
                masks_ref[slot, s * deltas + k : s * deltas + k + 1] = row


def plan(core, own, other, deltas, times):
    return pl.pallas_call(
        plan_kernel,
        out_shape=[
            jax.ShapeDtypeStruct((times,), I32),
            jax.ShapeDtypeStruct((2 * times,), I32),
            jax.ShapeDtypeStruct((1,), I32),
            jax.ShapeDtypeStruct((times, 2 * deltas.shape[0], 128), F32),
        ],
        in_specs=[SMEM] * 4,
        out_specs=[SMEM] * 3 + [VMEM],
        cost_estimate=cost(0, 1000),
        name="plan",
    )(core, own, other, deltas)


def weights_kernel(s, pieces, order_ref, active_ref, *refs):
    far_ref, own_ref, far_cols, own_cols, m_cols, b_cols, a_ref, d_ref, *refs = refs
    *b_refs, u_ref, la, ld, bs, yn, held, sems = refs
    slot = pl.program_id(0)
    rows, per_row, size = a_ref.shape[1], a_ref.shape[2], a_ref.shape[3]
    times = order_ref.shape[0]
    step = rows * per_row
    base = order_ref[slot] * step
    a_base = lax.rem(far_ref[0], I32(times)) * step
    d_base = lax.rem(own_ref[0], I32(times)) * step
    lo, hi = pl.ds(0, size), pl.ds(size, size)

    b_copies = [[] for _ in range(times)]
    for at, ((piece_slot, first, count), b_ref) in enumerate(zip(pieces, b_refs)):
        for part in range(2):
            to = held.at[piece_slot % 2, part, pl.ds(first, count)]
            b_copies[piece_slot].append(pltpu.make_async_copy(b_ref.at[part], to, sems.at[at, part]))

    @pl.when(slot == 0)
    def _():
        for copy in b_copies[0]:
            copy.start()
        for r in range(rows):
            for j in range(per_row):
                real, imag = a_ref[0, r, j], a_ref[1, r, j]
                la[r, j, lo, lo] = real
                la[r, j, lo, hi] = -imag
                la[r, j, hi, lo] = imag
                la[r, j, hi, hi] = real
                real, imag = d_ref[0, r, j].T, d_ref[1, r, j].T
                ld[r, j, lo, lo] = real
                ld[r, j, lo, hi] = -imag
                ld[r, j, hi, lo] = imag
                ld[r, j, hi, hi] = real

    for at in range(times):

        @pl.when(slot == at)
        def _():
            for copy in b_copies[at + 1] if at + 1 < times else []:
                copy.start()
            for copy in b_copies[at]:
                copy.wait()

    @pl.when(active_ref[s * times + slot] == 0)
    def _():
        u_ref[...] = jnp.zeros_like(u_ref)

    @pl.when(active_ref[s * times + slot] != 0)
    def _():
        for r in range(rows):
            for j in range(per_row):
                bs[r, lo, pl.ds(j * size, size)] = held[slot % 2, 0, r, j]
                bs[r, hi, pl.ds(j * size, size)] = held[slot % 2, 1, r, j]

        yn[...] = jnp.zeros_like(yn)
        for r in range(rows):
            inners = [far_cols[a_base + r * per_row + j] for j in range(per_row)]
            parts = [
                jnp.dot(la[r, j], bs[inners[j]], preferred_element_type=F32) for j in range(per_row)
            ]
            pieces = []
            for j in range(per_row):
                for k in range(per_row):
                    col = b_cols[base + inners[j] * per_row + k]
                    pieces.append((j, col, parts[j][:, k * size : (k + 1) * size]))
            for at in reversed(range(len(pieces))):
                j, col, value = pieces[at]
                for other_j, other_col, other in pieces:
                    if other_j > j:
                        value = value + jnp.where(other_col == col, 1.0, 0.0) * other
                yn[col, pl.ds(r * size, size), lo] = value[:size].astype(BF16)
                yn[col, pl.ds(r * size, size), hi] = value[size:].astype(BF16)

        trace_real = jnp.zeros((size, size), F32)
        trace_imag = jnp.zeros((size, size), F32)
        for r in range(rows):
            trace_real += yn[r, pl.ds(r * size, size), lo].astype(F32)
            trace_imag += yn[r, pl.ds(r * size, size), hi].astype(F32)
        diagonal = lax.broadcasted_iota(I32, (size, size), 0) == lax.broadcasted_iota(I32, (size, size), 1)
        trace_real = jnp.sum(jnp.where(diagonal, trace_real, 0.0), axis=(0, 1), keepdims=True)
        trace_imag = jnp.sum(jnp.where(diagonal, trace_imag, 0.0), axis=(0, 1), keepdims=True)

        for r in range(rows):
            for j in range(per_row):
                col = m_cols[base + r * per_row + j]
                pick = I32(0)
                keep = F32(0)
                for k in range(per_row):
                    hit = own_cols[d_base + col * per_row + k] == r
                    pick = jnp.where(hit, I32(k), pick)
                    keep = jnp.where(hit, F32(1), keep)
                real = ld[col, pick, lo, lo].astype(F32)
                imag = ld[col, pick, hi, lo].astype(F32)
                weight_real, weight_imag = trace_real * keep, trace_imag * keep
                u_ref[0, r, j, 0] = weight_real * real - weight_imag * imag
                u_ref[0, r, j, 1] = weight_real * imag + weight_imag * real

        for i in range(rows):
            for j in range(per_row):
                r = own_cols[d_base + i * per_row + j]
                met = [m_cols[base + r * per_row + k] for k in range(per_row)]
                right = jnp.concatenate(
                    [yn[i, pl.ds(pl.multiple_of(col * size, size), size)] for col in met], axis=0
                )
                part = lax.dot_general(
                    ld[i, j], right, (((1,), (1,)), ((), ())), preferred_element_type=F32
                )
                for k in range(per_row):
                    u_ref[0, r, k, 0] -= part[:size, k * size : (k + 1) * size]
                    u_ref[0, r, k, 1] -= part[size:, k * size : (k + 1) * size]


def weights(flops, s, pieces, order, active, far_time, own_time, far_cols, own_cols, m_cols, b_cols, a, d, picked):
    times = order.shape[0]
    _, rows, per_row, size, _ = a.shape
    whole = lambda slot, *_: (0, 0, 0, 0, 0)
    return pl.pallas_call(
        lambda *refs: weights_kernel(s, pieces, *refs),
        out_shape=jax.ShapeDtypeStruct((times, rows, per_row, 2, size, size), F32),
        grid_spec=pltpu.PrefetchScalarGridSpec(
            num_scalar_prefetch=8,
            grid=(times,),
            in_specs=[
                pl.BlockSpec(a.shape, whole),
                pl.BlockSpec(a.shape, whole),
                *[ANY] * len(picked),
            ],
            out_specs=pl.BlockSpec(
                (1, rows, per_row, 2, size, size), lambda slot, *_: (slot, 0, 0, 0, 0, 0)
            ),
            scratch_shapes=[
                pltpu.VMEM((rows, per_row, 2 * size, 2 * size), BF16),
                pltpu.VMEM((rows, per_row, 2 * size, 2 * size), BF16),
                pltpu.VMEM((rows, 2 * size, per_row * size), BF16),
                pltpu.VMEM((rows, rows * size, 2 * size), BF16),
                pltpu.VMEM((2,) + a.shape, a.dtype),
                pltpu.SemaphoreType.DMA((len(picked), 2)),
            ],
        ),
        compiler_params=pltpu.CompilerParams(vmem_limit_bytes=16 * 2**20),
        cost_estimate=cost(flops, times * 1_000_000),
        name="weights",
    )(order, active, far_time, own_time, far_cols, own_cols, m_cols, b_cols, a, d, *picked)


def products(field_ref, u_refs, slot, first):
    _, rows, per_row, size, _ = field_ref.shape
    chunk = min(size, 32)
    fold = lambda x: jnp.sum(x.reshape(chunk // 8, 8, size), axis=0)
    sums = [jnp.zeros((8, size), F32) for _ in range(2 * len(u_refs))]
    for r in range(rows):
        for j in range(per_row):
            for start in range(0, size, chunk):
                at = pl.ds(start, chunk)
                real = field_ref[0, r, j, at].astype(F32)
                imag = field_ref[1, r, j, at].astype(F32)
                for s, u_ref in enumerate(u_refs):
                    u_real, u_imag = u_ref[slot, first + r, j, 0, at], u_ref[slot, first + r, j, 1, at]
                    sums[2 * s] += fold(real * u_real - imag * u_imag)
                    sums[2 * s + 1] += fold(real * u_imag + imag * u_real)
    return sums


def add_lines(slot, first, field_ref, u0_ref, u1_ref, masks_ref, before_ref):
    sums = products(field_ref, (u0_ref, u1_ref), slot, first)
    deltas = masks_ref.shape[1] // 2
    lines = []
    for part in range(2):
        for k in range(deltas):
            line = before_ref[part * deltas + k] if before_ref is not None else 0.0
            for s in range(2):
                at = s * deltas + k
                line = line + masks_ref[slot, at : at + 1] * sums[2 * s + part]
            lines.append(line)
    return lines


def inner_kernel(slot, first, field_ref, u0_ref, u1_ref, masks_ref, *refs):
    *before, out_ref = refs
    lines = add_lines(slot, first, field_ref, u0_ref, u1_ref, masks_ref, before[0] if before else None)
    for at, line in enumerate(lines):
        out_ref[at] = line


def inner(slot, first, field, u0, u1, masks, *before):
    return pl.pallas_call(
        lambda *refs: inner_kernel(slot, first, *refs),
        out_shape=jax.ShapeDtypeStruct((masks.shape[1], 8, field.shape[-1]), F32),
        in_specs=[VMEM] * (4 + len(before)),
        out_specs=VMEM,
        cost_estimate=cost(4_000_000, 4_000_000),
        compiler_params=pltpu.CompilerParams(vmem_limit_bytes=16 * 2**20),
        name="inner",
    )(field, u0, u1, masks, *before)


def stage_kernel(slot, u0_ref, u1_ref, masks_ref, out0_ref, out1_ref, out_masks_ref, sems, masks_sem):
    copies = [
        pltpu.make_async_copy(u_ref.at[slot, r], out_ref.at[0, r], sems.at[s, r])
        for s, (u_ref, out_ref) in enumerate(((u0_ref, out0_ref), (u1_ref, out1_ref)))
        for r in range(u_ref.shape[1])
    ]
    copies.append(pltpu.make_async_copy(masks_ref.at[slot], out_masks_ref.at[0], masks_sem))
    for copy in copies:
        copy.start()
    for copy in copies:
        copy.wait()


def stage(slot, u0, u1, masks):
    one = lambda value: jax.ShapeDtypeStruct((1,) + value.shape[1:], value.dtype)
    return pl.pallas_call(
        lambda *refs: stage_kernel(slot, *refs),
        out_shape=[one(u0), one(u1), one(masks)],
        in_specs=[ANY] * 3,
        out_specs=[VMEM] * 3,
        scratch_shapes=[pltpu.SemaphoreType.DMA((2, u0.shape[1])), pltpu.SemaphoreType.DMA],
        cost_estimate=cost(0, 6_000_000),
        compiler_params=pltpu.CompilerParams(vmem_limit_bytes=8 * 2**20),
        name="stage",
    )(u0, u1, masks)


def last_kernel(field_ref, u0_ref, u1_ref, masks_ref, before_ref, out_ref):
    lines = add_lines(0, 0, field_ref, u0_ref, u1_ref, masks_ref, before_ref)
    table = jnp.concatenate([jnp.sum(line, axis=0, keepdims=True) for line in lines], axis=0)
    table = jnp.sum(table, axis=1, keepdims=True)
    share = out_ref.shape[2]
    for part in range(2):
        for owner in range(2):
            at = (2 * part + owner) * share
            out_ref[owner, part] = table[at : at + share]


def last(field, u0, u1, masks, lines):
    return pl.pallas_call(
        last_kernel,
        out_shape=jax.ShapeDtypeStruct((2, 2, masks.shape[1] // 4, 1), F32),
        in_specs=[VMEM] * 5,
        out_specs=VMEM,
        cost_estimate=cost(4_000_000, 4_000_000),
        compiler_params=pltpu.CompilerParams(vmem_limit_bytes=8 * 2**20),
        name="last",
    )(field, u0, u1, masks, lines)


def local(fields, block_cols, sources, deltas, partner):
    assert fields.shape[0] == 1 and lax.axis_size("src") == 2
    del partner
    fields = fields[0]
    times = fields.shape[0]
    core = lax.axis_index("src").reshape(1)
    pairs = one_way_pairs(lax.axis_size("mom"))
    swap = lambda value: lax.ppermute(value, "src", [(0, 1), (1, 0)])
    to_partner = lambda value: lax.ppermute(value, "mom", pairs)

    cols = block_cols.reshape(-1)
    far_cols = to_partner(cols)
    group = lax.axis_index("mom")
    sends = (group >= min(a for a, _ in pairs)) & (group <= max(a for a, _ in pairs))
    picked = lax.cond(sends, pick_source, lambda _, fields: no_field(fields), sources, fields)
    far = [to_partner(picked)]

    other_time = swap(sources)
    order, active, full, masks = plan(core, sources, other_time, deltas, times)
    rows = fields.shape[2]
    half = rows - rows // 3
    pieces = [(slot, 0, rows) for slot in range(times - 1)]
    pieces += [(times - 1, 0, half), (times - 1, half, rows - half)]
    picked = pick_others(order, fields, pieces)
    own_field = picked[0]
    *early, near, late_low, late_high = picked
    far += [to_partner(field) for field in early[1:]]
    near, far[0] = lax.optimization_barrier((near, far[0]))
    near = to_partner(near)

    other_cols = swap(cols)
    far_other_cols = swap(far_cols)
    other_field = swap(own_field)
    far_other = swap(far[0])
    u0 = weights(
        80_000_000_000,
        0,
        pieces,
        order,
        active,
        sources,
        sources,
        far_cols,
        cols,
        far_cols,
        cols,
        far[0],
        own_field,
        picked,
    )
    u1 = weights(
        2_000_000_000,
        1,
        pieces,
        order,
        active,
        other_time,
        other_time,
        far_other_cols,
        other_cols,
        far_cols,
        cols,
        far_other,
        other_field,
        picked,
    )
    lines = inner(0, 0, far[0], u0, u1, masks)
    for slot, field in enumerate(far[1:], 1):
        lines = inner(slot, 0, field, u0, u1, masks, lines)

    both = ("mom", "src")

    def with_slot(cores):
        routes = [(2 * a + c, 2 * b + c) for a, b in pairs for c in cores]

        def branch(low, high, u0, u1, masks, lines):
            low, high = lax.ppermute(low, both, routes), lax.ppermute(high, both, routes)
            lines = inner(times - 1, 0, low, u0, u1, masks, lines)
            return inner(times - 1, half, high, u0, u1, masks, lines), *stage(times - 2, u0, u1, masks)

        return branch

    def without_slot(low, high, u0, u1, masks, lines):
        return lines, *stage(times - 2, u0, u1, masks)

    branches = [without_slot, with_slot([0]), with_slot([1]), with_slot([0, 1])]
    late_low, late_high, lines = lax.optimization_barrier((late_low, late_high, lines))
    lines, *staged = lax.switch(full[0], branches, late_low, late_high, u0, u1, masks, lines)
    sums = last(near, *staged, lines)

    back = [(2 * a + c, 2 * b + c) for b, a in pairs for c in range(2)]
    sums = sums + lax.ppermute(sums, both, back)
    return sums[0] + swap(sums[1])


def solution(mesh):
    in_specs = (
        P(("ens", "mom"), "src", None, None, None, None, None),
        P(("ens", "mom"), "src", None, None),
        P("src"),
        P(),
        P("mom"),
    )
    out_specs = P(None, "src", ("ens", "mom"))
    return jax.shard_map(local, mesh=mesh, in_specs=in_specs, out_specs=out_specs, check_vma=False)
```

```python
import jax
import jax.numpy as jnp
from jax import lax
from jax.experimental import pallas as pl
from jax.experimental.pallas import tpu as pltpu
from jax.sharding import PartitionSpec as P

F32 = jnp.float32
BF16 = jnp.bfloat16
I32 = jnp.int32
SMEM = pl.BlockSpec(memory_space=pltpu.SMEM)
VMEM = pl.BlockSpec(memory_space=pltpu.VMEM)
ANY = pl.BlockSpec(memory_space=pl.ANY)


def one_way_pairs(count):
    half = count // 2
    outer = half // 2
    return [(g + half, g) if g < outer else (g, g + half) for g in range(half)]


def cost(flops, size):
    return pl.CostEstimate(flops=flops, bytes_accessed=size, transcendentals=0)


def pick_source_kernel(source_ref, fields_ref, out_ref, sems):
    time = lax.rem(source_ref[0], I32(fields_ref.shape[0]))
    copies = [
        pltpu.make_async_copy(fields_ref.at[time, part, r], out_ref.at[part, r], sems.at[part, r])
        for part in range(fields_ref.shape[1])
        for r in range(fields_ref.shape[2])
    ]
    for copy in copies:
        copy.start()
    for copy in copies:
        copy.wait()


def pick_source(source, fields):
    return pl.pallas_call(
        pick_source_kernel,
        out_shape=jax.ShapeDtypeStruct(fields.shape[1:], fields.dtype),
        in_specs=[SMEM, ANY],
        out_specs=VMEM,
        scratch_shapes=[pltpu.SemaphoreType.DMA(fields.shape[1:3])],
        cost_estimate=cost(0, 1_600_000),
        compiler_params=pltpu.CompilerParams(vmem_limit_bytes=52 * 2**20),
        name="pick_source",
    )(source, fields)


def no_field_kernel(out_ref):
    out_ref[...] = jnp.zeros_like(out_ref)


def no_field(fields):
    return pl.pallas_call(
        no_field_kernel,
        out_shape=jax.ShapeDtypeStruct(fields.shape[1:], fields.dtype),
        out_specs=VMEM,
        cost_estimate=cost(0, 800_000),
        name="no_field",
    )()


def pick_kernel(pieces, order_ref, fields_ref, *refs):
    *outs, sems = refs
    copies = [
        pltpu.make_async_copy(
            fields_ref.at[order_ref[slot], part, pl.ds(first, rows)], out.at[part], sems.at[at, part]
        )
        for at, ((slot, first, rows), out) in enumerate(zip(pieces, outs))
        for part in range(2)
    ]
    for copy in copies:
        copy.start()
    for copy in copies:
        copy.wait()


def pick_others(order, fields, pieces):
    return pl.pallas_call(
        lambda *refs: pick_kernel(pieces, *refs),
        out_shape=[
            jax.ShapeDtypeStruct((2, rows) + fields.shape[3:], fields.dtype) for _, _, rows in pieces
        ],
        in_specs=[SMEM, ANY],
        out_specs=[VMEM] * len(pieces),
        scratch_shapes=[pltpu.SemaphoreType.DMA((len(pieces), 2))],
        cost_estimate=cost(0, 5_000_000),
        compiler_params=pltpu.CompilerParams(vmem_limit_bytes=51 * 2**20),
        name="pick_others",
    )(order, fields)


def plan_kernel(core_ref, own_ref, other_ref, deltas_ref, order_ref, active_ref, full_ref, masks_ref):
    times = order_ref.shape[0]
    deltas = deltas_ref.shape[0]
    sinks = []
    for s, ref in enumerate((own_ref, other_ref)):
        for k in range(deltas):
            sinks.append(lax.rem(ref[0] + deltas_ref[k], I32(2 * times)))
    base = core_ref[0] * times
    first = own_ref[0] - base
    keys = []
    for t in range(times):
        needed = sinks[0] == base + t
        for sink in sinks[1:]:
            needed = needed | (sink == base + t)
        key = jnp.where(needed, I32(t), I32(times + t))
        keys.append(jnp.where(first == t, I32(-1), key))
    for t in range(times):
        rank = I32(0)
        for other in range(times):
            if other != t:
                rank += (keys[other] < keys[t]).astype(I32)
        order_ref[rank] = I32(t)
        for s in range(2):
            active = sinks[s * deltas] == base + t
            for k in range(1, deltas):
                active = active | (sinks[s * deltas + k] == base + t)
            active_ref[s * times + rank] = active.astype(I32)
    full = I32(0)
    for c in range(2):
        count = I32(0)
        for t in range(times):
            needed = (own_ref[0] == c * times + t) | (other_ref[0] == c * times + t)
            for sink in sinks:
                needed = needed | (sink == c * times + t)
            count += needed.astype(I32)
        full += jnp.where(count == times, I32(1 << c), I32(0))
    full_ref[0] = full
    for slot in range(times):
        time = base + order_ref[slot]
        for s in range(2):
            for k in range(deltas):
                own_first = sinks[s * deltas + (k + deltas // 2) % deltas]
                sink = jnp.where(core_ref[0] == 0, sinks[s * deltas + k], own_first)
                row = jnp.full((1, masks_ref.shape[2]), jnp.where(sink == time, F32(1), F32(0)))
                masks_ref[slot, s * deltas + k : s * deltas + k + 1] = row


def plan(core, own, other, deltas, times):
    return pl.pallas_call(
        plan_kernel,
        out_shape=[
            jax.ShapeDtypeStruct((times,), I32),
            jax.ShapeDtypeStruct((2 * times,), I32),
            jax.ShapeDtypeStruct((1,), I32),
            jax.ShapeDtypeStruct((times, 2 * deltas.shape[0], 128), F32),
        ],
        in_specs=[SMEM] * 4,
        out_specs=[SMEM] * 3 + [VMEM],
        cost_estimate=cost(0, 1000),
        name="plan",
    )(core, own, other, deltas)


def weights_kernel(s, pieces, order_ref, active_ref, *refs):
    far_ref, own_ref, far_cols, own_cols, m_cols, b_cols, a_ref, d_ref, *refs = refs
    *b_refs, u_ref, la, ld, bs, yn, held, sems = refs
    slot = pl.program_id(0)
    rows, per_row, size = a_ref.shape[1], a_ref.shape[2], a_ref.shape[3]
    times = order_ref.shape[0]
    step = rows * per_row
    base = order_ref[slot] * step
    a_base = lax.rem(far_ref[0], I32(times)) * step
    d_base = lax.rem(own_ref[0], I32(times)) * step
    lo, hi = pl.ds(0, size), pl.ds(size, size)

    b_copies = [[] for _ in range(times)]
    for at, ((piece_slot, first, count), b_ref) in enumerate(zip(pieces, b_refs)):
        for part in range(2):
            to = held.at[piece_slot % 2, part, pl.ds(first, count)]
            b_copies[piece_slot].append(pltpu.make_async_copy(b_ref.at[part], to, sems.at[at, part]))

    @pl.when(slot == 0)
    def _():
        for copy in b_copies[0]:
            copy.start()
        for r in range(rows):
            for j in range(per_row):
                real, imag = a_ref[0, r, j], a_ref[1, r, j]
                la[r, j, lo, lo] = real
                la[r, j, lo, hi] = -imag
                la[r, j, hi, lo] = imag
                la[r, j, hi, hi] = real
                real, imag = d_ref[0, r, j].T, d_ref[1, r, j].T
                ld[r, j, lo, lo] = real
                ld[r, j, lo, hi] = -imag
                ld[r, j, hi, lo] = imag
                ld[r, j, hi, hi] = real

    for at in range(times):

        @pl.when(slot == at)
        def _():
            for copy in b_copies[at + 1] if at + 1 < times else []:
                copy.start()
            for copy in b_copies[at]:
                copy.wait()

    @pl.when(active_ref[s * times + slot] == 0)
    def _():
        u_ref[...] = jnp.zeros_like(u_ref)

    @pl.when(active_ref[s * times + slot] != 0)
    def _():
        for r in range(rows):
            for j in range(per_row):
                bs[r, lo, pl.ds(j * size, size)] = held[slot % 2, 0, r, j]
                bs[r, hi, pl.ds(j * size, size)] = held[slot % 2, 1, r, j]

        yn[...] = jnp.zeros_like(yn)
        for r in range(rows):
            inners = [far_cols[a_base + r * per_row + j] for j in range(per_row)]
            parts = [
                jnp.dot(la[r, j], bs[inners[j]], preferred_element_type=F32) for j in range(per_row)
            ]
            pieces = []
            for j in range(per_row):
                for k in range(per_row):
                    col = b_cols[base + inners[j] * per_row + k]
                    pieces.append((j, col, parts[j][:, k * size : (k + 1) * size]))
            for at in reversed(range(len(pieces))):
                j, col, value = pieces[at]
                for other_j, other_col, other in pieces:
                    if other_j > j:
                        value = value + jnp.where(other_col == col, 1.0, 0.0) * other
                yn[col, pl.ds(r * size, size), lo] = value[:size].astype(BF16)
                yn[col, pl.ds(r * size, size), hi] = value[size:].astype(BF16)

        trace_real = jnp.zeros((size, size), F32)
        trace_imag = jnp.zeros((size, size), F32)
        for r in range(rows):
            trace_real += yn[r, pl.ds(r * size, size), lo].astype(F32)
            trace_imag += yn[r, pl.ds(r * size, size), hi].astype(F32)
        diagonal = lax.broadcasted_iota(I32, (size, size), 0) == lax.broadcasted_iota(I32, (size, size), 1)
        trace_real = jnp.sum(jnp.where(diagonal, trace_real, 0.0), axis=(0, 1), keepdims=True)
        trace_imag = jnp.sum(jnp.where(diagonal, trace_imag, 0.0), axis=(0, 1), keepdims=True)

        for r in range(rows):
            for j in range(per_row):
                col = m_cols[base + r * per_row + j]
                pick = I32(0)
                keep = F32(0)
                for k in range(per_row):
                    hit = own_cols[d_base + col * per_row + k] == r
                    pick = jnp.where(hit, I32(k), pick)
                    keep = jnp.where(hit, F32(1), keep)
                real = ld[col, pick, lo, lo].astype(F32)
                imag = ld[col, pick, hi, lo].astype(F32)
                weight_real, weight_imag = trace_real * keep, trace_imag * keep
                u_ref[0, r, j, 0] = weight_real * real - weight_imag * imag
                u_ref[0, r, j, 1] = weight_real * imag + weight_imag * real

        for i in range(rows):
            for j in range(per_row):
                r = own_cols[d_base + i * per_row + j]
                met = [m_cols[base + r * per_row + k] for k in range(per_row)]
                right = jnp.concatenate(
                    [yn[i, pl.ds(pl.multiple_of(col * size, size), size)] for col in met], axis=0
                )
                part = lax.dot_general(
                    ld[i, j], right, (((1,), (1,)), ((), ())), preferred_element_type=F32
                )
                for k in range(per_row):
                    u_ref[0, r, k, 0] -= part[:size, k * size : (k + 1) * size]
                    u_ref[0, r, k, 1] -= part[size:, k * size : (k + 1) * size]


def weights(flops, s, pieces, order, active, far_time, own_time, far_cols, own_cols, m_cols, b_cols, a, d, picked):
    times = order.shape[0]
    _, rows, per_row, size, _ = a.shape
    whole = lambda slot, *_: (0, 0, 0, 0, 0)
    return pl.pallas_call(
        lambda *refs: weights_kernel(s, pieces, *refs),
        out_shape=jax.ShapeDtypeStruct((times, rows, per_row, 2, size, size), F32),
        grid_spec=pltpu.PrefetchScalarGridSpec(
            num_scalar_prefetch=8,
            grid=(times,),
            in_specs=[
                pl.BlockSpec(a.shape, whole),
                pl.BlockSpec(a.shape, whole),
                *[ANY] * len(picked),
            ],
            out_specs=pl.BlockSpec(
                (1, rows, per_row, 2, size, size), lambda slot, *_: (slot, 0, 0, 0, 0, 0)
            ),
            scratch_shapes=[
                pltpu.VMEM((rows, per_row, 2 * size, 2 * size), BF16),
                pltpu.VMEM((rows, per_row, 2 * size, 2 * size), BF16),
                pltpu.VMEM((rows, 2 * size, per_row * size), BF16),
                pltpu.VMEM((rows, rows * size, 2 * size), BF16),
                pltpu.VMEM((2,) + a.shape, a.dtype),
                pltpu.SemaphoreType.DMA((len(picked), 2)),
            ],
        ),
        compiler_params=pltpu.CompilerParams(vmem_limit_bytes=16 * 2**20),
        cost_estimate=cost(flops, times * 1_000_000),
        name="weights",
    )(order, active, far_time, own_time, far_cols, own_cols, m_cols, b_cols, a, d, *picked)


def products(field_ref, u_refs, slot, first):
    _, rows, per_row, size, _ = field_ref.shape
    chunk = min(size, 16)
    fold = lambda x: jnp.sum(x.reshape(chunk // 8, 8, size), axis=0)
    sums = [jnp.zeros((8, size), F32) for _ in range(2 * len(u_refs))]
    for r in range(rows):
        for j in range(per_row):
            for start in range(0, size, chunk):
                at = pl.ds(start, chunk)
                real = field_ref[0, r, j, at].astype(F32)
                imag = field_ref[1, r, j, at].astype(F32)
                for s, u_ref in enumerate(u_refs):
                    u_real, u_imag = u_ref[slot, first + r, j, 0, at], u_ref[slot, first + r, j, 1, at]
                    sums[2 * s] += fold(real * u_real - imag * u_imag)
                    sums[2 * s + 1] += fold(real * u_imag + imag * u_real)
    return sums


def add_lines(slot, first, field_ref, u0_ref, u1_ref, masks_ref, before_ref):
    sums = products(field_ref, (u0_ref, u1_ref), slot, first)
    deltas = masks_ref.shape[1] // 2
    lines = []
    for part in range(2):
        for k in range(deltas):
            line = before_ref[part * deltas + k] if before_ref is not None else 0.0
            for s in range(2):
                at = s * deltas + k
                line = line + masks_ref[slot, at : at + 1] * sums[2 * s + part]
            lines.append(line)
    return lines


def inner_kernel(slot, first, field_ref, u0_ref, u1_ref, masks_ref, *refs):
    *before, out_ref = refs
    lines = add_lines(slot, first, field_ref, u0_ref, u1_ref, masks_ref, before[0] if before else None)
    for at, line in enumerate(lines):
        out_ref[at] = line


def inner(slot, first, field, u0, u1, masks, *before):
    return pl.pallas_call(
        lambda *refs: inner_kernel(slot, first, *refs),
        out_shape=jax.ShapeDtypeStruct((masks.shape[1], 8, field.shape[-1]), F32),
        in_specs=[VMEM] * (4 + len(before)),
        out_specs=VMEM,
        cost_estimate=cost(4_000_000, 4_000_000),
        compiler_params=pltpu.CompilerParams(vmem_limit_bytes=16 * 2**20),
        name="inner",
    )(field, u0, u1, masks, *before)


def stage_kernel(slot, u0_ref, u1_ref, masks_ref, out0_ref, out1_ref, out_masks_ref, sems, masks_sem):
    copies = [
        pltpu.make_async_copy(u_ref.at[slot, r], out_ref.at[0, r], sems.at[s, r])
        for s, (u_ref, out_ref) in enumerate(((u0_ref, out0_ref), (u1_ref, out1_ref)))
        for r in range(u_ref.shape[1])
    ]
    copies.append(pltpu.make_async_copy(masks_ref.at[slot], out_masks_ref.at[0], masks_sem))
    for copy in copies:
        copy.start()
    for copy in copies:
        copy.wait()


def stage(slot, u0, u1, masks):
    one = lambda value: jax.ShapeDtypeStruct((1,) + value.shape[1:], value.dtype)
    return pl.pallas_call(
        lambda *refs: stage_kernel(slot, *refs),
        out_shape=[one(u0), one(u1), one(masks)],
        in_specs=[ANY] * 3,
        out_specs=[VMEM] * 3,
        scratch_shapes=[pltpu.SemaphoreType.DMA((2, u0.shape[1])), pltpu.SemaphoreType.DMA],
        cost_estimate=cost(0, 6_000_000),
        compiler_params=pltpu.CompilerParams(vmem_limit_bytes=8 * 2**20),
        name="stage",
    )(u0, u1, masks)


def last_kernel(field_ref, u0_ref, u1_ref, masks_ref, before_ref, out_ref):
    lines = add_lines(0, 0, field_ref, u0_ref, u1_ref, masks_ref, before_ref)
    table = jnp.concatenate([jnp.sum(line, axis=0, keepdims=True) for line in lines], axis=0)
    table = jnp.sum(table, axis=1, keepdims=True)
    share = out_ref.shape[2]
    for part in range(2):
        for owner in range(2):
            at = (2 * part + owner) * share
            out_ref[owner, part] = table[at : at + share]


def last(field, u0, u1, masks, lines):
    return pl.pallas_call(
        last_kernel,
        out_shape=jax.ShapeDtypeStruct((2, 2, masks.shape[1] // 4, 1), F32),
        in_specs=[VMEM] * 5,
        out_specs=VMEM,
        cost_estimate=cost(4_000_000, 4_000_000),
        compiler_params=pltpu.CompilerParams(vmem_limit_bytes=8 * 2**20),
        name="last",
    )(field, u0, u1, masks, lines)


def local(fields, block_cols, sources, deltas, partner):
    assert fields.shape[0] == 1 and lax.axis_size("src") == 2
    del partner
    fields = fields[0]
    times = fields.shape[0]
    core = lax.axis_index("src").reshape(1)
    pairs = one_way_pairs(lax.axis_size("mom"))
    swap = lambda value: lax.ppermute(value, "src", [(0, 1), (1, 0)])
    to_partner = lambda value: lax.ppermute(value, "mom", pairs)

    cols = block_cols.reshape(-1)
    far_cols = to_partner(cols)
    group = lax.axis_index("mom")
    sends = (group >= min(a for a, _ in pairs)) & (group <= max(a for a, _ in pairs))
    picked = lax.cond(sends, pick_source, lambda _, fields: no_field(fields), sources, fields)
    far = [to_partner(picked)]

    other_time = swap(sources)
    order, active, full, masks = plan(core, sources, other_time, deltas, times)
    rows = fields.shape[2]
    half = rows // 2
    pieces = [(slot, 0, rows) for slot in range(times - 1)]
    pieces += [(times - 1, 0, half), (times - 1, half, rows - half)]
    picked = pick_others(order, fields, pieces)
    own_field = picked[0]
    *early, near, late_low, late_high = picked
    far += [to_partner(field) for field in early[1:]]
    near, far[0] = lax.optimization_barrier((near, far[0]))
    near = to_partner(near)

    other_cols = swap(cols)
    far_other_cols = swap(far_cols)
    other_field = swap(own_field)
    far_other = swap(far[0])
    u0 = weights(
        80_000_000_000,
        0,
        pieces,
        order,
        active,
        sources,
        sources,
        far_cols,
        cols,
        far_cols,
        cols,
        far[0],
        own_field,
        picked,
    )
    u1 = weights(
        2_000_000_000,
        1,
        pieces,
        order,
        active,
        other_time,
        other_time,
        far_other_cols,
        other_cols,
        far_cols,
        cols,
        far_other,
        other_field,
        picked,
    )
    lines = inner(0, 0, far[0], u0, u1, masks)
    for slot, field in enumerate(far[1:], 1):
        lines = inner(slot, 0, field, u0, u1, masks, lines)

    both = ("mom", "src")

    def with_slot(cores):
        routes = [(2 * a + c, 2 * b + c) for a, b in pairs for c in cores]

        def branch(low, high, u0, u1, masks, lines):
            low, high = lax.ppermute(low, both, routes), lax.ppermute(high, both, routes)
            lines = inner(times - 1, 0, low, u0, u1, masks, lines)
            return inner(times - 1, half, high, u0, u1, masks, lines), *stage(times - 2, u0, u1, masks)

        return branch

    def without_slot(low, high, u0, u1, masks, lines):
        return lines, *stage(times - 2, u0, u1, masks)

    branches = [without_slot, with_slot([0]), with_slot([1]), with_slot([0, 1])]
    late_low, late_high, lines = lax.optimization_barrier((late_low, late_high, lines))
    lines, *staged = lax.switch(full[0], branches, late_low, late_high, u0, u1, masks, lines)
    sums = last(near, *staged, lines)

    back = [(2 * a + c, 2 * b + c) for b, a in pairs for c in range(2)]
    sums = sums + lax.ppermute(sums, both, back)
    return sums[0] + swap(sums[1])


def solution(mesh):
    in_specs = (
        P(("ens", "mom"), "src", None, None, None, None, None),
        P(("ens", "mom"), "src", None, None),
        P("src"),
        P(),
        P("mom"),
    )
    out_specs = P(None, "src", ("ens", "mom"))
    return jax.shard_map(local, mesh=mesh, in_specs=in_specs, out_specs=out_specs, check_vma=False)
```
